128 devices in a mesh: sec: 4 (over x), lat: 8 (over y, core), lon: 4 (over z).
Axes of the slice: x: 4, y: 4, z: 4, core: 2. Of those that a mesh axis runs over, the one named last changes fastest.
Arguments:
- climate_driver_values: bfloat16 [4, 40, 16, 360], P('sec', None, 'lat', 'lon'), may hold values from -6 to 6
- oceanic_values_now: bfloat16 [4, 77, 64, 1440], P('sec', None, 'lat', 'lon'), may hold values from -6 to 6
- water_box_flags: int32 [64, 1440], P('lat', 'lon'), may hold values 0 or 1
- marine_patch_flags: int32 [8, 120], P('lat', 'lon'), may hold values from 0 to 1, as said below
- recorded_topmost_heat: float32 [64, 1440], P('lat', 'lon'), may hold values from -6 to 6
- air_intake_matrix: bfloat16 [40, 384], replicated, may hold values from -1 to 1
- fourier_inphase_mixer: bfloat16 [384, 384], replicated, may hold values from -0.3125 to 0.3125
- fourier_quadrature_mixer: bfloat16 [384, 384], replicated, may hold values from -0.3125 to 0.3125
- exchange_readout_matrix: bfloat16 [384, 8], replicated, may hold values from -0.3125 to 0.3125
- marine_intake_matrix: bfloat16 [85, 300], replicated, may hold values from -0.625 to 0.625
- perchannel_stencil: bfloat16 [49, 300], replicated, may hold values from -0.875 to 0.875
- standardize_scale: float32 [300], replicated, may hold values from 0.25 to 1.75
- marine_widening_matrix: bfloat16 [300, 1200], replicated, may hold values from -0.375 to 0.375
- marine_narrowing_matrix: bfloat16 [1200, 300], replicated, may hold values from -0.1875 to 0.1875
- marine_readout_matrix: bfloat16 [300, 77], replicated, may hold values from -0.375 to 0.375
Outputs:
- stepped_oceanic_values: bfloat16 [4, 77, 64, 1440], P('sec', None, 'lat', 'lon')
- pooled_skin_warmth: float32 [4, 16, 360], P('sec', 'lat', 'lon')
- cellwise_fair_score: float32 [64, 1440], P('lat', 'lon')
- probabilistic_skill: float32 [], replicated
The draws below stay inside these ranges and needn't reach their ends.
Inputs may be any that keep to these rules, and one draw needn't show every extreme that they name: `marine_patch_flags`: exactly 448 tiles are marked, and every tile of at least one aligned block of 1 tile rows by 30 tile columns is marked.
All inputs are finite; a program needn't handle non-finite values. No bound on the sum of `water_box_flags` on one device may be relied on, other than what follows from the above.
Results may differ from the reference program's by a relative error of at most 0.008.
Values may be sent and summed in bfloat16 or wider, within the bound.
A program may use at most 128 MiB of HBM per device.

```python
import math
import jax
import jax.numpy as jnp
from jax import lax

CLIMATE_CHANNELS = 40
CA = 384
WIND_LONGITUDES = 360
KM = 128
FLUX = 8
OCEANIC_CHANNELS = 77
CH = 300
HID = 1200
TH = 8
TW = 12
PREDICTION_RUNS = 4
WIND_LATITUDES = 16
OCEANIC_LATS = 64
OCEANIC_LONGS = 1440
CI = 85
ACTIVE = 448
N_LAT = 8
N_LON = 4


def draw_marine_patch_flags(key, part):
    key = jax.random.fold_in(key, 11)
    tile_rows = OCEANIC_LATS // TH
    tile_cols = OCEANIC_LONGS // TW
    rows_block = tile_rows // N_LAT
    cols_block = tile_cols // N_LON
    key_base, key_level, key_pick = jax.random.split(key, 3)
    base_score = jax.random.randint(key_base, (tile_rows, tile_cols), 0, 4096)
    block_level = jax.random.randint(key_level, (N_LAT, N_LON), 0, 3)
    chosen_block = jax.random.randint(key_pick, (), 0, N_LAT * N_LON)
    row_block = jnp.arange(tile_rows) // rows_block
    col_block = jnp.arange(tile_cols) // cols_block
    block_id = row_block[:, None] * N_LON + col_block[None, :]
    level_map = block_level[row_block][:, col_block]
    scores = base_score + 4096 * level_map + 16384 * (block_id == chosen_block).astype(jnp.int32)
    flat_scores = scores.reshape(-1) * (tile_rows * tile_cols) + jnp.arange(tile_rows * tile_cols, dtype=jnp.int32)
    picked = jax.lax.top_k(flat_scores, ACTIVE)[1]
    marked = jnp.zeros(tile_rows * tile_cols, jnp.int32).at[picked].set(1)
    return marked.reshape(tile_rows, tile_cols)


def draw_climate_driver_values(key, part):
    key = jax.random.fold_in(key, 23)
    key_noise, key_phase = jax.random.split(key, 2)
    shape = (PREDICTION_RUNS, CLIMATE_CHANNELS, WIND_LATITUDES, WIND_LONGITUDES)
    noise = jax.random.truncated_normal(key_noise, -3.5, 3.5, shape, jnp.float32)
    amplitude = 2.0
    phase = jax.random.uniform(key_phase, (PREDICTION_RUNS, 1, WIND_LATITUDES, 1), jnp.float32, -math.pi, math.pi)
    column = jnp.arange(WIND_LONGITUDES, dtype=jnp.int32)
    turns = (2 * KM - 1) * column % (2 * WIND_LONGITUDES)
    angle = turns.astype(jnp.float32) * (math.pi / WIND_LONGITUDES)
    pattern = amplitude * jnp.cos(angle[None, None, None, :] + phase)
    return (noise + pattern).astype(jnp.bfloat16)


def draw_recorded_topmost_heat(key, part):
    key = jax.random.fold_in(key, 29)
    shape = (OCEANIC_LATS, OCEANIC_LONGS)
    noise = jax.random.truncated_normal(key, -2.5, 2.5, shape, jnp.float32)
    row_share = jnp.arange(OCEANIC_LATS, dtype=jnp.int32).astype(jnp.float32) / OCEANIC_LATS
    col_share = jnp.arange(OCEANIC_LONGS, dtype=jnp.int32).astype(jnp.float32) / OCEANIC_LONGS
    trend = -1.0 + 3.0 * col_share[None, :] + 1.5 * row_share[:, None]
    return (noise + trend).astype(jnp.float32)


def set_ends(entries, rng, least, top_value):
    longest = entries.shape.index(max(entries.shape))
    spots = []
    for shift in (0, 1):
        where = [jax.random.randint(jax.random.fold_in(rng, axis), (), 0, length) for axis, length in enumerate(entries.shape)]
        where[longest] = (where[longest] + shift) % entries.shape[longest]
        spots.append(tuple(where))
    return entries.at[spots[0]].set(least).at[spots[1]].set(top_value)


def shard_levels(own_key, extent, cuts, low, top_value):
    factor_of, own = 1.0, jax.random.fold_in(own_key, 6)
    for dim, parts in cuts:
        draws = jnp.exp(jax.random.uniform(jax.random.fold_in(own, dim), (parts,), jnp.float32, low / len(cuts), top_value / len(cuts)))
        factor_of = factor_of * jnp.repeat(draws, extent[dim] // parts).reshape([-1 if axis == dim else 1 for axis in range(len(extent))])
    return factor_of


def scatter_about(rng, extent, scale, limit, shards=(), kind=jnp.bfloat16):
    array = scale * jax.random.normal(rng, extent, jnp.float32)
    if shards:
        array = array * shard_levels(rng, extent, shards, -0.22, 0.18)
    return jnp.clip(array, -limit, limit).astype(kind)


def setup_inputs(seed: int = 0) -> dict:
    splits = jax.random.split(jax.random.key(seed), 16)
    climate_driver_values = draw_climate_driver_values(jax.random.fold_in(splits[15], 71), 0)
    oceanic_values_now = scatter_about(splits[1], (PREDICTION_RUNS, OCEANIC_CHANNELS, OCEANIC_LATS, OCEANIC_LONGS), 1.0, 6.0, ((0, 4), (2, 8), (3, 4)))
    water_box_flags = set_ends((jax.random.randint(splits[2], (OCEANIC_LATS, OCEANIC_LONGS), 0, 10) < 7).astype(jnp.int32), jax.random.fold_in(splits[2], 1), 0, 1)
    marine_patch_flags = draw_marine_patch_flags(jax.random.fold_in(splits[15], 71), 0)
    recorded_topmost_heat = draw_recorded_topmost_heat(jax.random.fold_in(splits[15], 71), 0)
    air_intake_matrix = scatter_about(splits[5], (CLIMATE_CHANNELS, CA), CLIMATE_CHANNELS ** -0.5, 1.0)
    fourier_inphase_mixer = scatter_about(splits[6], (CA, CA), CA ** -0.5, 0.3125)
    fourier_quadrature_mixer = scatter_about(splits[7], (CA, CA), CA ** -0.5, 0.3125)
    exchange_readout_matrix = scatter_about(splits[8], (CA, FLUX), CA ** -0.5, 0.3125)
    marine_intake_matrix = scatter_about(splits[9], (CI, CH), CI ** -0.5, 0.625)
    perchannel_stencil = scatter_about(splits[10], (49, CH), 49 ** -0.5, 0.875)
    standardize_scale = jnp.clip(1.0 + 0.15 * jax.random.normal(splits[11], (CH,), jnp.float32), 0.25, 1.75)
    marine_widening_matrix = scatter_about(splits[12], (CH, HID), CH ** -0.5, 0.375)
    marine_narrowing_matrix = scatter_about(splits[13], (HID, CH), HID ** -0.5, 0.1875)
    marine_readout_matrix = scatter_about(splits[14], (CH, OCEANIC_CHANNELS), CH ** -0.5, 0.375)
    return dict(climate_driver_values=climate_driver_values, oceanic_values_now=oceanic_values_now, water_box_flags=water_box_flags, marine_patch_flags=marine_patch_flags, recorded_topmost_heat=recorded_topmost_heat, air_intake_matrix=air_intake_matrix, fourier_inphase_mixer=fourier_inphase_mixer, fourier_quadrature_mixer=fourier_quadrature_mixer, exchange_readout_matrix=exchange_readout_matrix, marine_intake_matrix=marine_intake_matrix, perchannel_stencil=perchannel_stencil, standardize_scale=standardize_scale, marine_widening_matrix=marine_widening_matrix, marine_narrowing_matrix=marine_narrowing_matrix, marine_readout_matrix=marine_readout_matrix)


PRECISE = lax.Precision.HIGHEST

def fourier_tables(length, mode_count):
    position = jnp.arange(length, dtype=jnp.int32)[:, None]
    wave_index = jnp.arange(mode_count, dtype=jnp.int32)[None, :]
    phase_angle = (position * wave_index % length).astype(jnp.float32) * (2.0 * math.pi / length)
    return (jnp.cos(phase_angle), jnp.sin(phase_angle))

def mode_weights(length, mode_count):
    wave_index = jnp.arange(mode_count, dtype=jnp.int32)
    return jnp.where(wave_index == 0, 1.0, 2.0).astype(jnp.float32) / length

def reference(climate_driver_values, oceanic_values_now, water_box_flags, marine_patch_flags, recorded_topmost_heat, air_intake_matrix, fourier_inphase_mixer, fourier_quadrature_mixer, exchange_readout_matrix, marine_intake_matrix, perchannel_stencil, standardize_scale, marine_widening_matrix, marine_narrowing_matrix, marine_readout_matrix):
    lifted = jnp.einsum('bail,ac->bcil', climate_driver_values.astype(jnp.float32), air_intake_matrix.astype(jnp.float32), precision=PRECISE).astype(jnp.bfloat16)
    lifted_wide = lifted.astype(jnp.float32)
    cosine, sine_table = fourier_tables(WIND_LONGITUDES, KM)
    scaled = mode_weights(WIND_LONGITUDES, KM)
    coef_re = jnp.einsum('bcil,lk->bcik', lifted_wide, cosine, precision=PRECISE)
    coef_im = -jnp.einsum('bcil,lk->bcik', lifted_wide, sine_table, precision=PRECISE)
    real_weight = fourier_inphase_mixer.astype(jnp.float32)
    imag_weight = fourier_quadrature_mixer.astype(jnp.float32)
    mix_re = jnp.einsum('bcik,cd->bdik', coef_re, real_weight, precision=PRECISE) - jnp.einsum('bcik,cd->bdik', coef_im, imag_weight, precision=PRECISE)
    mix_im = jnp.einsum('bcik,cd->bdik', coef_im, real_weight, precision=PRECISE) + jnp.einsum('bcik,cd->bdik', coef_re, imag_weight, precision=PRECISE)
    spectral = jnp.einsum('bcik,lk->bcil', mix_re * scaled, cosine, precision=PRECISE) - jnp.einsum('bcik,lk->bcil', mix_im * scaled, sine_table, precision=PRECISE)
    atm_hidden = (lifted_wide + jax.nn.gelu(spectral, approximate=False)).astype(jnp.bfloat16)
    fluxes = jnp.einsum('bcil,cf->bfil', atm_hidden.astype(jnp.float32), exchange_readout_matrix.astype(jnp.float32), precision=PRECISE).astype(jnp.bfloat16)
    up_flux = jnp.repeat(jnp.repeat(fluxes, 4, axis=2), 4, axis=3)
    sea_cells = water_box_flags.astype(jnp.bfloat16)
    ocean_in = jnp.concatenate([oceanic_values_now, up_flux], axis=1) * sea_cells
    cell_active = jnp.repeat(jnp.repeat(marine_patch_flags, TH, axis=0), TW, axis=1)
    update_mask = water_box_flags * cell_active > 0
    enc_weight = marine_intake_matrix.astype(jnp.float32)
    kernel_wide = perchannel_stencil.astype(jnp.float32)
    gain_wide = standardize_scale.astype(jnp.float32)

    def one_member(member_pair):
        member_in, member_state = member_pair
        encoded = jnp.einsum('aij,ac->cij', member_in.astype(jnp.float32), enc_weight, precision=PRECISE)
        padded = jnp.pad(encoded, ((0, 0), (3, 3), (0, 0)))
        padded = jnp.concatenate([padded[:, :, -3:], padded, padded[:, :, :3]], axis=2)
        convolved = jnp.zeros(encoded.shape, jnp.float32)
        for row_shift in range(7):
            for col_shift in range(7):
                convolved = convolved + kernel_wide[row_shift * 7 + col_shift][:, None, None] * padded[:, row_shift:row_shift + OCEANIC_LATS, col_shift:col_shift + OCEANIC_LONGS]
        channel_mean = lax.optimization_barrier(jnp.mean(convolved, axis=0, keepdims=True))
        centered = convolved - channel_mean
        variance = lax.optimization_barrier(jnp.mean(centered * centered, axis=0, keepdims=True))
        normed = (centered * lax.rsqrt(variance + 1e-06) * gain_wide[:, None, None]).astype(jnp.bfloat16)
        expanded = jax.nn.gelu(jnp.einsum('cij,ch->hij', normed.astype(jnp.float32), marine_widening_matrix.astype(jnp.float32), precision=PRECISE), approximate=False).astype(jnp.bfloat16)
        block_out = (encoded + jnp.einsum('hij,hc->cij', expanded.astype(jnp.float32), marine_narrowing_matrix.astype(jnp.float32), precision=PRECISE)).astype(jnp.bfloat16)
        increment = jnp.einsum('cij,co->oij', block_out.astype(jnp.float32), marine_readout_matrix.astype(jnp.float32), precision=PRECISE)
        updated_state = (member_state.astype(jnp.float32) + increment).astype(jnp.bfloat16)
        return jnp.where(update_mask[None], updated_state, member_state)
    stepped_oceanic_values = lax.map(one_member, (ocean_in, oceanic_values_now))
    adjusted_topmost_heat = stepped_oceanic_values[:, 0].astype(jnp.float32)
    latitude_cosine_share = update_mask.astype(jnp.float32)
    combined_weighted_accum = (adjusted_topmost_heat * latitude_cosine_share).reshape(PREDICTION_RUNS, WIND_LATITUDES, 4, WIND_LONGITUDES, 4).sum(axis=(2, 4))
    pooled_box_tally = latitude_cosine_share.reshape(WIND_LATITUDES, 4, WIND_LONGITUDES, 4).sum(axis=(1, 3))
    pooled_skin_warmth = combined_weighted_accum / jnp.maximum(pooled_box_tally, 1.0)
    prediction_deviation = lax.optimization_barrier(jnp.sum(jnp.abs(adjusted_topmost_heat - recorded_topmost_heat[None]), axis=0))
    runwise_spread_accum = lax.optimization_barrier(jnp.sum(jnp.abs(adjusted_topmost_heat[:, None] - adjusted_topmost_heat[None, :]), axis=(0, 1)))
    dispersion_epsilon = 0.05 / PREDICTION_RUNS
    cellwise_fair_score = prediction_deviation / PREDICTION_RUNS - (1.0 - dispersion_epsilon) / (2.0 * PREDICTION_RUNS * (PREDICTION_RUNS - 1)) * runwise_spread_accum
    latitude = 84.0 - 0.25 * (jnp.arange(OCEANIC_LATS).astype(jnp.float32) + 0.5)
    area_weight = jnp.cos(latitude * (math.pi / 180.0))[:, None] * latitude_cosine_share
    probabilistic_skill = jnp.sum(area_weight * cellwise_fair_score) / jnp.sum(area_weight)
    return (stepped_oceanic_values, pooled_skin_warmth, cellwise_fair_score, probabilistic_skill)
```

```python
import functools
import math

import jax
import jax.numpy as jnp
import numpy as np
from jax import lax
from jax.experimental import pallas as pl
from jax.experimental.pallas import tpu as pltpu
from jax.sharding import PartitionSpec as P

F32 = jnp.float32
BF16 = jnp.bfloat16
MESH = pl.DeviceIdType.MESH

WIND_LONGITUDES = 360
KM = 128
N_SEC, N_LAT, N_LON = 4, 8, 4
STATE = 77
SP = 80
CH = 300
CP = 304
HID = 1200
ROWS = 8
COLS = 360
WIDE = 384
DRV = 40
DP = 48
HALO = 3
KS = 7 * SP
KF = 64
PAIR = 2 * WIDE

DRIVER_MOVES = [(dl, k) for dl in (0, 1, -1) for k in range(N_LON) if (dl, k) != (0, 0)]
EDGE_MOVES = [(dl, k) for dl in (0, 1, -1) for k in (1, 3)]
ROW_MOVES = [1, -1]


def circle_tables():
    offset = np.arange(WIND_LONGITUDES)
    waves = np.arange(KM)
    weight = np.where(waves == 0, 1.0, 2.0) / WIND_LONGITUDES
    angle = 2.0 * math.pi / WIND_LONGITUDES * (offset[:, None] * waves[None, :] % WIND_LONGITUDES)
    low = (np.cos(angle) * weight).sum(1)
    quad = (np.sin(angle) * weight).sum(1)
    block = WIND_LONGITUDES // N_LON
    source = (block * np.arange(N_LON)[:, None] + np.arange(128)[None, :]).reshape(-1)
    real = np.tile(np.arange(128) < block, N_LON)
    target = np.arange(128) - 1
    gap = (source[:, None] - target[None, :]) % WIND_LONGITUDES
    keep = real[:, None] & (np.arange(128) < block + 2)[None, :]
    tables = [np.where(keep, t, 0.0) for t in (low[gap], quad[gap], (gap == 0) * 1.0)]
    return np.concatenate(tables, axis=1).astype(jnp.bfloat16)


def area_table():
    latitude = 84.0 - 0.25 * (np.arange(N_LAT * ROWS) + 0.5)
    cosine = np.cos(latitude * (math.pi / 180.0)).astype(np.float32)
    return np.broadcast_to(cosine.reshape(N_LAT, ROWS, 1), (N_LAT, ROWS, 128)).copy()


def iota(shape, dim):
    return lax.broadcasted_iota(jnp.int32, shape, dim)


def dot(a, b):
    return jnp.dot(a, b, preferred_element_type=F32)


def put_zeros(rows, cols):
    return jnp.zeros((rows, cols), F32)


def padded_to(x, rows, cols):
    if x.shape[1] < cols:
        x = jnp.concatenate([x, put_zeros(x.shape[0], cols - x.shape[1])], axis=1)
    if x.shape[0] < rows:
        x = jnp.concatenate([x, put_zeros(rows - x.shape[0], cols)], axis=0)
    return x


def gelu(x):
    return 0.5 * x * (1.0 + lax.erf(x * (0.5**0.5)))


def kernel(
    state, flags, tiles, heat, drivers, circle, area,
    air, inphase, quadrature, exchange, intake, stencil, gain, widening, narrowing, readout,
    stepped, pooled, score, skill,
    grid, base, edge_send, edge_recv, rows_recv, dx, xall,
    w_state, w_flux, w_wide, w_narrow, w_read, w_encf, gains, w_atm, w_lift, w_exch,
    xs, xf, hidden, fresh, x_own, x_all, part, part_lon, part2, part_lat,
    send_sem, recv_sem,
):
    sec, lat, lon = lax.axis_index("sec"), lax.axis_index("lat"), lax.axis_index("lon")

    def at(ds, dl, dk):
        return (
            lax.rem(sec + (ds + N_SEC), N_SEC),
            lax.rem(lat + (dl + N_LAT), N_LAT),
            lax.rem(lon + (dk + N_LON), N_LON),
        )

    partners = (
        [(0, dl, k) for dl, k in DRIVER_MOVES]
        + [(ds, 0, 0) for ds in range(1, N_SEC)]
        + [(0, dl, 0) for dl in range(2, N_LAT - 1)]
    )
    barrier = pltpu.get_barrier_semaphore()
    for step in partners:
        pl.semaphore_signal(barrier, inc=1, device_id=at(*step), device_id_type=MESH)

    driven = drivers[...].astype(F32)
    for i in range(2):
        dx[i] = padded_to(driven[:, i, :], DP, 128).astype(BF16)
    sea = flags[...].astype(F32)
    grid[:, :, 256:WIDE] = jnp.zeros((SP, ROWS, WIDE - 256), F32)
    grid[:STATE, :, :COLS] = state[...].astype(F32) * sea[None]
    grid[STATE, :, :COLS] = sea
    grid[STATE + 1 :] = jnp.zeros((SP - STATE - 1, ROWS, WIDE), F32)
    lane = iota((SP, 128), 1)
    left_edge = jnp.zeros((SP, 128), F32)
    right_edge = jnp.zeros((SP, 128), F32)
    for r in range(ROWS):
        row = pltpu.roll(grid[:, r, :], HALO, 1)
        base[r] = row.astype(BF16)
        here = (lane >= 3 * r) & (lane < 3 * r + 3)
        left_edge = jnp.where(here, pltpu.roll(row[:, :128], (3 * r - 3) % 128, 1), left_edge)
        right_edge = jnp.where(here, pltpu.roll(row[:, 256:], (3 * r - 104) % 128, 1), right_edge)
    edge_send[0] = left_edge.astype(BF16)
    edge_send[1] = right_edge.astype(BF16)

    pl.semaphore_wait(barrier, len(partners))

    copies = []

    def send(src, dst, step):
        n = len(copies)
        copy = pltpu.make_async_remote_copy(
            src_ref=src, dst_ref=dst, send_sem=send_sem.at[n], recv_sem=recv_sem.at[n],
            device_id=at(*step), device_id_type=MESH,
        )
        copy.start()
        copies.append(copy)
        return copy

    row_copies, edge_copies, driver_copies = [], [], []
    for dl, k in DRIVER_MOVES:
        slot = (-k) % N_LON
        if dl == 0:
            src, dst = dx, xall.at[slot, pl.ds(1, 2)]
        elif dl == 1:
            src, dst = dx.at[1], xall.at[slot, 0]
        else:
            src, dst = dx.at[0], xall.at[slot, 3]
        driver_copies.append(send(src, dst, (0, dl, k)))
    row_copies.append(send(base.at[pl.ds(5, 3)], rows_recv.at[pl.ds(0, 3)], (0, 1, 0)))
    row_copies.append(send(base.at[pl.ds(0, 3)], rows_recv.at[pl.ds(3, 3)], (0, -1, 0)))
    for dl, k in EDGE_MOVES:
        side = 0 if k == 1 else 1
        edge_copies.append(send(edge_send.at[1 - side], edge_recv.at[side, dl + 1], (0, dl, k)))
    xall[0, pl.ds(1, 2)] = dx[...]

    def turned(x, rows, cols):
        return jnp.transpose(padded_to(x, rows, cols))

    intake_wide = intake[...].astype(F32)
    intake_t = turned(intake_wide, 128, WIDE)[:CP].astype(BF16)
    stencil_t = turned(stencil[...].astype(F32), 128, WIDE)[:CP].astype(BF16)
    chan = iota((128, 640), 0)
    place = iota((128, 640), 1)
    repeat = jnp.zeros((128, 640), F32)
    for m in range(8):
        repeat = jnp.where((place - SP * m == chan) & (chan < STATE), 1.0, repeat)
    intake_rep = dot(intake_t, repeat.astype(BF16))
    for m in range(0, 49, 8):
        width = min(640, (49 - m) * SP)
        tap = place + SP * m - SP * chan
        select = jnp.where((tap >= 0) & (tap < SP), 1.0, 0.0).astype(BF16)
        taps = dot(stencil_t, select)
        w_state[:, SP * m : SP * m + width] = (taps * intake_rep)[:, :width].astype(BF16)
    chan = iota((128, 7 * KF), 0)
    place = iota((128, 7 * KF), 1)
    repeat = jnp.zeros((128, 7 * KF), F32)
    select = jnp.zeros((128, 7 * KF), F32)
    for u in range(7):
        for v in range(7):
            start = u * KF + 8 * v
            inside = (place >= start) & (place < start + 8)
            repeat = jnp.where(inside & (place - start + STATE == chan), 1.0, repeat)
            select = jnp.where(inside & (chan == 7 * u + v), 1.0, select)
    intake_flux = dot(intake_t, repeat.astype(BF16))
    w_flux[...] = (intake_flux * dot(stencil_t, select.astype(BF16))).astype(BF16)
    spot = iota((CP, KF), 1)
    w_encf[...] = jnp.where((spot >= 24) & (spot < 32), intake_flux[:, :KF], 0.0).astype(BF16)
    w_wide[...] = turned(widening[...].astype(F32), WIDE, 1280)[:HID, :CP].astype(BF16)
    both = jnp.concatenate([narrowing[...].astype(F32), intake_wide[:STATE], put_zeros(3, CH)], axis=0)
    w_narrow[...] = turned(both, 1280, WIDE)[:CP].astype(BF16)
    w_read[...] = turned(readout[...].astype(F32), WIDE, 128)[:SP, :CP].astype(BF16)
    gains[...] = jnp.transpose(jnp.broadcast_to(padded_to(gain[...], 1, WIDE), (128, WIDE)))[:CP]
    air_wide = padded_to(air[...].astype(F32), DP, 384)
    mixed = jnp.concatenate(
        [
            padded_to(dot(air[...], inphase[...]), DP, 384),
            padded_to(dot(air[...], quadrature[...]), DP, 384),
        ],
        axis=0,
    )
    w_atm[...] = turned(mixed, 128, 384).astype(BF16)
    w_lift[...] = turned(air_wide, 128, 384).astype(BF16)
    w_exch[...] = turned(exchange[...].astype(F32), 384, 128)[:16].astype(BF16)

    for copy in driver_copies:
        copy.wait_recv()
    circles = jnp.concatenate([xall[s].reshape(4 * DP, 128) for s in range(N_LON)], axis=1)
    filtered = dot(circles, circle[...])
    lanes_of = lambda t: jnp.concatenate(
        [filtered[i * DP : (i + 1) * DP, t * 128 : (t + 1) * 128] for i in range(4)], axis=1
    )
    smooth = jnp.concatenate([lanes_of(0), lanes_of(1), put_zeros(32, 512)], axis=0).astype(BF16)
    centre = jnp.concatenate([lanes_of(2), put_zeros(80, 512)], axis=0).astype(BF16)
    spectral = dot(w_atm[...], smooth)
    lifted = dot(w_lift[...], centre).astype(BF16).astype(F32)
    atm_hidden = (lifted + gelu(spectral)).astype(BF16)
    fluxes = dot(w_exch[...], atm_hidden)[:8]
    stacked = jnp.concatenate([fluxes[:, i * 128 : (i + 1) * 128] for i in range(4)], axis=0)
    box = 4 * iota((128, WIDE), 0) - 4
    column = iota((128, WIDE), 1) - HALO
    spread = jnp.where((column >= box) & (column < box + 4), 1.0, 0.0).astype(BF16)
    up_flux = dot(stacked.astype(BF16), spread)

    for copy in row_copies + edge_copies:
        copy.wait_recv()
    lane = iota((SP, WIDE), 1)
    for e in range(ROWS + 2 * HALO):
        if e < 3:
            row, r, dl = rows_recv[e].astype(F32), e + 5, 1
            row = jnp.where(lat == 0, 0.0, 1.0) * row
        elif e < 11:
            row, r, dl = base[e - 3].astype(F32), e - 3, 0
        else:
            row, r, dl = rows_recv[e - 8].astype(F32), e - 11, -1
        left = pltpu.roll(edge_recv[0, dl + 1].astype(F32), (-3 * r) % 128, 1)
        right = pltpu.roll(edge_recv[1, dl + 1].astype(F32), (107 - 3 * r) % 128, 1)
        row = jnp.where(lane < 3, jnp.concatenate([left, left, left], axis=1), row)
        row = jnp.where(lane >= 363, jnp.concatenate([right, right, right], axis=1), row)
        row = jnp.where(lane >= 366, 0.0, row)
        if e < 3:
            row = row * jnp.where(lat == 0, 0.0, 1.0)
        if e >= 11:
            row = row * jnp.where(lat == N_LAT - 1, 0.0, 1.0)
        flux_row = (0, 0, 0, 1, 1, 1, 1, 2, 2, 2, 2, 3, 3, 3)[e]
        flux = up_flux[8 * flux_row : 8 * flux_row + 8] * row[STATE : STATE + 1]
        places = [(p, h) for p, h in ((e, 0), (e - 1, 1)) if 0 <= p < 13]
        shifted_flux = []
        for v in range(7):
            shifted = row if v == 0 else pltpu.roll(row, WIDE - v, 1)
            shifted = shifted.astype(BF16)
            for p, h in places:
                xs[p, SP * v : SP * (v + 1), WIDE * h : WIDE * (h + 1)] = shifted
            shifted_flux.append(flux if v == 0 else pltpu.roll(flux, WIDE - v, 1))
        block = jnp.concatenate(shifted_flux + [put_zeros(8, WIDE)], axis=0).astype(BF16)
        for p, h in places:
            xf[p, :, WIDE * h : WIDE * (h + 1)] = block

    def two_rows(p, carry):
        r = 2 * p
        state_part = xs[pl.ds(r, 7)].reshape(7 * KS, PAIR)
        flux_part = xf[pl.ds(r, 7)].reshape(7 * KF, PAIR)
        conv = dot(w_state[...], state_part) + dot(w_flux[...], flux_part)
        mean = jnp.sum(conv, axis=0, keepdims=True) * (1.0 / CH)
        centered = jnp.where(iota((CP, PAIR), 0) < CH, conv - mean, 0.0)
        variance = jnp.sum(centered * centered, axis=0, keepdims=True) * (1.0 / CH)
        scale = jnp.concatenate([gains[...]] * (PAIR // 128), axis=1)
        normed = (centered * lax.rsqrt(variance + 1e-6) * scale).astype(BF16)
        hidden[:HID] = gelu(dot(w_wide[...], normed)).astype(BF16)
        middle = xs[r + 3, 3 * SP : 4 * SP]
        hidden[HID:] = middle
        block_out = dot(w_narrow[...], hidden[...]) + dot(w_encf[...], xf[r + 3])
        new = middle.astype(F32) + dot(w_read[...], block_out.astype(BF16))
        fresh[r] = new[:, :WIDE]
        fresh[r + 1] = new[:, WIDE:]
        return carry

    lax.fori_loop(0, ROWS // 2, two_rows, 0)

    for r in range(ROWS):
        grid[:, r, :] = fresh[r]
    tile = iota((32, WIDE), 0) * 12
    column = iota((32, WIDE), 1)
    widen_tiles = jnp.where((column >= tile) & (column < tile + 12), 1.0, 0.0).astype(BF16)
    marks = padded_to(tiles[...].astype(F32), 1, 32)
    marked = dot(jnp.broadcast_to(marks, (8, 32)).astype(BF16), widen_tiles)[:, :COLS]
    mask = sea * marked
    mask_wide = jnp.broadcast_to(mask[None], (STATE, ROWS, COLS))
    result = jnp.where(mask_wide > 0.5, grid[:STATE, :, :COLS], state[...].astype(F32)).astype(BF16)
    stepped[...] = result
    x = padded_to(result[0].astype(F32), ROWS, WIDE)
    x_own[...] = x
    x_all[sec] = x
    x_copies = [send(x_own, x_all.at[sec], (ds, 0, 0)) for ds in range(1, N_SEC)]

    mask = padded_to(mask, ROWS, WIDE)
    quad = iota((WIDE, 128), 1) * 4
    column = iota((WIDE, 128), 0)
    pool = jnp.where((column >= quad) & (column < quad + 4), 1.0, 0.0).astype(BF16)
    heat_boxes = dot((x * mask).astype(BF16), pool)
    count_boxes = dot(mask.astype(BF16), pool)
    for i in range(2):
        total = jnp.sum(heat_boxes[4 * i : 4 * i + 4], axis=0, keepdims=True)
        count = jnp.sum(count_boxes[4 * i : 4 * i + 4], axis=0, keepdims=True)
        pooled[i : i + 1, :] = (total / jnp.maximum(count, 1.0))[:, :90]
    weight = jnp.concatenate([area[lat]] * 3, axis=1) * mask
    seen = padded_to(heat[...], ROWS, WIDE)

    for copy in x_copies:
        copy.wait_recv()
    members = [x_all[m] for m in range(N_SEC)]
    deviation = sum(jnp.abs(m - seen) for m in members)
    gaps = sum(
        jnp.abs(members[m] - members[n]) for m in range(N_SEC) for n in range(m + 1, N_SEC)
    )
    epsilon = 0.05 / N_SEC
    fair = deviation * (1.0 / N_SEC) - (1.0 - epsilon) / (N_SEC * (N_SEC - 1)) * gaps
    score[...] = fair[:, :COLS]

    def folded(y):
        return y[:, :128] + y[:, 128:256] + y[:, 256:]

    part[0] = folded(weight * fair)
    part[1] = folded(weight)
    part_lon[lon] = part[...]
    lon_copies = [send(part, part_lon.at[lon], (0, 0, k)) for k in range(1, N_LON)]
    for copy in lon_copies:
        copy.wait_recv()
    total = part_lon[0] + part_lon[1] + part_lon[2] + part_lon[3]
    part2[...] = total
    part_lat[lat] = total
    lat_copies = [send(part2, part_lat.at[lat], (0, dl, 0)) for dl in range(1, N_LAT)]
    for copy in lat_copies:
        copy.wait_recv()
    total = part_lat[0]
    for m in range(1, N_LAT):
        total = total + part_lat[m]
    top = jnp.sum(jnp.sum(total[0], axis=1, keepdims=True), axis=0, keepdims=True)
    bottom = jnp.sum(jnp.sum(total[1], axis=1, keepdims=True), axis=0, keepdims=True)
    skill[...] = top / bottom

    for copy in copies:
        copy.wait_send()


N_COPIES = len(DRIVER_MOVES) + len(ROW_MOVES) + len(EDGE_MOVES) + 3 + 3 + 7


def on_device(*args):
    (drivers, state, flags, tiles, heat, air, inphase, quadrature, exchange, intake, stencil, gain,
     widening, narrowing, readout) = args
    vmem = pl.BlockSpec(memory_space=pltpu.VMEM)
    operands = (
        state[0], flags, tiles, heat, drivers[0], jnp.asarray(circle_tables()), jnp.asarray(area_table()),
        air, inphase, quadrature, exchange, intake, stencil, gain.reshape(1, CH),
        widening, narrowing, readout,
    )
    stepped, pooled, score, skill = pl.pallas_call(
        kernel,
        out_shape=(
            jax.ShapeDtypeStruct((STATE, ROWS, COLS), BF16),
            jax.ShapeDtypeStruct((2, 90), F32),
            jax.ShapeDtypeStruct((ROWS, COLS), F32),
            jax.ShapeDtypeStruct((1, 1), F32),
        ),
        in_specs=[vmem] * len(operands),
        out_specs=(vmem,) * 4,
        scratch_shapes=[
            pltpu.VMEM((SP, ROWS, WIDE), F32),
            pltpu.VMEM((ROWS, SP, WIDE), BF16),
            pltpu.VMEM((2, SP, 128), BF16),
            pltpu.VMEM((2, 3, SP, 128), BF16),
            pltpu.VMEM((6, SP, WIDE), BF16),
            pltpu.VMEM((2, DP, 128), BF16),
            pltpu.VMEM((N_LON, 4, DP, 128), BF16),
            pltpu.VMEM((CP, 7 * KS), BF16),
            pltpu.VMEM((CP, 7 * KF), BF16),
            pltpu.VMEM((HID, CP), BF16),
            pltpu.VMEM((CP, 1280), BF16),
            pltpu.VMEM((SP, CP), BF16),
            pltpu.VMEM((CP, KF), BF16),
            pltpu.VMEM((CP, 128), F32),
            pltpu.VMEM((384, 128), BF16),
            pltpu.VMEM((384, 128), BF16),
            pltpu.VMEM((16, 384), BF16),
            pltpu.VMEM((13, KS, PAIR), BF16),
            pltpu.VMEM((13, KF, PAIR), BF16),
            pltpu.VMEM((1280, PAIR), BF16),
            pltpu.VMEM((ROWS, SP, WIDE), F32),
            pltpu.VMEM((ROWS, WIDE), F32),
            pltpu.VMEM((N_SEC, ROWS, WIDE), F32),
            pltpu.VMEM((2, 8, 128), F32),
            pltpu.VMEM((N_LON, 2, 8, 128), F32),
            pltpu.VMEM((2, 8, 128), F32),
            pltpu.VMEM((N_LAT, 2, 8, 128), F32),
            pltpu.SemaphoreType.DMA((N_COPIES,)),
            pltpu.SemaphoreType.DMA((N_COPIES,)),
        ],
        compiler_params=pltpu.CompilerParams(
            collective_id=0, has_side_effects=True, vmem_limit_bytes=58 << 20
        ),
        name="coupled_step",
    )(*operands)
    return (
        stepped.reshape(1, STATE, ROWS, COLS),
        pooled.reshape(1, 2, 90),
        score,
        skill.reshape(()),
    )


def solution(mesh):
    in_specs = (
        P("sec", None, "lat", "lon"),
        P("sec", None, "lat", "lon"),
        P("lat", "lon"),
        P("lat", "lon"),
        P("lat", "lon"),
    ) + (P(),) * 10
    out_specs = (P("sec", None, "lat", "lon"), P("sec", "lat", "lon"), P("lat", "lon"), P())
    return jax.shard_map(
        on_device, mesh=mesh, in_specs=in_specs, out_specs=out_specs, check_vma=False
    )
```

```python
import functools
import math

import jax
import jax.numpy as jnp
import numpy as np
from jax import lax
from jax.experimental import pallas as pl
from jax.experimental.pallas import tpu as pltpu
from jax.sharding import PartitionSpec as P

F32 = jnp.float32
BF16 = jnp.bfloat16
MESH = pl.DeviceIdType.MESH

WIND_LONGITUDES = 360
KM = 128
N_SEC, N_LAT, N_LON = 4, 8, 4
STATE = 77
SP = 80
CH = 300
CP = 304
HID = 1200
ROWS = 8
COLS = 360
WIDE = 384
DRV = 40
DP = 48
HALO = 3
KS = 7 * SP
KF = 64
PAIR = 2 * WIDE

DRIVER_MOVES = [(dl, k) for dl in (0, 1, -1) for k in range(N_LON) if (dl, k) != (0, 0)]
EDGE_MOVES = [(dl, k) for dl in (0, 1, -1) for k in (1, 3)]
ROW_MOVES = [1, -1]


def circle_tables():
    offset = np.arange(WIND_LONGITUDES)
    waves = np.arange(KM)
    weight = np.where(waves == 0, 1.0, 2.0) / WIND_LONGITUDES
    angle = 2.0 * math.pi / WIND_LONGITUDES * (offset[:, None] * waves[None, :] % WIND_LONGITUDES)
    low = (np.cos(angle) * weight).sum(1)
    quad = (np.sin(angle) * weight).sum(1)
    block = WIND_LONGITUDES // N_LON
    source = (block * np.arange(N_LON)[:, None] + np.arange(128)[None, :]).reshape(-1)
    real = np.tile(np.arange(128) < block, N_LON)
    target = np.arange(128) - 1
    gap = (source[:, None] - target[None, :]) % WIND_LONGITUDES
    keep = real[:, None] & (np.arange(128) < block + 2)[None, :]
    tables = [np.where(keep, t, 0.0) for t in (low[gap], quad[gap], (gap == 0) * 1.0)]
    return np.concatenate(tables, axis=1).astype(np.float32)


def area_table():
    latitude = 84.0 - 0.25 * (np.arange(N_LAT * ROWS) + 0.5)
    cosine = np.cos(latitude * (math.pi / 180.0)).astype(np.float32)
    return np.broadcast_to(cosine.reshape(N_LAT, ROWS, 1), (N_LAT, ROWS, 128)).copy()


def iota(shape, dim):
    return lax.broadcasted_iota(jnp.int32, shape, dim)


def dot(a, b):
    return jnp.dot(a, b, preferred_element_type=F32)


def put_zeros(rows, cols):
    return jnp.zeros((rows, cols), F32)


def padded_to(x, rows, cols):
    if x.shape[1] < cols:
        x = jnp.concatenate([x, put_zeros(x.shape[0], cols - x.shape[1])], axis=1)
    if x.shape[0] < rows:
        x = jnp.concatenate([x, put_zeros(rows - x.shape[0], cols)], axis=0)
    return x


def gelu(x):
    return 0.5 * x * (1.0 + lax.erf(x * (0.5**0.5)))


def kernel(
    state_h, flags_h, tiles_h, heat_h, drivers_h, circle_h, area_h,
    air_h, inphase_h, quadrature_h, exchange_h, intake_h, stencil_h, gain_h, widening_h, narrowing_h, readout_h,
    stepped, pooled, score, skill,
    state, flags, tiles, heat, drivers, circle, area,
    air, inphase, quadrature, exchange, intake, stencil, gain, widening, narrowing, readout,
    grid, base, edge_send, edge_recv, rows_recv, dx, xall,
    w_all, w_from1, w_from3, w_from4, w_from6, w_flux, w_wide, w_narrow, w_read, w_encf, gains, w_atm, w_lift, w_exch,
    xs, xf, acc, hidden, fresh, out_buf, x_own, x_all, part, part_twin, pair, chips,
    load_sem, out_sem, send_sem, recv_sem,
):
    sec, lat, lon = lax.axis_index("sec"), lax.axis_index("lat"), lax.axis_index("lon")
    core = lax.rem(lat, 2)
    chip_y = lat // 2

    def at(ds, dl, dk):
        return (
            lax.rem(sec + (ds + N_SEC), N_SEC),
            lax.rem(lat + (dl + N_LAT), N_LAT),
            lax.rem(lon + (dk + N_LON), N_LON),
        )

    partners = [(0, dl, k) for dl, k in DRIVER_MOVES] + [(ds, 0, 0) for ds in range(1, N_SEC)]
    for (dl0, k0), (dl1, k1) in FAR_PARTNERS:
        partners.append((0, dl0 + core * (dl1 - dl0), k0 + core * (k1 - k0)))
    barrier = pltpu.get_barrier_semaphore()
    for step in partners:
        pl.semaphore_signal(barrier, inc=1, device_id=at(*step), device_id_type=MESH)

    loads = {}
    for n, (src, dst) in enumerate(
        [
            (flags_h, flags), (state_h, state), (drivers_h, drivers), (intake_h, intake), (stencil_h, stencil),
            (narrowing_h, narrowing), (widening_h, widening), (circle_h, circle), (air_h, air),
            (inphase_h, inphase), (quadrature_h, quadrature), (exchange_h, exchange), (gain_h, gain),
            (readout_h, readout), (tiles_h, tiles), (heat_h, heat), (area_h, area),
        ]
    ):
        copy = pltpu.make_async_copy(src, dst, load_sem.at[n])
        copy.start()
        loads[id(dst)] = copy

    def loaded(*refs):
        for ref in refs:
            loads.pop(id(ref)).wait()

    loaded(flags, state)
    sea = flags[...].astype(F32)
    grid[:, :, 256:WIDE] = jnp.zeros((SP, ROWS, WIDE - 256), F32)
    grid[:STATE, :, :COLS] = state[...].astype(F32) * sea[None]
    grid[STATE, :, :COLS] = sea
    grid[STATE + 1 :] = jnp.zeros((SP - STATE - 1, ROWS, WIDE), F32)
    lane = iota((SP, 128), 1)
    left_edge = jnp.zeros((SP, 128), F32)
    right_edge = jnp.zeros((SP, 128), F32)
    for r in range(ROWS):
        row = pltpu.roll(grid[:, r, :], HALO, 1)
        base[r] = row.astype(BF16)
        here = (lane >= 3 * r) & (lane < 3 * r + 3)
        left_edge = jnp.where(here, pltpu.roll(row[:, :128], (3 * r - 3) % 128, 1), left_edge)
        right_edge = jnp.where(here, pltpu.roll(row[:, 256:], (3 * r - 104) % 128, 1), right_edge)
    edge_send[0] = left_edge.astype(BF16)
    edge_send[1] = right_edge.astype(BF16)
    loaded(drivers)
    driven = drivers[...].astype(F32)
    for i in range(2):
        dx[i] = padded_to(driven[:, i, :], DP, 128).astype(BF16)

    pl.semaphore_wait(barrier, len(partners))

    copies = []

    def send(src, dst, step):
        n = len(copies)
        copy = pltpu.make_async_remote_copy(
            src_ref=src, dst_ref=dst, send_sem=send_sem.at[n], recv_sem=recv_sem.at[n],
            device_id=at(*step), device_id_type=MESH,
        )
        copy.start()
        copies.append(copy)
        return copy

    row_copies, edge_copies, driver_copies = [], [], []
    row_copies.append(send(base.at[pl.ds(5, 3)], rows_recv.at[pl.ds(0, 3)], (0, 1, 0)))
    row_copies.append(send(base.at[pl.ds(0, 3)], rows_recv.at[pl.ds(3, 3)], (0, -1, 0)))
    for dl, k in DRIVER_MOVES:
        slot = (-k) % N_LON
        if dl == 0:
            src, dst = dx, xall.at[slot, pl.ds(1, 2)]
        elif dl == 1:
            src, dst = dx.at[1], xall.at[slot, 0]
        else:
            src, dst = dx.at[0], xall.at[slot, 3]
        driver_copies.append(send(src, dst, (0, dl, k)))
    for dl, k in EDGE_MOVES:
        side = 0 if k == 1 else 1
        edge_copies.append(send(edge_send.at[1 - side], edge_recv.at[side, dl + 1], (0, dl, k)))
    xall[0, pl.ds(1, 2)] = dx[...]

    def turned(x, rows, cols):
        return jnp.transpose(padded_to(x, rows, cols))

    loaded(intake, stencil)
    intake_wide = intake[...].astype(F32)
    intake_t = turned(intake_wide, 128, WIDE)[:CP].astype(BF16)
    stencil_t = turned(stencil[...].astype(F32), 128, WIDE)[:CP].astype(BF16)
    chan = iota((128, 640), 0)
    place = iota((128, 640), 1)
    repeat = jnp.zeros((128, 640), F32)
    for m in range(8):
        repeat = jnp.where((place - SP * m == chan) & (chan < STATE), 1.0, repeat)
    intake_rep = dot(intake_t, repeat.astype(BF16))
    for ref, first in ((w_all, 0), (w_from1, 7), (w_from3, 21), (w_from4, 28), (w_from6, 42)):
        for m in range(first, 49, 8):
            width = min(640, (49 - m) * SP)
            tap = place + SP * m - SP * chan
            select = jnp.where((tap >= 0) & (tap < SP), 1.0, 0.0).astype(BF16)
            taps = dot(stencil_t, select)
            begin = SP * (m - first)
            ref[:, begin : begin + width] = (taps * intake_rep)[:, :width].astype(BF16)

    def own_columns(row, e):
        places = [(p, h) for p, h in ((e, 0), (e - 1, 1)) if 0 <= p < 13]
        for v in range(7):
            shifted = pltpu.roll(row, WIDE - 52 - v, 1)[:, :256].astype(BF16)
            for p, h in places:
                xs[p, SP * v : SP * (v + 1), 256 * h : 256 * (h + 1)] = shifted

    for e in range(3, 11):
        own_columns(base[e - 3].astype(F32), e)

    def stack(first, count):
        return xs[first : first + count].reshape(count * KS, 512)

    acc[0] = dot(w_from3[...], stack(3, 4))
    acc[1] = dot(w_from1[...], stack(3, 6))
    acc[2] = dot(w_all[:, : 6 * KS], stack(4, 6))
    acc[3] = dot(w_all[:, : 4 * KS], stack(6, 4))

    chan = iota((128, 7 * KF), 0)
    place = iota((128, 7 * KF), 1)
    repeat = jnp.zeros((128, 7 * KF), F32)
    select = jnp.zeros((128, 7 * KF), F32)
    for u in range(7):
        for v in range(7):
            start = u * KF + 8 * v
            inside = (place >= start) & (place < start + 8)
            repeat = jnp.where(inside & (place - start + STATE == chan), 1.0, repeat)
            select = jnp.where(inside & (chan == 7 * u + v), 1.0, select)
    intake_flux = dot(intake_t, repeat.astype(BF16))
    w_flux[...] = (intake_flux * dot(stencil_t, select.astype(BF16))).astype(BF16)
    spot = iota((CP, KF), 1)
    w_encf[...] = jnp.where((spot >= 24) & (spot < 32), intake_flux[:, :KF], 0.0).astype(BF16)
    loaded(widening, narrowing, readout, gain)
    w_wide[...] = turned(widening[...].astype(F32), WIDE, 1280)[:HID, :CP].astype(BF16)
    w_narrow[:, :HID] = padded_to(narrowing[...].astype(F32), CP, HID).astype(BF16)
    keep = iota((CP, SP), 1) < STATE
    w_narrow[:, HID:] = jnp.where(keep, intake_t[:, :SP].astype(F32), 0.0).astype(BF16)
    w_read[...] = padded_to(readout[...].astype(F32), SP, CP).astype(BF16)
    gains[...] = jnp.transpose(jnp.broadcast_to(padded_to(gain[...].reshape(1, CH), 1, WIDE), (128, WIDE)))[:CP]
    loaded(air, inphase, quadrature, exchange, circle)
    air_wide = padded_to(air[...].astype(F32), DP, 384)
    mixed = jnp.concatenate(
        [
            padded_to(dot(air[...], inphase[...]), DP, 384),
            padded_to(dot(air[...], quadrature[...]), DP, 384),
        ],
        axis=0,
    )
    w_atm[...] = turned(mixed, 128, 384).astype(BF16)
    w_lift[...] = turned(air_wide, 128, 384).astype(BF16)
    w_exch[...] = padded_to(exchange[...].astype(F32), 16, 384).astype(BF16)

    for copy in driver_copies:
        copy.wait_recv()
    circles = jnp.concatenate([xall[s].reshape(4 * DP, 128) for s in range(N_LON)], axis=1)
    filtered = dot(circles, circle[...].astype(BF16))
    lanes_of = lambda t: jnp.concatenate(
        [filtered[i * DP : (i + 1) * DP, t * 128 : (t + 1) * 128] for i in range(4)], axis=1
    )
    smooth = jnp.concatenate([lanes_of(0), lanes_of(1), put_zeros(32, 512)], axis=0).astype(BF16)
    centre = jnp.concatenate([lanes_of(2), put_zeros(80, 512)], axis=0).astype(BF16)
    spectral = dot(w_atm[...], smooth)
    lifted = dot(w_lift[...], centre).astype(BF16).astype(F32)
    atm_hidden = (lifted + gelu(spectral)).astype(BF16)
    fluxes = dot(w_exch[...], atm_hidden)[:8]
    stacked = jnp.concatenate([fluxes[:, i * 128 : (i + 1) * 128] for i in range(4)], axis=0)
    box = 4 * iota((128, WIDE), 0) - 4
    column = iota((128, WIDE), 1) - HALO
    spread = jnp.where((column >= box) & (column < box + 4), 1.0, 0.0).astype(BF16)
    up_flux = dot(stacked.astype(BF16), spread)

    for copy in row_copies + edge_copies:
        copy.wait_recv()
    lane = iota((SP, 128), 1)
    flux_lane = iota((8, 128), 1)

    def wrapped(first, last, v, lanes):
        return pltpu.roll(jnp.where(lanes >= 52 + v, last, first), 76 - v, 1)

    for e in range(ROWS + 2 * HALO):
        if e < 3:
            row, r, dl = rows_recv[e].astype(F32), e + 5, 1
        elif e < 11:
            row, r, dl = base[e - 3].astype(F32), e - 3, 0
        else:
            row, r, dl = rows_recv[e - 8].astype(F32), e - 11, -1
        left = pltpu.roll(edge_recv[0, dl + 1].astype(F32), (-3 * r) % 128, 1)
        right = pltpu.roll(edge_recv[1, dl + 1].astype(F32), (107 - 3 * r) % 128, 1)
        first = jnp.where(lane < 3, left, row[:, :128])
        last = jnp.where(lane >= 107, right, row[:, 256:])
        last = jnp.where(lane >= 110, 0.0, last)
        row = jnp.concatenate([first, row[:, 128:256], last], axis=1)
        if e < 3:
            row = row * jnp.where(lat == 0, 0.0, 1.0)
        if e >= 11:
            row = row * jnp.where(lat == N_LAT - 1, 0.0, 1.0)
        if e < 3 or e >= 11:
            own_columns(row, e)
        flux_row = (0, 0, 0, 1, 1, 1, 1, 2, 2, 2, 2, 3, 3, 3)[e]
        flux = up_flux[8 * flux_row : 8 * flux_row + 8] * row[STATE : STATE + 1]
        pairs = [(p, h) for p, h in ((e, 0), (e - 1, 1)) if 0 <= p < 13]
        quads = [(13 + e - h, h) for h in range(4) if 0 <= e - h < 11]
        inner, outer = [], []
        for v in range(7):
            shifted = wrapped(row[:, :128], row[:, 256:], v, lane).astype(BF16)
            for p, h in quads:
                xs[p, SP * v : SP * (v + 1), 128 * h : 128 * (h + 1)] = shifted
            inner.append(pltpu.roll(flux, WIDE - 52 - v, 1)[:, :256])
            outer.append(wrapped(flux[:, :128], flux[:, 256:], v, flux_lane))
        inner = jnp.concatenate(inner + [put_zeros(8, 256)], axis=0).astype(BF16)
        outer = jnp.concatenate(outer + [put_zeros(8, 128)], axis=0).astype(BF16)
        for p, h in pairs:
            xf[p, :, 256 * h : 256 * (h + 1)] = inner
        for p, h in quads:
            xf[p, :, 128 * h : 128 * (h + 1)] = outer

    def flux_stack(first):
        return dot(w_flux[...], xf[first : first + 7].reshape(7 * KF, 512))

    acc[0] = acc[0] + dot(w_all[:, : 3 * KS], stack(0, 3)) + flux_stack(0)
    acc[1] = acc[1] + dot(w_all[:, :KS], stack(2, 1)) + flux_stack(2)
    acc[2] = acc[2] + dot(w_from6[...], stack(10, 1)) + flux_stack(4)
    acc[3] = acc[3] + dot(w_from4[...], stack(10, 3)) + flux_stack(6)
    acc[4] = dot(w_all[...], stack(13, 7)) + flux_stack(13)
    acc[5] = dot(w_all[...], stack(17, 7)) + flux_stack(17)

    def group(g, carry):
        r = jnp.where(g < 4, 2 * g, 4 * g - 3)
        conv = acc[g]
        mean = jnp.sum(conv, axis=0, keepdims=True) * (1.0 / CH)
        centered = jnp.where(iota((CP, 512), 0) < CH, conv - mean, 0.0)
        variance = jnp.sum(centered * centered, axis=0, keepdims=True) * (1.0 / CH)
        scale = jnp.concatenate([gains[...]] * 4, axis=1)
        normed = (centered * lax.rsqrt(variance + 1e-6) * scale).astype(BF16)
        hidden[:HID] = gelu(dot(w_wide[...], normed)).astype(BF16)
        middle = xs[r + 3, 3 * SP : 4 * SP]
        hidden[HID:] = middle
        block_out = dot(w_narrow[...], hidden[...]) + dot(w_encf[...], xf[r + 3])
        fresh[g] = middle.astype(F32) + dot(w_read[...], block_out.astype(BF16))
        return carry

    lax.fori_loop(0, 6, group, 0)

    def fresh_row(r, rows):
        inner = fresh[r // 2, :rows, 256 * (r % 2) : 256 * (r % 2 + 1)]
        outer = fresh[4 + r // 4, :rows, 128 * (r % 4) : 128 * (r % 4 + 1)]
        return jnp.concatenate([inner, outer], axis=1)

    loaded(tiles)
    tile = iota((32, WIDE), 0) * 12
    column = iota((32, WIDE), 1)
    widen_tiles = jnp.where((column >= tile) & (column < tile + 12), 1.0, 0.0).astype(BF16)
    marks = padded_to(tiles[...].astype(F32), 1, 32)
    marked = dot(jnp.broadcast_to(marks, (8, 32)).astype(BF16), widen_tiles)
    mask = padded_to(sea, ROWS, WIDE) * marked
    x_new = jnp.concatenate([fresh_row(r, 8)[:1] for r in range(ROWS)], axis=0)
    x_new = pltpu.roll(x_new, 52, 1).astype(BF16).astype(F32)
    x = jnp.where(mask > 0.5, x_new, padded_to(state[0].astype(F32), ROWS, WIDE))
    x_own[...] = x
    x_all[sec] = x
    x_copies = [send(x_own, x_all.at[sec], (ds, 0, 0)) for ds in (2, 1, 3)]

    for r in range(ROWS):
        grid[:, r, :] = pltpu.roll(fresh_row(r, SP), 52, 1)
    mask_wide = jnp.broadcast_to(mask[None, :, :COLS], (STATE, ROWS, COLS))
    out_buf[...] = jnp.where(mask_wide > 0.5, grid[:STATE, :, :COLS], state[...].astype(F32)).astype(BF16)
    out_copy = pltpu.make_async_copy(out_buf, stepped, out_sem)
    out_copy.start()

    quad = iota((WIDE, 128), 1) * 4
    column = iota((WIDE, 128), 0)
    pool = jnp.where((column >= quad) & (column < quad + 4), 1.0, 0.0).astype(BF16)
    heat_boxes = dot((x * mask).astype(BF16), pool)
    count_boxes = dot(mask.astype(BF16), pool)
    for i in range(2):
        total = jnp.sum(heat_boxes[4 * i : 4 * i + 4], axis=0, keepdims=True)
        count = jnp.sum(count_boxes[4 * i : 4 * i + 4], axis=0, keepdims=True)
        pooled[i : i + 1, :] = (total / jnp.maximum(count, 1.0))[:, :90]
    loaded(area, heat)
    weight = jnp.concatenate([area[lat]] * 3, axis=1) * mask
    seen = padded_to(heat[...], ROWS, WIDE)

    def folded(y):
        return jnp.sum(y[:, :128] + y[:, 128:256] + y[:, 256:], axis=0, keepdims=True)

    area_sum = folded(weight)

    for copy in x_copies:
        copy.wait_recv()
    members = [x_all[m] for m in range(N_SEC)]
    deviation = sum(jnp.abs(m - seen) for m in members)
    gaps = sum(
        jnp.abs(members[m] - members[n]) for m in range(N_SEC) for n in range(m + 1, N_SEC)
    )
    epsilon = 0.05 / N_SEC
    fair = deviation * (1.0 / N_SEC) - (1.0 - epsilon) / (N_SEC * (N_SEC - 1)) * gaps
    score[...] = fair[:, :COLS]

    part[...] = jnp.concatenate([folded(weight * fair), area_sum, put_zeros(6, 128)], axis=0)
    twin = (0, 1 - 2 * core, 0)
    twin_copy = send(part, part_twin, twin)
    twin_copy.wait_recv()
    both = part[...] + part_twin[...]
    pair[...] = both

    def slot_of(y, z):
        return lax.rem(y, 2) * 8 + (y // 2) * 4 + z

    mine = slot_of(chip_y, lon)
    chips[core * 16 + (1 - core) * mine] = both
    chip_copies = []
    for dy, dz in ((2, 2), (2, 1), (2, 3), (0, 2), (2, 0), (0, 1), (0, 3)):
        chip_copies.append(send(pair, chips.at[mine], (0, 2 * (dy + core), dz)))
    chip_copies.append(send(pair, chips.at[core * mine + (1 - core) * 17], (0, 2, 0)))
    for copy in chip_copies:
        copy.wait_recv()
    here = pl.ds(lax.rem(chip_y + core, 2) * 8, 8)
    half_copy = send(chips.at[here], chips.at[here], twin)
    half_copy.wait_recv()
    total = chips[0]
    for m in range(1, 16):
        total = total + chips[m]
    sums = jnp.sum(total, axis=1, keepdims=True)
    skill[...] = sums[0:1] / sums[1:2]

    for copy in copies:
        copy.wait_send()
    out_copy.wait()


FAR_PARTNERS = list(
    zip(
        [(4, 0), (4, 1), (4, 2), (4, 3), (2, 0), (6, 0), (2, 1), (6, 3)],
        [(2, 0), (2, 1), (2, 2), (2, 3), (6, 0), (6, 1), (6, 2), (6, 3)],
    )
)
N_COPIES = len(DRIVER_MOVES) + len(ROW_MOVES) + len(EDGE_MOVES) + 3 + 1 + 8 + 1


def hand_over(*refs):
    count = len(refs) // 2
    for n in range(count):
        refs[count + n][...] = refs[n][...]


def on_device(*args):
    (drivers, state, flags, tiles, heat, air, inphase, quadrature, exchange, intake, stencil, gain,
     widening, narrowing, readout) = args
    anywhere = pl.BlockSpec(memory_space=pl.ANY)
    vmem = pl.BlockSpec(memory_space=pltpu.VMEM)
    operands = (
        state[0], flags, tiles, heat, drivers[0], jnp.asarray(circle_tables()), jnp.asarray(area_table()),
        air, inphase, quadrature, exchange.T, intake, stencil, gain,
        widening, narrowing.T, readout.T,
    )
    outputs = (
        jax.ShapeDtypeStruct((STATE, ROWS, COLS), BF16),
        jax.ShapeDtypeStruct((2, 90), F32),
        jax.ShapeDtypeStruct((ROWS, COLS), F32),
        jax.ShapeDtypeStruct((1, 1), F32),
    )
    results = pl.pallas_call(
        kernel,
        out_shape=outputs,
        in_specs=[anywhere] * len(operands),
        out_specs=(anywhere, vmem, vmem, vmem),
        scratch_shapes=[pltpu.VMEM(x.shape, x.dtype) for x in operands]
        + [
            pltpu.VMEM((SP, ROWS, WIDE), F32),
            pltpu.VMEM((ROWS, SP, WIDE), BF16),
            pltpu.VMEM((2, SP, 128), BF16),
            pltpu.VMEM((2, 3, SP, 128), BF16),
            pltpu.VMEM((6, SP, WIDE), BF16),
            pltpu.VMEM((2, DP, 128), BF16),
            pltpu.VMEM((N_LON, 4, DP, 128), BF16),
            pltpu.VMEM((CP, 7 * KS), BF16),
            pltpu.VMEM((CP, 6 * KS), BF16),
            pltpu.VMEM((CP, 4 * KS), BF16),
            pltpu.VMEM((CP, 3 * KS), BF16),
            pltpu.VMEM((CP, KS), BF16),
            pltpu.VMEM((CP, 7 * KF), BF16),
            pltpu.VMEM((HID, CP), BF16),
            pltpu.VMEM((CP, 1280), BF16),
            pltpu.VMEM((SP, CP), BF16),
            pltpu.VMEM((CP, KF), BF16),
            pltpu.VMEM((CP, 128), F32),
            pltpu.VMEM((384, 128), BF16),
            pltpu.VMEM((384, 128), BF16),
            pltpu.VMEM((16, 384), BF16),
            pltpu.VMEM((24, KS, 512), BF16),
            pltpu.VMEM((24, KF, 512), BF16),
            pltpu.VMEM((6, CP, 512), F32),
            pltpu.VMEM((1280, 512), BF16),
            pltpu.VMEM((6, SP, 512), F32),
            pltpu.VMEM((STATE, ROWS, COLS), BF16),
            pltpu.VMEM((ROWS, WIDE), F32),
            pltpu.VMEM((N_SEC, ROWS, WIDE), F32),
            pltpu.VMEM((8, 128), F32),
            pltpu.VMEM((8, 128), F32),
            pltpu.VMEM((8, 128), F32),
            pltpu.VMEM((18, 8, 128), F32),
            pltpu.SemaphoreType.DMA((len(operands),)),
            pltpu.SemaphoreType.DMA,
            pltpu.SemaphoreType.DMA((N_COPIES,)),
            pltpu.SemaphoreType.DMA((N_COPIES,)),
        ],
        compiler_params=pltpu.CompilerParams(
            collective_id=0, has_side_effects=True, vmem_limit_bytes=58 << 20
        ),
        name="coupled_step",
    )(*operands)
    stepped, pooled, score, skill = pl.pallas_call(
        hand_over,
        out_shape=outputs,
        in_specs=[vmem] * 4,
        out_specs=(vmem,) * 4,
        name="hand_over",
    )(*results)
    return (
        stepped.reshape(1, STATE, ROWS, COLS),
        pooled.reshape(1, 2, 90),
        score,
        skill.reshape(()),
    )


def solution(mesh):
    in_specs = (
        P("sec", None, "lat", "lon"),
        P("sec", None, "lat", "lon"),
        P("lat", "lon"),
        P("lat", "lon"),
        P("lat", "lon"),
    ) + (P(),) * 10
    out_specs = (P("sec", None, "lat", "lon"), P("sec", "lat", "lon"), P("lat", "lon"), P())
    return jax.shard_map(
        on_device, mesh=mesh, in_specs=in_specs, out_specs=out_specs, check_vma=False
    )
```

```python
import functools
import math

import jax
import jax.numpy as jnp
import numpy as np
from jax import lax
from jax.experimental import pallas as pl
from jax.experimental.pallas import tpu as pltpu
from jax.sharding import PartitionSpec as P

F32 = jnp.float32
BF16 = jnp.bfloat16
MESH = pl.DeviceIdType.MESH

WIND_LONGITUDES = 360
KM = 128
N_SEC, N_LAT, N_LON = 4, 8, 4
STATE = 77
SP = 80
CH = 300
CP = 304
HID = 1200
ROWS = 8
COLS = 360
WIDE = 384
DRV = 40
DP = 48
HALO = 3
KS = 640
KF = 64
HK = HID + SP + KF

DRIVER_MOVES = [(dl, k) for dl in (0, 1, -1) for k in range(N_LON) if (dl, k) != (0, 0)]
EDGE_MOVES = [(dl, k) for dl in (0, 1, -1) for k in (1, 3)]
ROW_MOVES = [1, -1]


def circle_tables():
    offset = np.arange(WIND_LONGITUDES)
    waves = np.arange(KM)
    weight = np.where(waves == 0, 1.0, 2.0) / WIND_LONGITUDES
    angle = 2.0 * math.pi / WIND_LONGITUDES * (offset[:, None] * waves[None, :] % WIND_LONGITUDES)
    low = (np.cos(angle) * weight).sum(1)
    quad = (np.sin(angle) * weight).sum(1)
    block = WIND_LONGITUDES // N_LON
    source = (block * np.arange(N_LON)[:, None] + np.arange(128)[None, :]).reshape(-1)
    real = np.tile(np.arange(128) < block, N_LON)
    target = np.arange(128) - 1
    gap = (source[:, None] - target[None, :]) % WIND_LONGITUDES
    keep = real[:, None] & (np.arange(128) < block + 2)[None, :]
    tables = [np.where(keep, t, 0.0) for t in (low[gap], quad[gap], (gap == 0) * 1.0)]
    return np.concatenate(tables, axis=1).astype(np.float32)


def area_table():
    latitude = 84.0 - 0.25 * (np.arange(N_LAT * ROWS) + 0.5)
    cosine = np.cos(latitude * (math.pi / 180.0)).astype(np.float32)
    return np.broadcast_to(cosine.reshape(N_LAT, ROWS, 1), (N_LAT, ROWS, 128)).copy()


def iota(shape, dim):
    return lax.broadcasted_iota(jnp.int32, shape, dim)


def dot(a, b):
    return jnp.dot(a, b, preferred_element_type=F32)


def put_zeros(rows, cols):
    return jnp.zeros((rows, cols), F32)


def padded_to(x, rows, cols):
    if x.shape[1] < cols:
        x = jnp.concatenate([x, put_zeros(x.shape[0], cols - x.shape[1])], axis=1)
    if x.shape[0] < rows:
        x = jnp.concatenate([x, put_zeros(rows - x.shape[0], cols)], axis=0)
    return x


def gelu(x):
    return 0.5 * x * (1.0 + lax.erf(x * (0.5**0.5)))


def kernel(
    state_h, flags_h, tiles_h, heat_h, drivers_h, circle_h, area_h,
    air_h, inphase_h, quadrature_h, exchange_h, intake_h, stencil_h, gain_h, widening_h, narrowing_h, readout_h,
    stepped, pooled, score, skill,
    state, flags, tiles, heat, drivers, circle, area,
    air, inphase, quadrature, exchange, intake, stencil, gain, widening, narrowing, readout,
    grid, base, edge_send, edge_recv, rows_recv, dx, xall,
    w_all, w_flux, w_wide, w_out, gains, w_atm, w_lift, w_exch,
    xs, xf, acc, hidden, fresh, out_buf, x_own, x_all, part, part_twin, pair, chips,
    load_sem, out_sem, send_sem, recv_sem,
):
    sec, lat, lon = lax.axis_index("sec"), lax.axis_index("lat"), lax.axis_index("lon")
    core = lax.rem(lat, 2)
    chip_y = lat // 2

    def at(ds, dl, dk):
        return (
            lax.rem(sec + (ds + N_SEC), N_SEC),
            lax.rem(lat + (dl + N_LAT), N_LAT),
            lax.rem(lon + (dk + N_LON), N_LON),
        )

    partners = [(0, dl, k) for dl, k in DRIVER_MOVES] + [(ds, 0, 0) for ds in range(1, N_SEC)]
    for (dl0, k0), (dl1, k1) in FAR_PARTNERS:
        partners.append((0, dl0 + core * (dl1 - dl0), k0 + core * (k1 - k0)))
    barrier = pltpu.get_barrier_semaphore()
    for step in partners:
        pl.semaphore_signal(barrier, inc=1, device_id=at(*step), device_id_type=MESH)

    loads = {}
    for n, (src, dst) in enumerate(
        [
            (flags_h, flags), (state_h, state), (drivers_h, drivers), (intake_h, intake), (stencil_h, stencil),
            (narrowing_h, narrowing), (widening_h, widening), (circle_h, circle), (air_h, air),
            (inphase_h, inphase), (quadrature_h, quadrature), (exchange_h, exchange), (gain_h, gain),
            (readout_h, readout), (tiles_h, tiles), (heat_h, heat), (area_h, area),
        ]
    ):
        copy = pltpu.make_async_copy(src, dst, load_sem.at[n])
        copy.start()
        loads[id(dst)] = copy

    def loaded(*refs):
        for ref in refs:
            loads.pop(id(ref)).wait()

    loaded(flags, state)
    sea = flags[...].astype(F32)
    grid[:, :, 256:WIDE] = jnp.zeros((SP, ROWS, WIDE - 256), F32)
    grid[:STATE, :, :COLS] = state[...].astype(F32) * sea[None]
    grid[STATE, :, :COLS] = sea
    grid[STATE + 1 :] = jnp.zeros((SP - STATE - 1, ROWS, WIDE), F32)
    lane = iota((SP, 128), 1)
    left_edge = jnp.zeros((SP, 128), F32)
    right_edge = jnp.zeros((SP, 128), F32)
    for r in range(ROWS):
        row = pltpu.roll(grid[:, r, :], HALO, 1)
        base[r] = row.astype(BF16)
        here = (lane >= 3 * r) & (lane < 3 * r + 3)
        left_edge = jnp.where(here, pltpu.roll(row[:, :128], (3 * r - 3) % 128, 1), left_edge)
        right_edge = jnp.where(here, pltpu.roll(row[:, 256:], (3 * r - 104) % 128, 1), right_edge)
    edge_send[0] = left_edge.astype(BF16)
    edge_send[1] = right_edge.astype(BF16)
    loaded(drivers)
    driven = drivers[...].astype(F32)
    for i in range(2):
        dx[i] = padded_to(driven[:, i, :], DP, 128).astype(BF16)

    pl.semaphore_wait(barrier, len(partners))

    copies = []

    def send(src, dst, step):
        n = len(copies)
        copy = pltpu.make_async_remote_copy(
            src_ref=src, dst_ref=dst, send_sem=send_sem.at[n], recv_sem=recv_sem.at[n],
            device_id=at(*step), device_id_type=MESH,
        )
        copy.start()
        copies.append(copy)
        return copy

    row_copies, edge_copies, driver_copies = [], [], []
    row_copies.append(send(base.at[pl.ds(5, 3)], rows_recv.at[pl.ds(0, 3)], (0, 1, 0)))
    row_copies.append(send(base.at[pl.ds(0, 3)], rows_recv.at[pl.ds(3, 3)], (0, -1, 0)))
    for dl, k in DRIVER_MOVES:
        slot = (-k) % N_LON
        if dl == 0:
            src, dst = dx, xall.at[slot, pl.ds(1, 2)]
        elif dl == 1:
            src, dst = dx.at[1], xall.at[slot, 0]
        else:
            src, dst = dx.at[0], xall.at[slot, 3]
        driver_copies.append(send(src, dst, (0, dl, k)))
    for dl, k in EDGE_MOVES:
        side = 0 if k == 1 else 1
        edge_copies.append(send(edge_send.at[1 - side], edge_recv.at[side, dl + 1], (0, dl, k)))
    xall[0, pl.ds(1, 2)] = dx[...]

    def turned(x, rows, cols):
        return jnp.transpose(padded_to(x, rows, cols))

    loaded(intake, stencil)
    intake_t = turned(intake[...].astype(F32), 128, WIDE)[:CP].astype(BF16)
    stencil_t = turned(stencil[...].astype(F32), 64, WIDE)[:CP].astype(BF16)
    place = iota((8, KS), 1)
    tap = jnp.zeros((8, KS), jnp.int32)
    for m in range(1, 7):
        tap = jnp.where(place >= SP * m, m, tap)
    is_state = place < 7 * SP
    tap = jnp.where(is_state, tap, (place - 7 * SP) // 8)
    source = jnp.where(is_state, place - SP * tap, STATE + (place - 7 * SP) - 8 * tap)
    source = jnp.where((is_state & (source >= STATE)) | (tap > 6), -1, source)
    tap, source = tap[:1], source[:1]
    chan = iota((128, KS), 0)
    intake_rep = dot(intake_t, jnp.where(chan == source, 1.0, 0.0).astype(BF16))
    chan = iota((64, KS), 0) - tap
    for u in range(7):
        taps = dot(stencil_t, jnp.where(chan == 7 * u, 1.0, 0.0).astype(BF16))
        product = taps * intake_rep
        w_all[:, KS * u : KS * (u + 1)] = product.astype(BF16)
        w_flux[:, KF * u : KF * (u + 1)] = product[:, 7 * SP : 7 * SP + KF].astype(BF16)

    xs[:, 7 * SP :] = jnp.zeros((24, KS - 7 * SP, 512), BF16)

    def own_columns(row, e):
        places = [(p, h) for p, h in ((e, 0), (e - 1, 1)) if 0 <= p < 13]
        for v in range(7):
            shifted = pltpu.roll(row, WIDE - 52 - v, 1)[:, :256]
            for p, h in places:
                xs[p, SP * v : SP * (v + 1), 256 * h : 256 * (h + 1)] = shifted

    for e in range(3, 11):
        own_columns(base[e - 3], e)

    def stack(first, count):
        return xs[first : first + count].reshape(count * KS, 512)

    acc[0, :, :512] = dot(w_all[:, 3 * KS :], stack(3, 4))
    acc[0, :, 512:] = dot(w_all[:, KS:], stack(3, 6))
    acc[1, :, :512] = dot(w_all[:, : 6 * KS], stack(4, 6))
    acc[1, :, 512:] = dot(w_all[:, : 4 * KS], stack(6, 4))

    loaded(widening, narrowing, readout, gain)
    w_wide[...] = turned(widening[...].astype(F32), WIDE, 1280)[:HID, :CP].astype(BF16)
    read = padded_to(readout[...].astype(F32), SP, CH).astype(BF16)
    w_out[:, :HID] = dot(read, narrowing[...]).astype(BF16)
    direct = dot(padded_to(read.astype(F32), SP, CP).astype(BF16), intake_t)
    own = iota((SP, 128), 1)
    w_out[:, HID : HID + SP] = jnp.where(own < STATE, direct, 0.0)[:, :SP].astype(BF16)
    direct = pltpu.roll(direct, 128 + 24 - STATE, 1)
    w_out[:, HID + SP :] = jnp.where((own >= 24) & (own < 32), direct, 0.0)[:, :KF].astype(BF16)
    gains[...] = jnp.transpose(jnp.broadcast_to(padded_to(gain[...].reshape(1, CH), 1, WIDE), (128, WIDE)))[:CP]
    loaded(air, inphase, quadrature, exchange, circle)
    air_wide = padded_to(air[...].astype(F32), DP, 384)
    mixed = jnp.concatenate(
        [
            padded_to(dot(air[...], inphase[...]), DP, 384),
            padded_to(dot(air[...], quadrature[...]), DP, 384),
        ],
        axis=0,
    )
    w_atm[...] = turned(mixed, 128, 384).astype(BF16)
    w_lift[...] = turned(air_wide, 128, 384).astype(BF16)
    w_exch[...] = padded_to(exchange[...].astype(F32), 16, 384).astype(BF16)

    for copy in driver_copies:
        copy.wait_recv()
    circles = jnp.concatenate([xall[s].reshape(4 * DP, 128) for s in range(N_LON)], axis=1)
    filtered = dot(circles, circle[...].astype(BF16))
    lanes_of = lambda t: jnp.concatenate(
        [filtered[i * DP : (i + 1) * DP, t * 128 : (t + 1) * 128] for i in range(4)], axis=1
    )
    smooth = jnp.concatenate([lanes_of(0), lanes_of(1), put_zeros(32, 512)], axis=0).astype(BF16)
    centre = jnp.concatenate([lanes_of(2), put_zeros(80, 512)], axis=0).astype(BF16)
    spectral = dot(w_atm[...], smooth)
    lifted = dot(w_lift[...], centre).astype(BF16).astype(F32)
    atm_hidden = (lifted + gelu(spectral)).astype(BF16)
    fluxes = dot(w_exch[...], atm_hidden)[:8]
    stacked = jnp.concatenate([fluxes[:, i * 128 : (i + 1) * 128] for i in range(4)], axis=0)
    box = 4 * iota((128, WIDE), 0) - 4
    column = iota((128, WIDE), 1) - HALO
    spread = jnp.where((column >= box) & (column < box + 4), 1.0, 0.0).astype(BF16)
    up_flux = dot(stacked.astype(BF16), spread)

    for copy in row_copies + edge_copies:
        copy.wait_recv()
    lane = iota((SP, 128), 1)
    flux_lane = iota((8, 128), 1)

    def wrapped(first, last, v, lanes):
        return pltpu.roll(jnp.where(lanes >= 52 + v, last, first), 76 - v, 1)

    for e in range(ROWS + 2 * HALO):
        if e < 3:
            row, r, dl = rows_recv[e].astype(F32), e + 5, 1
        elif e < 11:
            row, r, dl = base[e - 3].astype(F32), e - 3, 0
        else:
            row, r, dl = rows_recv[e - 8].astype(F32), e - 11, -1
        left = pltpu.roll(edge_recv[0, dl + 1].astype(F32), (-3 * r) % 128, 1)
        right = pltpu.roll(edge_recv[1, dl + 1].astype(F32), (107 - 3 * r) % 128, 1)
        first = jnp.where(lane < 3, left, row[:, :128])
        last = jnp.where(lane >= 107, right, row[:, 256:])
        last = jnp.where(lane >= 110, 0.0, last)
        row = jnp.concatenate([first, row[:, 128:256], last], axis=1)
        if e < 3:
            row = row * jnp.where(lat == 0, 0.0, 1.0)
        if e >= 11:
            row = row * jnp.where(lat == N_LAT - 1, 0.0, 1.0)
        if e < 3 or e >= 11:
            own_columns(row.astype(BF16), e)
        flux_row = (0, 0, 0, 1, 1, 1, 1, 2, 2, 2, 2, 3, 3, 3)[e]
        flux = up_flux[8 * flux_row : 8 * flux_row + 8] * row[STATE : STATE + 1]
        pairs = [(p, h) for p, h in ((e, 0), (e - 1, 1)) if 0 <= p < 13]
        quads = [(13 + e - h, h) for h in range(4) if 0 <= e - h < 11]
        inner, outer = [], []
        for v in range(7):
            shifted = wrapped(row[:, :128], row[:, 256:], v, lane).astype(BF16)
            for p, h in quads:
                xs[p, SP * v : SP * (v + 1), 128 * h : 128 * (h + 1)] = shifted
            inner.append(pltpu.roll(flux, WIDE - 52 - v, 1)[:, :256])
            outer.append(wrapped(flux[:, :128], flux[:, 256:], v, flux_lane))
        inner = jnp.concatenate(inner + [put_zeros(8, 256)], axis=0).astype(BF16)
        outer = jnp.concatenate(outer + [put_zeros(8, 128)], axis=0).astype(BF16)
        for p, h in pairs:
            xf[p, :, 256 * h : 256 * (h + 1)] = inner
        for p, h in quads:
            xf[p, :, 128 * h : 128 * (h + 1)] = outer
            xs[p, 7 * SP : 7 * SP + KF, 128 * h : 128 * (h + 1)] = outer

    def rest(u, rows, first):
        weights = jnp.concatenate([w_all[:, KS * u : KS * u + rows.shape[0]], w_flux[...]], axis=1)
        return dot(weights, jnp.concatenate([rows, xf[first : first + 7].reshape(7 * KF, 512)], axis=0))

    acc[0, :, :512] += rest(0, stack(0, 3), 0)
    acc[0, :, 512:] += rest(0, stack(2, 1), 2)
    acc[1, :, :512] += rest(6, stack(10, 1), 4)
    acc[1, :, 512:] += rest(4, stack(10, 3), 6)
    acc[2, :, :512] = dot(w_all[...], stack(13, 7))
    acc[2, :, 512:] = dot(w_all[...], stack(17, 7))

    def group(g, carry):
        conv = acc[g]
        mean = jnp.sum(conv, axis=0, keepdims=True) * (1.0 / CH)
        centered = jnp.where(iota((CP, 1024), 0) < CH, conv - mean, 0.0)
        variance = jnp.sum(centered * centered, axis=0, keepdims=True) * (1.0 / CH)
        scale = jnp.concatenate([gains[...]] * 8, axis=1)
        normed = (centered * lax.rsqrt(variance + 1e-6) * scale).astype(BF16)
        hidden[:HID] = gelu(dot(w_wide[...], normed)).astype(BF16)
        for h in range(2):
            p = jnp.where(g < 2, 4 * g + 2 * h, 13 + 4 * h) + 3
            hidden[HID : HID + SP, 512 * h : 512 * (h + 1)] = xs[p, 3 * SP : 4 * SP]
            hidden[HID + SP :, 512 * h : 512 * (h + 1)] = xf[p]
        fresh[g] = hidden[HID : HID + SP].astype(F32) + dot(w_out[...], hidden[...])
        return carry

    lax.fori_loop(0, 3, group, 0)

    def fresh_row(r, rows):
        inner = fresh[r // 4, :rows, 256 * (r % 4) : 256 * (r % 4 + 1)]
        outer = fresh[2, :rows, 128 * r : 128 * (r + 1)]
        return jnp.concatenate([inner, outer], axis=1)

    loaded(tiles)
    tile = iota((32, WIDE), 0) * 12
    column = iota((32, WIDE), 1)
    widen_tiles = jnp.where((column >= tile) & (column < tile + 12), 1.0, 0.0).astype(BF16)
    marks = padded_to(tiles[...].astype(F32), 1, 32)
    marked = dot(jnp.broadcast_to(marks, (8, 32)).astype(BF16), widen_tiles)
    mask = padded_to(sea, ROWS, WIDE) * marked
    x_new = jnp.concatenate([fresh_row(r, 8)[:1] for r in range(ROWS)], axis=0)
    x_new = pltpu.roll(x_new, 52, 1).astype(BF16).astype(F32)
    x = jnp.where(mask > 0.5, x_new, padded_to(state[0].astype(F32), ROWS, WIDE))
    x_own[...] = x
    x_all[sec] = x
    x_copies = [send(x_own, x_all.at[sec], (ds, 0, 0)) for ds in (2, 1, 3)]

    for r in range(ROWS):
        grid[:, r, :] = pltpu.roll(fresh_row(r, SP), 52, 1)
    mask_wide = jnp.broadcast_to(mask[None, :, :COLS], (STATE, ROWS, COLS))
    out_buf[...] = jnp.where(mask_wide > 0.5, grid[:STATE, :, :COLS], state[...].astype(F32)).astype(BF16)
    out_copy = pltpu.make_async_copy(out_buf, stepped, out_sem)
    out_copy.start()

    quad = iota((WIDE, 128), 1) * 4
    column = iota((WIDE, 128), 0)
    pool = jnp.where((column >= quad) & (column < quad + 4), 1.0, 0.0).astype(BF16)
    heat_boxes = dot((x * mask).astype(BF16), pool)
    count_boxes = dot(mask.astype(BF16), pool)
    for i in range(2):
        total = jnp.sum(heat_boxes[4 * i : 4 * i + 4], axis=0, keepdims=True)
        count = jnp.sum(count_boxes[4 * i : 4 * i + 4], axis=0, keepdims=True)
        pooled[i : i + 1, :] = (total / jnp.maximum(count, 1.0))[:, :90]
    loaded(area, heat)
    weight = jnp.concatenate([area[lat]] * 3, axis=1) * mask
    seen = padded_to(heat[...], ROWS, WIDE)

    def folded(y):
        return jnp.sum(y[:, :128] + y[:, 128:256] + y[:, 256:], axis=0, keepdims=True)

    area_sum = folded(weight)

    for copy in x_copies:
        copy.wait_recv()
    members = [x_all[m] for m in range(N_SEC)]
    deviation = sum(jnp.abs(m - seen) for m in members)
    gaps = sum(
        jnp.abs(members[m] - members[n]) for m in range(N_SEC) for n in range(m + 1, N_SEC)
    )
    epsilon = 0.05 / N_SEC
    fair = deviation * (1.0 / N_SEC) - (1.0 - epsilon) / (N_SEC * (N_SEC - 1)) * gaps
    score[...] = fair[:, :COLS]

    part[...] = jnp.concatenate([folded(weight * fair), area_sum, put_zeros(6, 128)], axis=0)
    twin = (0, 1 - 2 * core, 0)
    twin_copy = send(part, part_twin, twin)
    twin_copy.wait_recv()
    both = part[...] + part_twin[...]
    pair[...] = both

    def slot_of(y, z):
        return lax.rem(y, 2) * 8 + (y // 2) * 4 + z

    mine = slot_of(chip_y, lon)
    chips[core * 16 + (1 - core) * mine] = both
    chip_copies = []
    for dy, dz in ((2, 2), (2, 1), (2, 3), (0, 2), (2, 0), (0, 1), (0, 3)):
        chip_copies.append(send(pair, chips.at[mine], (0, 2 * (dy + core), dz)))
    chip_copies.append(send(pair, chips.at[core * mine + (1 - core) * 17], (0, 2, 0)))
    for copy in chip_copies:
        copy.wait_recv()
    here = pl.ds(lax.rem(chip_y + core, 2) * 8, 8)
    half_copy = send(chips.at[here], chips.at[here], twin)
    half_copy.wait_recv()
    total = chips[0]
    for m in range(1, 16):
        total = total + chips[m]
    sums = jnp.sum(total, axis=1, keepdims=True)
    skill[...] = sums[0:1] / sums[1:2]

    for copy in copies:
        copy.wait_send()
    out_copy.wait()


FAR_PARTNERS = list(
    zip(
        [(4, 0), (4, 1), (4, 2), (4, 3), (2, 0), (6, 0), (2, 1), (6, 3)],
        [(2, 0), (2, 1), (2, 2), (2, 3), (6, 0), (6, 1), (6, 2), (6, 3)],
    )
)
N_COPIES = len(DRIVER_MOVES) + len(ROW_MOVES) + len(EDGE_MOVES) + 3 + 1 + 8 + 1


def hand_over(*refs):
    count = len(refs) // 2
    for n in range(count):
        refs[count + n][...] = refs[n][...]


def on_device(*args):
    (drivers, state, flags, tiles, heat, air, inphase, quadrature, exchange, intake, stencil, gain,
     widening, narrowing, readout) = args
    anywhere = pl.BlockSpec(memory_space=pl.ANY)
    vmem = pl.BlockSpec(memory_space=pltpu.VMEM)
    operands = (
        state[0], flags, tiles, heat, drivers[0], jnp.asarray(circle_tables()), jnp.asarray(area_table()),
        air, inphase, quadrature, exchange.T, intake, stencil, gain,
        widening, narrowing.T, readout.T,
    )
    outputs = (
        jax.ShapeDtypeStruct((STATE, ROWS, COLS), BF16),
        jax.ShapeDtypeStruct((2, 90), F32),
        jax.ShapeDtypeStruct((ROWS, COLS), F32),
        jax.ShapeDtypeStruct((1, 1), F32),
    )
    results = pl.pallas_call(
        kernel,
        out_shape=outputs,
        in_specs=[anywhere] * len(operands),
        out_specs=(anywhere, vmem, vmem, vmem),
        scratch_shapes=[pltpu.VMEM(x.shape, x.dtype) for x in operands]
        + [
            pltpu.VMEM((SP, ROWS, WIDE), F32),
            pltpu.VMEM((ROWS, SP, WIDE), BF16),
            pltpu.VMEM((2, SP, 128), BF16),
            pltpu.VMEM((2, 3, SP, 128), BF16),
            pltpu.VMEM((6, SP, WIDE), BF16),
            pltpu.VMEM((2, DP, 128), BF16),
            pltpu.VMEM((N_LON, 4, DP, 128), BF16),
            pltpu.VMEM((CP, 7 * KS), BF16),
            pltpu.VMEM((CP, 7 * KF), BF16),
            pltpu.VMEM((HID, CP), BF16),
            pltpu.VMEM((SP, HK), BF16),
            pltpu.VMEM((CP, 128), F32),
            pltpu.VMEM((384, 128), BF16),
            pltpu.VMEM((384, 128), BF16),
            pltpu.VMEM((16, 384), BF16),
            pltpu.VMEM((24, KS, 512), BF16),
            pltpu.VMEM((24, KF, 512), BF16),
            pltpu.VMEM((3, CP, 1024), F32),
            pltpu.VMEM((HK, 1024), BF16),
            pltpu.VMEM((3, SP, 1024), F32),
            pltpu.VMEM((STATE, ROWS, COLS), BF16),
            pltpu.VMEM((ROWS, WIDE), F32),
            pltpu.VMEM((N_SEC, ROWS, WIDE), F32),
            pltpu.VMEM((8, 128), F32),
            pltpu.VMEM((8, 128), F32),
            pltpu.VMEM((8, 128), F32),
            pltpu.VMEM((18, 8, 128), F32),
            pltpu.SemaphoreType.DMA((len(operands),)),
            pltpu.SemaphoreType.DMA,
            pltpu.SemaphoreType.DMA((N_COPIES,)),
            pltpu.SemaphoreType.DMA((N_COPIES,)),
        ],
        compiler_params=pltpu.CompilerParams(
            collective_id=0, has_side_effects=True, vmem_limit_bytes=58 << 20
        ),
        name="coupled_step",
    )(*operands)
    stepped, pooled, score, skill = pl.pallas_call(
        hand_over,
        out_shape=outputs,
        in_specs=[vmem] * 4,
        out_specs=(vmem,) * 4,
        name="hand_over",
    )(*results)
    return (
        stepped.reshape(1, STATE, ROWS, COLS),
        pooled.reshape(1, 2, 90),
        score,
        skill.reshape(()),
    )


def solution(mesh):
    in_specs = (
        P("sec", None, "lat", "lon"),
        P("sec", None, "lat", "lon"),
        P("lat", "lon"),
        P("lat", "lon"),
        P("lat", "lon"),
    ) + (P(),) * 10
    out_specs = (P("sec", None, "lat", "lon"), P("sec", "lat", "lon"), P("lat", "lon"), P())
    return jax.shard_map(
        on_device, mesh=mesh, in_specs=in_specs, out_specs=out_specs, check_vma=False
    )
```

```python
import functools
import math

import jax
import jax.numpy as jnp
import numpy as np
from jax import lax
from jax.experimental import pallas as pl
from jax.experimental.pallas import tpu as pltpu
from jax.sharding import PartitionSpec as P

F32 = jnp.float32
BF16 = jnp.bfloat16
MESH = pl.DeviceIdType.MESH

WIND_LONGITUDES = 360
KM = 128
N_SEC, N_LAT, N_LON = 4, 8, 4
STATE = 77
SP = 80
CH = 300
CP = 304
HID = 1200
ROWS = 8
COLS = 360
WIDE = 384
DRV = 40
DP = 48
HALO = 3
KS = 640
KF = 64
HK = HID + SP + KF

LON_MOVES = [(0, 2), (0, 1), (0, 3)]
CORNER_MOVES = [(dl, k) for dl in (1, -1) for k in (1, 3)]
ROW_MOVES = [(1, 0), (-1, 0)]


def circle_tables():
    offset = np.arange(WIND_LONGITUDES)
    waves = np.arange(KM)
    weight = np.where(waves == 0, 1.0, 2.0) / WIND_LONGITUDES
    angle = 2.0 * math.pi / WIND_LONGITUDES * (offset[:, None] * waves[None, :] % WIND_LONGITUDES)
    low = (np.cos(angle) * weight).sum(1)
    quad = (np.sin(angle) * weight).sum(1)
    block = WIND_LONGITUDES // N_LON
    source = (block * np.arange(N_LON)[:, None] + np.arange(128)[None, :]).reshape(-1)
    real = np.tile(np.arange(128) < block, N_LON)
    target = np.arange(128) - 1
    gap = (source[:, None] - target[None, :]) % WIND_LONGITUDES
    keep = real[:, None] & (np.arange(128) < block + 2)[None, :]
    tables = [np.where(keep, t, 0.0) for t in (low[gap], quad[gap], (gap == 0) * 1.0)]
    return np.concatenate(tables, axis=1).astype(np.float32)


def area_table():
    latitude = 84.0 - 0.25 * (np.arange(N_LAT * ROWS) + 0.5)
    cosine = np.cos(latitude * (math.pi / 180.0)).astype(np.float32)
    return np.broadcast_to(cosine.reshape(N_LAT, ROWS, 1), (N_LAT, ROWS, 128)).copy()


def iota(shape, dim):
    return lax.broadcasted_iota(jnp.int32, shape, dim)


def dot(a, b):
    return jnp.dot(a, b, preferred_element_type=F32)


def put_zeros(rows, cols):
    return jnp.zeros((rows, cols), F32)


def padded_to(x, rows, cols):
    if x.shape[1] < cols:
        x = jnp.concatenate([x, put_zeros(x.shape[0], cols - x.shape[1])], axis=1)
    if x.shape[0] < rows:
        x = jnp.concatenate([x, put_zeros(rows - x.shape[0], cols)], axis=0)
    return x


def gelu(x):
    return 0.5 * x * (1.0 + lax.erf(x * (0.5**0.5)))


def kernel(
    state_h, flags_h, tiles_h, heat_h, drivers_h, circle_h, area_h,
    air_h, inphase_h, quadrature_h, exchange_h, intake_h, stencil_h, gain_h, widening_h, narrowing_h, readout_h,
    stepped, pooled, score, skill,
    state, flags, tiles, heat, drivers, circle, area,
    air, inphase, quadrature, exchange, intake, stencil, gain, widening, narrowing, readout,
    grid, base, pack, lon_recv, corner, rows_recv, flux_send, flux_recv,
    w_all, w_flux, w_wide, w_out, gains, w_atm, w_lift, w_exch,
    xs, xf, acc, hidden, fresh, out_buf, x_own, x_all, part, part_twin, pair, chips,
    load_sem, out_sem, send_sem, recv_sem,
):
    sec, lat, lon = lax.axis_index("sec"), lax.axis_index("lat"), lax.axis_index("lon")
    core = lax.rem(lat, 2)
    chip_y = lat // 2

    def at(ds, dl, dk):
        return (
            lax.rem(sec + (ds + N_SEC), N_SEC),
            lax.rem(lat + (dl + N_LAT), N_LAT),
            lax.rem(lon + (dk + N_LON), N_LON),
        )

    partners = []
    partners += [(0, 2 * dy, k) for dy in (2, 1, 3) for k in range(N_LON)]
    partners += [(0, dl, k) for dl, k in LON_MOVES + CORNER_MOVES + ROW_MOVES] + [(ds, 0, 0) for ds in range(1, N_SEC)]
    barrier = pltpu.get_barrier_semaphore()
    for step in partners:
        pl.semaphore_signal(barrier, inc=1, device_id=at(*step), device_id_type=MESH)

    loads = {}
    for n, (src, dst) in enumerate(
        [
            (flags_h, flags), (state_h, state), (drivers_h, drivers), (intake_h, intake), (stencil_h, stencil),
            (narrowing_h, narrowing), (widening_h, widening), (circle_h, circle), (air_h, air),
            (inphase_h, inphase), (quadrature_h, quadrature), (exchange_h, exchange), (gain_h, gain),
            (readout_h, readout), (tiles_h, tiles), (heat_h, heat), (area_h, area),
        ]
    ):
        copy = pltpu.make_async_copy(src, dst, load_sem.at[n])
        copy.start()
        loads[id(dst)] = copy

    def loaded(*refs):
        for ref in refs:
            loads.pop(id(ref)).wait()

    loaded(flags, state)
    sea = flags[...].astype(F32)
    grid[:, :, 256:WIDE] = jnp.zeros((SP, ROWS, WIDE - 256), F32)
    grid[:STATE, :, :COLS] = state[...].astype(F32) * sea[None]
    grid[STATE, :, :COLS] = sea
    grid[STATE + 1 :] = jnp.zeros((SP - STATE - 1, ROWS, WIDE), F32)
    lane = iota((SP, 128), 1)
    left_edge = jnp.zeros((SP, 128), F32)
    right_edge = jnp.zeros((SP, 128), F32)
    for r in range(ROWS):
        row = pltpu.roll(grid[:, r, :], HALO, 1)
        base[r] = row.astype(BF16)
        here = (lane >= 3 * r) & (lane < 3 * r + 3)
        left_edge = jnp.where(here, pltpu.roll(row[:, :128], (3 * r - 3) % 128, 1), left_edge)
        right_edge = jnp.where(here, pltpu.roll(row[:, 256:], (3 * r - 104) % 128, 1), right_edge)
    pack[0, 2 * DP :] = right_edge.astype(BF16)
    pack[1, 2 * DP :] = left_edge.astype(BF16)
    loaded(drivers)
    driven = drivers[...].astype(F32)
    for i in range(2):
        own = padded_to(driven[:, i, :], DP, 128).astype(BF16)
        pack[0, DP * i : DP * (i + 1)] = own
        pack[1, DP * i : DP * (i + 1)] = own
        lon_recv[0, DP * i : DP * (i + 1)] = own

    pl.semaphore_wait(barrier, len(partners))

    copies = []

    def send(src, dst, step):
        n = len(copies)
        copy = pltpu.make_async_remote_copy(
            src_ref=src, dst_ref=dst, send_sem=send_sem.at[n], recv_sem=recv_sem.at[n],
            device_id=at(*step), device_id_type=MESH,
        )
        copy.start()
        copies.append(copy)
        return copy

    row_copies = [
        send(base.at[pl.ds(5, 3)], rows_recv.at[pl.ds(0, 3)], (0, 1, 0)),
        send(base.at[pl.ds(0, 3)], rows_recv.at[pl.ds(3, 3)], (0, -1, 0)),
    ]
    lon_copies = [
        send(pack.at[0, pl.ds(0, 2 * DP)], lon_recv.at[2, pl.ds(0, 2 * DP)], (0, 0, 2)),
        send(pack.at[0], lon_recv.at[3], (0, 0, 1)),
        send(pack.at[1], lon_recv.at[1], (0, 0, 3)),
    ]
    for dl, k in CORNER_MOVES:
        side, end = (0 if k == 1 else 1), (0 if dl == 1 else 1)
        row_copies.append(send(pack.at[side, pl.ds(2 * DP, SP)], corner.at[side, end], (0, dl, k)))

    def turned(x, rows, cols):
        return jnp.transpose(padded_to(x, rows, cols))

    loaded(intake, stencil)
    intake_t = turned(intake[...].astype(F32), 128, WIDE)[:CP].astype(BF16)
    stencil_t = turned(stencil[...].astype(F32), 64, WIDE)[:CP].astype(BF16)
    place = iota((8, KS), 1)
    tap = jnp.zeros((8, KS), jnp.int32)
    for m in range(1, 7):
        tap = jnp.where(place >= SP * m, m, tap)
    is_state = place < 7 * SP
    tap = jnp.where(is_state, tap, (place - 7 * SP) // 8)
    source = jnp.where(is_state, place - SP * tap, STATE + (place - 7 * SP) - 8 * tap)
    source = jnp.where((is_state & (source >= STATE)) | (tap > 6), -1, source)
    tap, source = tap[:1], source[:1]
    chan = iota((128, KS), 0)
    intake_rep = dot(intake_t, jnp.where(chan == source, 1.0, 0.0).astype(BF16))
    chan = iota((64, KS), 0) - tap
    for u in range(7):
        taps = dot(stencil_t, jnp.where(chan == 7 * u, 1.0, 0.0).astype(BF16))
        product = taps * intake_rep
        w_all[:, KS * u : KS * (u + 1)] = product.astype(BF16)
        w_flux[:, KF * u : KF * (u + 1)] = product[:, 7 * SP : 7 * SP + KF].astype(BF16)

    xs[:, 7 * SP :] = jnp.zeros((24, KS - 7 * SP, 512), BF16)

    def own_columns(row, e):
        places = [(p, h) for p, h in ((e, 0), (e - 1, 1)) if 0 <= p < 13]
        for v in range(7):
            shifted = pltpu.roll(row, WIDE - 52 - v, 1)[:, :256]
            for p, h in places:
                xs[p, SP * v : SP * (v + 1), 256 * h : 256 * (h + 1)] = shifted

    for e in range(3, 11):
        own_columns(base[e - 3], e)

    def stack(first, count):
        return xs[first : first + count].reshape(count * KS, 512)

    acc[0, :, :512] = dot(w_all[:, 3 * KS :], stack(3, 4))
    acc[0, :, 512:] = dot(w_all[:, KS:], stack(3, 6))
    acc[1, :, :512] = dot(w_all[:, : 6 * KS], stack(4, 6))
    acc[1, :, 512:] = dot(w_all[:, : 4 * KS], stack(6, 4))

    loaded(widening, narrowing, readout, gain)
    w_wide[...] = turned(widening[...].astype(F32), WIDE, 1280)[:HID, :CP].astype(BF16)
    read = padded_to(readout[...].astype(F32), SP, CH).astype(BF16)
    w_out[:, :HID] = dot(read, narrowing[...]).astype(BF16)
    direct = dot(padded_to(read.astype(F32), SP, CP).astype(BF16), intake_t)
    own = iota((SP, 128), 1)
    w_out[:, HID : HID + SP] = jnp.where(own < STATE, direct, 0.0)[:, :SP].astype(BF16)
    direct = pltpu.roll(direct, 128 + 24 - STATE, 1)
    w_out[:, HID + SP :] = jnp.where((own >= 24) & (own < 32), direct, 0.0)[:, :KF].astype(BF16)
    gains[...] = jnp.transpose(jnp.broadcast_to(padded_to(gain[...].reshape(1, CH), 1, WIDE), (128, WIDE)))[:CP]
    loaded(air, inphase, quadrature, exchange, circle)
    air_wide = padded_to(air[...].astype(F32), DP, 384)
    mixed = jnp.concatenate(
        [
            padded_to(dot(air[...], inphase[...]), DP, 384),
            padded_to(dot(air[...], quadrature[...]), DP, 384),
        ],
        axis=0,
    )
    w_atm[...] = turned(mixed, 128, 384).astype(BF16)
    w_lift[...] = turned(air_wide, 128, 384).astype(BF16)
    w_exch[...] = padded_to(exchange[...].astype(F32), 16, 384).astype(BF16)

    for copy in lon_copies:
        copy.wait_recv()
    circles = jnp.concatenate([lon_recv[s, : 2 * DP] for s in range(N_LON)], axis=1)
    filtered = dot(circles, circle[...].astype(BF16))
    lanes_of = lambda t: jnp.concatenate(
        [filtered[i * DP : (i + 1) * DP, t * 128 : (t + 1) * 128] for i in range(2)], axis=1
    )
    smooth = jnp.concatenate([lanes_of(0), lanes_of(1), put_zeros(32, 256)], axis=0).astype(BF16)
    centre = jnp.concatenate([lanes_of(2), put_zeros(80, 256)], axis=0).astype(BF16)
    spectral = dot(w_atm[...], smooth)
    lifted = dot(w_lift[...], centre).astype(BF16).astype(F32)
    atm_hidden = (lifted + gelu(spectral)).astype(BF16)
    fluxes = dot(w_exch[...], atm_hidden)[:8]
    stacked = jnp.concatenate([fluxes[:, i * 128 : (i + 1) * 128] for i in range(2)], axis=0)
    box = 4 * iota((128, WIDE), 0) - 4
    column = iota((128, WIDE), 1) - HALO
    spread = jnp.where((column >= box) & (column < box + 4), 1.0, 0.0).astype(BF16)
    up_flux = dot(stacked.astype(BF16), spread)
    for i in range(2):
        flux_send[i] = up_flux[8 * i : 8 * i + 8]
    flux_copies = [
        send(flux_send.at[1], flux_recv.at[0], (0, 1, 0)),
        send(flux_send.at[0], flux_recv.at[1], (0, -1, 0)),
    ]

    for copy in row_copies:
        copy.wait_recv()
    lane = iota((SP, 128), 1)

    def ring(row, v):
        x = jnp.concatenate([row[:, 256:], row[:, :128]], axis=1)
        return pltpu.roll(x, 256 - 52 - v, 1)[:, :128]

    def put_flux(e, flux):
        inner = [pltpu.roll(flux, WIDE - 52 - v, 1)[:, :256] for v in range(7)]
        outer = [ring(flux, v) for v in range(7)]
        inner = jnp.concatenate(inner + [put_zeros(8, 256)], axis=0).astype(BF16)
        outer = jnp.concatenate(outer + [put_zeros(8, 128)], axis=0).astype(BF16)
        for p, h in ((e, 0), (e - 1, 1)):
            if 0 <= p < 13:
                xf[p, :, 256 * h : 256 * (h + 1)] = inner
        for h in range(4):
            if 0 <= e - h < 11:
                xf[13 + e - h, :, 128 * h : 128 * (h + 1)] = outer
                xs[13 + e - h, 7 * SP : 7 * SP + KF, 128 * h : 128 * (h + 1)] = outer

    seas = {}
    def place(e):
        if e < 3:
            row, r = rows_recv[e].astype(F32), e + 5
            left, right = corner[0, 0], corner[1, 0]
        elif e < 11:
            row, r = base[e - 3].astype(F32), e - 3
            left, right = lon_recv[3, 2 * DP :], lon_recv[1, 2 * DP :]
        else:
            row, r = rows_recv[e - 8].astype(F32), e - 11
            left, right = corner[0, 1], corner[1, 1]
        left = pltpu.roll(left.astype(F32), (-3 * r) % 128, 1)
        right = pltpu.roll(right.astype(F32), (107 - 3 * r) % 128, 1)
        first = jnp.where(lane < 3, left, row[:, :128])
        last = jnp.where(lane >= 107, right, row[:, 256:])
        last = jnp.where(lane >= 110, 0.0, last)
        row = jnp.concatenate([first, row[:, 128:256], last], axis=1)
        if e < 3:
            row = row * jnp.where(lat == 0, 0.0, 1.0)
        if e >= 11:
            row = row * jnp.where(lat == N_LAT - 1, 0.0, 1.0)
        seas[e] = row[STATE : STATE + 1]
        row = row.astype(BF16)
        if e < 3 or e >= 11:
            own_columns(row, e)
        for v in range(7):
            shifted = ring(row, v)
            for h in range(4):
                if 0 <= e - h < 11:
                    xs[13 + e - h, SP * v : SP * (v + 1), 128 * h : 128 * (h + 1)] = shifted
        if 3 <= e < 11:
            i = (e - 3) // 4
            put_flux(e, up_flux[8 * i : 8 * i + 8] * seas[e])

    for e in (0, 1, 2):
        place(e)
    acc[0, :, :512] += dot(w_all[:, : 3 * KS], stack(0, 3))
    acc[0, :, 512:] += dot(w_all[:, :KS], stack(2, 1))
    for e in (11, 12, 13):
        place(e)
    acc[1, :, :512] += dot(w_all[:, 6 * KS :], stack(10, 1))
    acc[1, :, 512:] += dot(w_all[:, 4 * KS :], stack(10, 3))
    for e in range(3, 11):
        place(e)
    for copy in flux_copies:
        copy.wait_recv()
    for e in (0, 1, 2, 11, 12, 13):
        put_flux(e, flux_recv[0 if e < 3 else 1] * seas[e])

    def flux_stack(first):
        return xf[first : first + 7].reshape(7 * KF, 512)

    acc[2, :, :512] = dot(w_all[...], stack(13, 7))
    acc[2, :, 512:] = dot(w_all[...], stack(17, 7))
    for g in range(2):
        sides = jnp.concatenate([flux_stack(4 * g), flux_stack(4 * g + 2)], axis=1)
        acc[g] += dot(w_flux[...], sides)

    def group(g, carry):
        conv = acc[g]
        mean = jnp.sum(conv, axis=0, keepdims=True) * (1.0 / CH)
        centered = jnp.where(iota((CP, 1024), 0) < CH, conv - mean, 0.0)
        variance = jnp.sum(centered * centered, axis=0, keepdims=True) * (1.0 / CH)
        scale = jnp.concatenate([gains[...]] * 8, axis=1)
        normed = (centered * lax.rsqrt(variance + 1e-6) * scale).astype(BF16)
        hidden[g, :HID] = gelu(dot(w_wide[...], normed)).astype(BF16)
        for h in range(2):
            p = (4 * g + 2 * h if g < 2 else 13 + 4 * h) + 3
            hidden[g, HID : HID + SP, 512 * h : 512 * (h + 1)] = xs[p, 3 * SP : 4 * SP]
            hidden[g, HID + SP :, 512 * h : 512 * (h + 1)] = xf[p]
        fresh[g] = hidden[g, HID : HID + SP].astype(F32) + dot(w_out[...], hidden[g])
        return carry

    for g in range(3):
        group(g, 0)

    def fresh_row(r, rows):
        inner = fresh[r // 4, :rows, 256 * (r % 4) : 256 * (r % 4 + 1)]
        outer = fresh[2, :rows, 128 * r : 128 * (r + 1)]
        return jnp.concatenate([inner, outer], axis=1)

    loaded(tiles)
    tile = iota((32, WIDE), 0) * 12
    column = iota((32, WIDE), 1)
    widen_tiles = jnp.where((column >= tile) & (column < tile + 12), 1.0, 0.0).astype(BF16)
    marks = padded_to(tiles[...].astype(F32), 1, 32)
    marked = dot(jnp.broadcast_to(marks, (8, 32)).astype(BF16), widen_tiles)
    mask = padded_to(sea, ROWS, WIDE) * marked
    x_new = jnp.concatenate([fresh_row(r, 8)[:1] for r in range(ROWS)], axis=0)
    x_new = pltpu.roll(x_new, 52, 1).astype(BF16).astype(F32)
    x = jnp.where(mask > 0.5, x_new, padded_to(state[0].astype(F32), ROWS, WIDE))
    x_own[...] = x
    x_all[sec] = x
    x_copies = [send(x_own, x_all.at[sec], (ds, 0, 0)) for ds in (2, 1, 3)]

    for r in range(ROWS):
        grid[:, r, :] = pltpu.roll(fresh_row(r, SP), 52, 1)
    mask_wide = jnp.broadcast_to(mask[None, :, :COLS], (STATE, ROWS, COLS))
    out_buf[...] = jnp.where(mask_wide > 0.5, grid[:STATE, :, :COLS], state[...].astype(F32)).astype(BF16)
    out_copy = pltpu.make_async_copy(out_buf, stepped, out_sem)
    out_copy.start()

    quad = iota((WIDE, 128), 1) * 4
    column = iota((WIDE, 128), 0)
    pool = jnp.where((column >= quad) & (column < quad + 4), 1.0, 0.0).astype(BF16)
    heat_boxes = dot((x * mask).astype(BF16), pool)
    count_boxes = dot(mask.astype(BF16), pool)
    for i in range(2):
        total = jnp.sum(heat_boxes[4 * i : 4 * i + 4], axis=0, keepdims=True)
        count = jnp.sum(count_boxes[4 * i : 4 * i + 4], axis=0, keepdims=True)
        pooled[i : i + 1, :] = (total / jnp.maximum(count, 1.0))[:, :90]
    loaded(area, heat)
    weight = jnp.concatenate([area[lat]] * 3, axis=1) * mask
    seen = padded_to(heat[...], ROWS, WIDE)

    def folded(y):
        return jnp.sum(y[:, :128] + y[:, 128:256] + y[:, 256:], axis=0, keepdims=True)

    area_sum = folded(weight)

    for copy in x_copies:
        copy.wait_recv()
    members = [x_all[m] for m in range(N_SEC)]
    deviation = sum(jnp.abs(m - seen) for m in members)
    gaps = sum(
        jnp.abs(members[m] - members[n]) for m in range(N_SEC) for n in range(m + 1, N_SEC)
    )
    epsilon = 0.05 / N_SEC
    fair = deviation * (1.0 / N_SEC) - (1.0 - epsilon) / (N_SEC * (N_SEC - 1)) * gaps
    score[...] = fair[:, :COLS]

    part[...] = jnp.concatenate([folded(weight * fair), area_sum, put_zeros(6, 128)], axis=0)
    twin = (0, 1 - 2 * core, 0)
    twin_copy = send(part, part_twin, twin)
    twin_copy.wait_recv()
    both = part[...] + part_twin[...]
    pair[...] = both

    mine = chip_y * N_LON + lon
    chips[mine] = both
    chip_copies = [send(pair, chips.at[mine], (0, 2 * dy, k)) for dy, k in CHIP_MOVES]
    for copy in chip_copies:
        copy.wait_recv()
    total = chips[0]
    for m in range(1, 16):
        total = total + chips[m]
    sums = jnp.sum(total, axis=1, keepdims=True)
    skill[...] = sums[0:1] / sums[1:2]

    for copy in copies:
        copy.wait_send()
    out_copy.wait()


CHIP_MOVES = [(2, 2), (2, 1), (2, 3), (1, 2), (3, 2), (2, 0), (0, 2), (1, 1), (1, 3), (3, 1), (3, 3)]
CHIP_MOVES += [(1, 0), (3, 0), (0, 1), (0, 3)]
N_COPIES = len(LON_MOVES) + len(ROW_MOVES) + len(CORNER_MOVES) + 2 + 3 + 1 + 15


def hand_over(*refs):
    count = len(refs) // 2
    for n in range(count):
        refs[count + n][...] = refs[n][...]


def on_device(*args):
    (drivers, state, flags, tiles, heat, air, inphase, quadrature, exchange, intake, stencil, gain,
     widening, narrowing, readout) = args
    anywhere = pl.BlockSpec(memory_space=pl.ANY)
    vmem = pl.BlockSpec(memory_space=pltpu.VMEM)
    operands = (
        state[0], flags, tiles, heat, drivers[0], jnp.asarray(circle_tables()), jnp.asarray(area_table()),
        air, inphase, quadrature, exchange.T, intake, stencil, gain,
        widening, narrowing.T, readout.T,
    )
    outputs = (
        jax.ShapeDtypeStruct((STATE, ROWS, COLS), BF16),
        jax.ShapeDtypeStruct((2, 90), F32),
        jax.ShapeDtypeStruct((ROWS, COLS), F32),
        jax.ShapeDtypeStruct((1, 1), F32),
    )
    results = pl.pallas_call(
        kernel,
        out_shape=outputs,
        in_specs=[anywhere] * len(operands),
        out_specs=(anywhere, vmem, vmem, vmem),
        scratch_shapes=[pltpu.VMEM(x.shape, x.dtype) for x in operands]
        + [
            pltpu.VMEM((SP, ROWS, WIDE), F32),
            pltpu.VMEM((ROWS, SP, WIDE), BF16),
            pltpu.VMEM((2, 2 * DP + SP, 128), BF16),
            pltpu.VMEM((N_LON, 2 * DP + SP, 128), BF16),
            pltpu.VMEM((2, 2, SP, 128), BF16),
            pltpu.VMEM((6, SP, WIDE), BF16),
            pltpu.VMEM((2, 8, WIDE), F32),
            pltpu.VMEM((2, 8, WIDE), F32),
            pltpu.VMEM((CP, 7 * KS), BF16),
            pltpu.VMEM((CP, 7 * KF), BF16),
            pltpu.VMEM((HID, CP), BF16),
            pltpu.VMEM((SP, HK), BF16),
            pltpu.VMEM((CP, 128), F32),
            pltpu.VMEM((384, 128), BF16),
            pltpu.VMEM((384, 128), BF16),
            pltpu.VMEM((16, 384), BF16),
            pltpu.VMEM((24, KS, 512), BF16),
            pltpu.VMEM((24, KF, 512), BF16),
            pltpu.VMEM((3, CP, 1024), F32),
            pltpu.VMEM((3, HK, 1024), BF16),
            pltpu.VMEM((3, SP, 1024), F32),
            pltpu.VMEM((STATE, ROWS, COLS), BF16),
            pltpu.VMEM((ROWS, WIDE), F32),
            pltpu.VMEM((N_SEC, ROWS, WIDE), F32),
            pltpu.VMEM((8, 128), F32),
            pltpu.VMEM((8, 128), F32),
            pltpu.VMEM((8, 128), F32),
            pltpu.VMEM((16, 8, 128), F32),
            pltpu.SemaphoreType.DMA((len(operands),)),
            pltpu.SemaphoreType.DMA,
            pltpu.SemaphoreType.DMA((N_COPIES,)),
            pltpu.SemaphoreType.DMA((N_COPIES,)),
        ],
        compiler_params=pltpu.CompilerParams(
            collective_id=0, has_side_effects=True, vmem_limit_bytes=58 << 20
        ),
        name="coupled_step",
    )(*operands)
    stepped, pooled, score, skill = pl.pallas_call(
        hand_over,
        out_shape=outputs,
        in_specs=[vmem] * 4,
        out_specs=(vmem,) * 4,
        name="hand_over",
    )(*results)
    return (
        stepped.reshape(1, STATE, ROWS, COLS),
        pooled.reshape(1, 2, 90),
        score,
        skill.reshape(()),
    )


def solution(mesh):
    in_specs = (
        P("sec", None, "lat", "lon"),
        P("sec", None, "lat", "lon"),
        P("lat", "lon"),
        P("lat", "lon"),
        P("lat", "lon"),
    ) + (P(),) * 10
    out_specs = (P("sec", None, "lat", "lon"), P("sec", "lat", "lon"), P("lat", "lon"), P())
    return jax.shard_map(
        on_device, mesh=mesh, in_specs=in_specs, out_specs=out_specs, check_vma=False
    )
```

```python
import functools
import math

import jax
import jax.numpy as jnp
import numpy as np
from jax import lax
from jax.experimental import pallas as pl
from jax.experimental.pallas import tpu as pltpu
from jax.sharding import PartitionSpec as P

F32 = jnp.float32
BF16 = jnp.bfloat16
MESH = pl.DeviceIdType.MESH

WIND_LONGITUDES = 360
KM = 128
N_SEC, N_LAT, N_LON = 4, 8, 4
STATE = 77
SP = 80
CH = 300
CP = 304
HID = 1200
ROWS = 8
COLS = 360
WIDE = 384
DRV = 40
DP = 48
HALO = 3
KS = 640
KF = 64
HK = HID + SP + KF

LON_MOVES = [(0, 2), (0, 1), (0, 3)]
CORNER_MOVES = [(dl, k) for dl in (1, -1) for k in (1, 3)]
ROW_MOVES = [(1, 0), (-1, 0)]


def circle_tables():
    offset = np.arange(WIND_LONGITUDES)
    waves = np.arange(KM)
    weight = np.where(waves == 0, 1.0, 2.0) / WIND_LONGITUDES
    angle = 2.0 * math.pi / WIND_LONGITUDES * (offset[:, None] * waves[None, :] % WIND_LONGITUDES)
    low = (np.cos(angle) * weight).sum(1)
    quad = (np.sin(angle) * weight).sum(1)
    block = WIND_LONGITUDES // N_LON
    source = (block * np.arange(N_LON)[:, None] + np.arange(128)[None, :]).reshape(-1)
    real = np.tile(np.arange(128) < block, N_LON)
    target = np.arange(128) - 1
    gap = (source[:, None] - target[None, :]) % WIND_LONGITUDES
    keep = real[:, None] & (np.arange(128) < block + 2)[None, :]
    tables = [np.where(keep, t, 0.0) for t in (low[gap], quad[gap], (gap == 0) * 1.0)]
    return np.concatenate(tables, axis=1).astype(np.float32)


def area_table():
    latitude = 84.0 - 0.25 * (np.arange(N_LAT * ROWS) + 0.5)
    cosine = np.cos(latitude * (math.pi / 180.0)).astype(np.float32)
    return np.broadcast_to(cosine.reshape(N_LAT, ROWS, 1), (N_LAT, ROWS, 128)).copy()


def iota(shape, dim):
    return lax.broadcasted_iota(jnp.int32, shape, dim)


def dot(a, b):
    return jnp.dot(a, b, preferred_element_type=F32)


def put_zeros(rows, cols):
    return jnp.zeros((rows, cols), F32)


def padded_to(x, rows, cols):
    if x.shape[1] < cols:
        x = jnp.concatenate([x, put_zeros(x.shape[0], cols - x.shape[1])], axis=1)
    if x.shape[0] < rows:
        x = jnp.concatenate([x, put_zeros(rows - x.shape[0], cols)], axis=0)
    return x


def gelu(x):
    return 0.5 * x * (1.0 + lax.erf(x * (0.5**0.5)))


def kernel(
    state_h, flags_h, tiles_h, heat_h, drivers_h, circle_h, area_h,
    air_h, inphase_h, quadrature_h, exchange_h, intake_h, stencil_h, gain_h, widening_h, narrowing_h, readout_h,
    stepped, pooled, score, skill,
    state, flags, tiles, heat, drivers, circle, area,
    air, inphase, quadrature, exchange, intake, stencil, gain, widening, narrowing, readout,
    grid, base, pack, lon_recv, corner, rows_recv, flux_send, flux_recv,
    w_all, w_flux, w_wide, w_out, gains, w_atm, w_lift, w_exch,
    xs, xf, acc, hidden, fresh, out_buf, x_own, x_all, terms, pair, chips,
    load_sem, out_sem, send_sem, recv_sem,
):
    sec, lat, lon = lax.axis_index("sec"), lax.axis_index("lat"), lax.axis_index("lon")
    core = lax.rem(lat, 2)
    chip_y = lat // 2

    def at(ds, dl, dk):
        return (
            lax.rem(sec + (ds + N_SEC), N_SEC),
            lax.rem(lat + (dl + N_LAT), N_LAT),
            lax.rem(lon + (dk + N_LON), N_LON),
        )

    partners = []
    partners += [(0, 2 * dy, k) for dy in (2, 1, 3) for k in range(N_LON)]
    twin = 1 - 2 * core
    partners += [(ds, twin, 0) for ds in range(1, N_SEC)]
    partners += [(0, dl, k) for dl, k in LON_MOVES + CORNER_MOVES + ROW_MOVES] + [(ds, 0, 0) for ds in range(1, N_SEC)]
    barrier = pltpu.get_barrier_semaphore()
    for step in partners:
        pl.semaphore_signal(barrier, inc=1, device_id=at(*step), device_id_type=MESH)

    loads = {}
    for n, (src, dst) in enumerate(
        [
            (flags_h, flags), (state_h, state), (drivers_h, drivers), (intake_h, intake), (stencil_h, stencil),
            (narrowing_h, narrowing), (widening_h, widening), (circle_h, circle), (air_h, air),
            (inphase_h, inphase), (quadrature_h, quadrature), (exchange_h, exchange), (gain_h, gain),
            (readout_h, readout), (tiles_h, tiles), (heat_h, heat), (area_h, area),
        ]
    ):
        copy = pltpu.make_async_copy(src, dst, load_sem.at[n])
        copy.start()
        loads[id(dst)] = copy

    def loaded(*refs):
        for ref in refs:
            loads.pop(id(ref)).wait()

    loaded(flags, state)
    sea = flags[...].astype(F32)
    grid[:, :, 256:WIDE] = jnp.zeros((SP, ROWS, WIDE - 256), F32)
    grid[:STATE, :, :COLS] = state[...].astype(F32) * sea[None]
    grid[STATE, :, :COLS] = sea
    grid[STATE + 1 :] = jnp.zeros((SP - STATE - 1, ROWS, WIDE), F32)
    lane = iota((SP, 128), 1)
    left_edge = jnp.zeros((SP, 128), F32)
    right_edge = jnp.zeros((SP, 128), F32)
    for r in range(ROWS):
        row = pltpu.roll(grid[:, r, :], HALO, 1)
        base[r] = row.astype(BF16)
        here = (lane >= 3 * r) & (lane < 3 * r + 3)
        left_edge = jnp.where(here, pltpu.roll(row[:, :128], (3 * r - 3) % 128, 1), left_edge)
        right_edge = jnp.where(here, pltpu.roll(row[:, 256:], (3 * r - 104) % 128, 1), right_edge)
    pack[0, 2 * DP :] = right_edge.astype(BF16)
    pack[1, 2 * DP :] = left_edge.astype(BF16)
    loaded(drivers)
    driven = drivers[...].astype(F32)
    for i in range(2):
        own = padded_to(driven[:, i, :], DP, 128).astype(BF16)
        pack[0, DP * i : DP * (i + 1)] = own
        pack[1, DP * i : DP * (i + 1)] = own
        lon_recv[0, DP * i : DP * (i + 1)] = own

    pl.semaphore_wait(barrier, len(partners))

    copies = []

    def send(src, dst, step):
        n = len(copies)
        copy = pltpu.make_async_remote_copy(
            src_ref=src, dst_ref=dst, send_sem=send_sem.at[n], recv_sem=recv_sem.at[n],
            device_id=at(*step), device_id_type=MESH,
        )
        copy.start()
        copies.append(copy)
        return copy

    row_copies = [
        send(base.at[pl.ds(5, 3)], rows_recv.at[pl.ds(0, 3)], (0, 1, 0)),
        send(base.at[pl.ds(0, 3)], rows_recv.at[pl.ds(3, 3)], (0, -1, 0)),
    ]
    lon_copies = [
        send(pack.at[0, pl.ds(0, 2 * DP)], lon_recv.at[2, pl.ds(0, 2 * DP)], (0, 0, 2)),
        send(pack.at[0], lon_recv.at[3], (0, 0, 1)),
        send(pack.at[1], lon_recv.at[1], (0, 0, 3)),
    ]
    for dl, k in CORNER_MOVES:
        side, end = (0 if k == 1 else 1), (0 if dl == 1 else 1)
        row_copies.append(send(pack.at[side, pl.ds(2 * DP, SP)], corner.at[side, end], (0, dl, k)))

    def turned(x, rows, cols):
        return jnp.transpose(padded_to(x, rows, cols))

    loaded(intake, stencil)
    intake_t = turned(intake[...].astype(F32), 128, WIDE)[:CP].astype(BF16)
    stencil_t = turned(stencil[...].astype(F32), 64, WIDE)[:CP].astype(BF16)
    place = iota((8, KS), 1)
    tap = jnp.zeros((8, KS), jnp.int32)
    for m in range(1, 7):
        tap = jnp.where(place >= SP * m, m, tap)
    is_state = place < 7 * SP
    tap = jnp.where(is_state, tap, (place - 7 * SP) // 8)
    source = jnp.where(is_state, place - SP * tap, STATE + (place - 7 * SP) - 8 * tap)
    source = jnp.where((is_state & (source >= STATE)) | (tap > 6), -1, source)
    tap, source = tap[:1], source[:1]
    chan = iota((128, KS), 0)
    intake_rep = dot(intake_t, jnp.where(chan == source, 1.0, 0.0).astype(BF16))
    chan = iota((64, KS), 0) - tap
    for u in range(7):
        taps = dot(stencil_t, jnp.where(chan == 7 * u, 1.0, 0.0).astype(BF16))
        product = taps * intake_rep
        w_all[:, KS * u : KS * (u + 1)] = product.astype(BF16)
        w_flux[:, KF * u : KF * (u + 1)] = product[:, 7 * SP : 7 * SP + KF].astype(BF16)

    xs[:, 7 * SP :] = jnp.zeros((24, KS - 7 * SP, 512), BF16)

    def own_columns(row, e):
        places = [(p, h) for p, h in ((e, 0), (e - 1, 1)) if 0 <= p < 13]
        for v in range(7):
            shifted = pltpu.roll(row, WIDE - 52 - v, 1)[:, :256]
            for p, h in places:
                xs[p, SP * v : SP * (v + 1), 256 * h : 256 * (h + 1)] = shifted

    for e in range(3, 11):
        own_columns(base[e - 3], e)

    def stack(first, count):
        return xs[first : first + count].reshape(count * KS, 512)

    acc[0, :, :512] = dot(w_all[:, 3 * KS :], stack(3, 4))
    acc[0, :, 512:] = dot(w_all[:, KS:], stack(3, 6))
    acc[1, :, :512] = dot(w_all[:, : 6 * KS], stack(4, 6))
    acc[1, :, 512:] = dot(w_all[:, : 4 * KS], stack(6, 4))

    loaded(tiles, area, heat)
    tile = iota((32, WIDE), 0) * 12
    column = iota((32, WIDE), 1)
    widen_tiles = jnp.where((column >= tile) & (column < tile + 12), 1.0, 0.0).astype(BF16)
    marks = padded_to(tiles[...].astype(F32), 1, 32)
    marked = dot(jnp.broadcast_to(marks, (8, 32)).astype(BF16), widen_tiles)
    mask = padded_to(sea, ROWS, WIDE) * marked
    terms[0, 0] = jnp.concatenate([area[lat]] * 3, axis=1) * mask
    terms[0, 1] = padded_to(heat[...], ROWS, WIDE)
    terms_copy = send(terms.at[0], terms.at[1], (0, twin, 0))

    loaded(widening, narrowing, readout, gain)
    w_wide[...] = turned(widening[...].astype(F32), WIDE, 1280)[:HID, :CP].astype(BF16)
    read = padded_to(readout[...].astype(F32), SP, CH).astype(BF16)
    w_out[:, :HID] = dot(read, narrowing[...]).astype(BF16)
    direct = dot(padded_to(read.astype(F32), SP, CP).astype(BF16), intake_t)
    own = iota((SP, 128), 1)
    w_out[:, HID : HID + SP] = jnp.where(own < STATE, direct, 0.0)[:, :SP].astype(BF16)
    direct = pltpu.roll(direct, 128 + 24 - STATE, 1)
    w_out[:, HID + SP :] = jnp.where((own >= 24) & (own < 32), direct, 0.0)[:, :KF].astype(BF16)
    gains[...] = jnp.transpose(jnp.broadcast_to(padded_to(gain[...].reshape(1, CH), 1, WIDE), (128, WIDE)))[:CP]
    loaded(air, inphase, quadrature, exchange, circle)
    air_wide = padded_to(air[...].astype(F32), DP, 384)
    mixed = jnp.concatenate(
        [
            padded_to(dot(air[...], inphase[...]), DP, 384),
            padded_to(dot(air[...], quadrature[...]), DP, 384),
        ],
        axis=0,
    )
    w_atm[...] = turned(mixed, 128, 384).astype(BF16)
    w_lift[...] = turned(air_wide, 128, 384).astype(BF16)
    w_exch[...] = padded_to(exchange[...].astype(F32), 16, 384).astype(BF16)

    for copy in lon_copies:
        copy.wait_recv()
    circles = jnp.concatenate([lon_recv[s, : 2 * DP] for s in range(N_LON)], axis=1)
    filtered = dot(circles, circle[...].astype(BF16))
    lanes_of = lambda t: jnp.concatenate(
        [filtered[i * DP : (i + 1) * DP, t * 128 : (t + 1) * 128] for i in range(2)], axis=1
    )
    smooth = jnp.concatenate([lanes_of(0), lanes_of(1), put_zeros(32, 256)], axis=0).astype(BF16)
    centre = jnp.concatenate([lanes_of(2), put_zeros(80, 256)], axis=0).astype(BF16)
    spectral = dot(w_atm[...], smooth)
    lifted = dot(w_lift[...], centre).astype(BF16).astype(F32)
    atm_hidden = (lifted + gelu(spectral)).astype(BF16)
    fluxes = dot(w_exch[...], atm_hidden)[:8]
    stacked = jnp.concatenate([fluxes[:, i * 128 : (i + 1) * 128] for i in range(2)], axis=0)
    box = 4 * iota((128, WIDE), 0) - 4
    column = iota((128, WIDE), 1) - HALO
    spread = jnp.where((column >= box) & (column < box + 4), 1.0, 0.0).astype(BF16)
    up_flux = dot(stacked.astype(BF16), spread)
    for i in range(2):
        flux_send[i] = up_flux[8 * i : 8 * i + 8]
    flux_copies = [
        send(flux_send.at[1], flux_recv.at[0], (0, 1, 0)),
        send(flux_send.at[0], flux_recv.at[1], (0, -1, 0)),
    ]

    for copy in row_copies:
        copy.wait_recv()
    lane = iota((SP, 128), 1)

    def ring(row, v):
        x = jnp.concatenate([row[:, 256:], row[:, :128]], axis=1)
        return pltpu.roll(x, 256 - 52 - v, 1)[:, :128]

    def put_flux(e, flux):
        inner = [pltpu.roll(flux, WIDE - 52 - v, 1)[:, :256] for v in range(7)]
        outer = [ring(flux, v) for v in range(7)]
        inner = jnp.concatenate(inner + [put_zeros(8, 256)], axis=0).astype(BF16)
        outer = jnp.concatenate(outer + [put_zeros(8, 128)], axis=0).astype(BF16)
        for p, h in ((e, 0), (e - 1, 1)):
            if 0 <= p < 13:
                xf[p, :, 256 * h : 256 * (h + 1)] = inner
        for h in range(4):
            if 0 <= e - h < 11:
                xf[13 + e - h, :, 128 * h : 128 * (h + 1)] = outer

    seas = {}
    def place(e):
        if e < 3:
            row, r = rows_recv[e].astype(F32), e + 5
            left, right = corner[0, 0], corner[1, 0]
        elif e < 11:
            row, r = base[e - 3].astype(F32), e - 3
            left, right = lon_recv[3, 2 * DP :], lon_recv[1, 2 * DP :]
        else:
            row, r = rows_recv[e - 8].astype(F32), e - 11
            left, right = corner[0, 1], corner[1, 1]
        left = pltpu.roll(left.astype(F32), (-3 * r) % 128, 1)
        right = pltpu.roll(right.astype(F32), (107 - 3 * r) % 128, 1)
        first = jnp.where(lane < 3, left, row[:, :128])
        last = jnp.where(lane >= 107, right, row[:, 256:])
        last = jnp.where(lane >= 110, 0.0, last)
        row = jnp.concatenate([first, row[:, 128:256], last], axis=1)
        if e < 3:
            row = row * jnp.where(lat == 0, 0.0, 1.0)
        if e >= 11:
            row = row * jnp.where(lat == N_LAT - 1, 0.0, 1.0)
        seas[e] = row[STATE : STATE + 1]
        row = row.astype(BF16)
        if e < 3 or e >= 11:
            own_columns(row, e)
        for v in range(7):
            shifted = ring(row, v)
            for h in range(4):
                if 0 <= e - h < 11:
                    xs[13 + e - h, SP * v : SP * (v + 1), 128 * h : 128 * (h + 1)] = shifted
        if 3 <= e < 11:
            i = (e - 3) // 4
            put_flux(e, up_flux[8 * i : 8 * i + 8] * seas[e])

    for e in (0, 1, 2):
        place(e)
    acc[0, :, :512] += dot(w_all[:, : 3 * KS], stack(0, 3))
    acc[0, :, 512:] += dot(w_all[:, :KS], stack(2, 1))
    for e in (11, 12, 13):
        place(e)
    acc[1, :, :512] += dot(w_all[:, 6 * KS :], stack(10, 1))
    acc[1, :, 512:] += dot(w_all[:, 4 * KS :], stack(10, 3))
    for e in range(3, 11):
        place(e)
    acc[2, :, :512] = dot(w_all[...], stack(13, 7))
    acc[2, :, 512:] = dot(w_all[...], stack(17, 7))
    for copy in flux_copies:
        copy.wait_recv()
    for e in (0, 1, 2, 11, 12, 13):
        put_flux(e, flux_recv[0 if e < 3 else 1] * seas[e])

    def flux_stack(first):
        return xf[first : first + 7].reshape(7 * KF, 512)

    for g, first in ((0, 0), (1, 4), (2, 13)):
        second = first + (2 if g < 2 else 4)
        sides = jnp.concatenate([flux_stack(first), flux_stack(second)], axis=1)
        acc[g] += dot(w_flux[...], sides)

    def group(g, carry):
        conv = acc[g]
        mean = jnp.sum(conv, axis=0, keepdims=True) * (1.0 / CH)
        centered = jnp.where(iota((CP, 1024), 0) < CH, conv - mean, 0.0)
        variance = jnp.sum(centered * centered, axis=0, keepdims=True) * (1.0 / CH)
        scale = jnp.concatenate([gains[...]] * 8, axis=1)
        normed = (centered * lax.rsqrt(variance + 1e-6) * scale).astype(BF16)
        hidden[g, :HID] = gelu(dot(w_wide[...], normed)).astype(BF16)
        for h in range(2):
            p = (4 * g + 2 * h if g < 2 else 13 + 4 * h) + 3
            hidden[g, HID : HID + SP, 512 * h : 512 * (h + 1)] = xs[p, 3 * SP : 4 * SP]
            hidden[g, HID + SP :, 512 * h : 512 * (h + 1)] = xf[p]
        fresh[g] = hidden[g, HID : HID + SP].astype(F32) + dot(w_out[...], hidden[g])
        return carry

    for g in range(3):
        group(g, 0)

    def fresh_row(r, rows):
        inner = fresh[r // 4, :rows, 256 * (r % 4) : 256 * (r % 4 + 1)]
        outer = fresh[2, :rows, 128 * r : 128 * (r + 1)]
        return jnp.concatenate([inner, outer], axis=1)

    x_new = jnp.concatenate([fresh_row(r, 8)[:1] for r in range(ROWS)], axis=0)
    x_new = pltpu.roll(x_new, 52, 1).astype(BF16).astype(F32)
    x = jnp.where(mask > 0.5, x_new, padded_to(state[0].astype(F32), ROWS, WIDE))
    x_own[...] = x
    x_all[0, sec] = x
    x_copies = [send(x_own, x_all.at[0, sec], (ds, 0, 0)) for ds in (2, 1, 3)]
    x_copies += [send(x_own, x_all.at[1, sec], (ds, twin, 0)) for ds in (2, 1, 3, 0)]

    for r in range(ROWS):
        grid[:, r, :] = pltpu.roll(fresh_row(r, SP), 52, 1)
    mask_wide = jnp.broadcast_to(mask[None, :, :COLS], (STATE, ROWS, COLS))
    out_buf[...] = jnp.where(mask_wide > 0.5, grid[:STATE, :, :COLS], state[...].astype(F32)).astype(BF16)
    out_copy = pltpu.make_async_copy(out_buf, stepped, out_sem)
    out_copy.start()

    quad = iota((WIDE, 128), 1) * 4
    column = iota((WIDE, 128), 0)
    pool = jnp.where((column >= quad) & (column < quad + 4), 1.0, 0.0).astype(BF16)
    heat_boxes = dot((x * mask).astype(BF16), pool)
    count_boxes = dot(mask.astype(BF16), pool)
    for i in range(2):
        total = jnp.sum(heat_boxes[4 * i : 4 * i + 4], axis=0, keepdims=True)
        count = jnp.sum(count_boxes[4 * i : 4 * i + 4], axis=0, keepdims=True)
        pooled[i : i + 1, :] = (total / jnp.maximum(count, 1.0))[:, :90]
    def folded(y):
        return jnp.sum(y[:, :128] + y[:, 128:256] + y[:, 256:], axis=0, keepdims=True)

    terms_copy.wait_recv()
    area_sum = folded(terms[0, 0]) + folded(terms[1, 0])

    def fair_score(which):
        members = [x_all[which, m] for m in range(N_SEC)]
        deviation = sum(jnp.abs(m - terms[which, 1]) for m in members)
        gaps = sum(
            jnp.abs(members[m] - members[n]) for m in range(N_SEC) for n in range(m + 1, N_SEC)
        )
        epsilon = 0.05 / N_SEC
        return deviation * (1.0 / N_SEC) - (1.0 - epsilon) / (N_SEC * (N_SEC - 1)) * gaps

    for copy in x_copies:
        copy.wait_recv()
    fair = fair_score(0)
    score[...] = fair[:, :COLS]

    heat_sum = folded(terms[0, 0] * fair) + folded(terms[1, 0] * fair_score(1))
    both = jnp.concatenate([heat_sum, area_sum, put_zeros(6, 128)], axis=0)
    pair[...] = both
    mine = chip_y * N_LON + lon
    chips[mine] = both
    chip_copies = [send(pair, chips.at[mine], (0, 2 * dy, k)) for dy, k in CHIP_MOVES]
    for copy in chip_copies:
        copy.wait_recv()
    total = chips[0]
    for m in range(1, 16):
        total = total + chips[m]
    sums = jnp.sum(total, axis=1, keepdims=True)
    skill[...] = sums[0:1] / sums[1:2]

    for copy in copies:
        copy.wait_send()
    out_copy.wait()


CHIP_MOVES = [(2, 2), (2, 1), (2, 3), (1, 2), (3, 2), (2, 0), (0, 2), (1, 1), (1, 3), (3, 1), (3, 3)]
CHIP_MOVES += [(1, 0), (3, 0), (0, 1), (0, 3)]
N_COPIES = len(LON_MOVES) + len(ROW_MOVES) + len(CORNER_MOVES) + 2 + 1 + 7 + 15


def hand_over(*refs):
    count = len(refs) // 2
    for n in range(count):
        refs[count + n][...] = refs[n][...]


def on_device(*args):
    (drivers, state, flags, tiles, heat, air, inphase, quadrature, exchange, intake, stencil, gain,
     widening, narrowing, readout) = args
    anywhere = pl.BlockSpec(memory_space=pl.ANY)
    vmem = pl.BlockSpec(memory_space=pltpu.VMEM)
    operands = (
        state[0], flags, tiles, heat, drivers[0], jnp.asarray(circle_tables()), jnp.asarray(area_table()),
        air, inphase, quadrature, exchange.T, intake, stencil, gain,
        widening, narrowing.T, readout.T,
    )
    outputs = (
        jax.ShapeDtypeStruct((STATE, ROWS, COLS), BF16),
        jax.ShapeDtypeStruct((2, 90), F32),
        jax.ShapeDtypeStruct((ROWS, COLS), F32),
        jax.ShapeDtypeStruct((1, 1), F32),
    )
    results = pl.pallas_call(
        kernel,
        out_shape=outputs,
        in_specs=[anywhere] * len(operands),
        out_specs=(anywhere, vmem, vmem, vmem),
        scratch_shapes=[pltpu.VMEM(x.shape, x.dtype) for x in operands]
        + [
            pltpu.VMEM((SP, ROWS, WIDE), F32),
            pltpu.VMEM((ROWS, SP, WIDE), BF16),
            pltpu.VMEM((2, 2 * DP + SP, 128), BF16),
            pltpu.VMEM((N_LON, 2 * DP + SP, 128), BF16),
            pltpu.VMEM((2, 2, SP, 128), BF16),
            pltpu.VMEM((6, SP, WIDE), BF16),
            pltpu.VMEM((2, 8, WIDE), F32),
            pltpu.VMEM((2, 8, WIDE), F32),
            pltpu.VMEM((CP, 7 * KS), BF16),
            pltpu.VMEM((CP, 7 * KF), BF16),
            pltpu.VMEM((HID, CP), BF16),
            pltpu.VMEM((SP, HK), BF16),
            pltpu.VMEM((CP, 128), F32),
            pltpu.VMEM((384, 128), BF16),
            pltpu.VMEM((384, 128), BF16),
            pltpu.VMEM((16, 384), BF16),
            pltpu.VMEM((24, KS, 512), BF16),
            pltpu.VMEM((24, KF, 512), BF16),
            pltpu.VMEM((3, CP, 1024), F32),
            pltpu.VMEM((3, HK, 1024), BF16),
            pltpu.VMEM((3, SP, 1024), F32),
            pltpu.VMEM((STATE, ROWS, COLS), BF16),
            pltpu.VMEM((ROWS, WIDE), F32),
            pltpu.VMEM((2, N_SEC, ROWS, WIDE), F32),
            pltpu.VMEM((2, 2, ROWS, WIDE), F32),
            pltpu.VMEM((8, 128), F32),
            pltpu.VMEM((16, 8, 128), F32),
            pltpu.SemaphoreType.DMA((len(operands),)),
            pltpu.SemaphoreType.DMA,
            pltpu.SemaphoreType.DMA((N_COPIES,)),
            pltpu.SemaphoreType.DMA((N_COPIES,)),
        ],
        compiler_params=pltpu.CompilerParams(
            collective_id=0, has_side_effects=True, vmem_limit_bytes=58 << 20
        ),
        name="coupled_step",
    )(*operands)
    stepped, pooled, score, skill = pl.pallas_call(
        hand_over,
        out_shape=outputs,
        in_specs=[vmem] * 4,
        out_specs=(vmem,) * 4,
        name="hand_over",
    )(*results)
    return (
        stepped.reshape(1, STATE, ROWS, COLS),
        pooled.reshape(1, 2, 90),
        score,
        skill.reshape(()),
    )


def solution(mesh):
    in_specs = (
        P("sec", None, "lat", "lon"),
        P("sec", None, "lat", "lon"),
        P("lat", "lon"),
        P("lat", "lon"),
        P("lat", "lon"),
    ) + (P(),) * 10
    out_specs = (P("sec", None, "lat", "lon"), P("sec", "lat", "lon"), P("lat", "lon"), P())
    return jax.shard_map(
        on_device, mesh=mesh, in_specs=in_specs, out_specs=out_specs, check_vma=False
    )
```

```python
import functools
import math

import jax
import jax.numpy as jnp
import numpy as np
from jax import lax
from jax.experimental import pallas as pl
from jax.experimental.pallas import tpu as pltpu
from jax.sharding import PartitionSpec as P

F32 = jnp.float32
BF16 = jnp.bfloat16
MESH = pl.DeviceIdType.MESH

WIND_LONGITUDES = 360
KM = 128
N_SEC, N_LAT, N_LON = 4, 8, 4
STATE = 77
SP = 80
CH = 300
CP = 304
HID = 1200
ROWS = 8
COLS = 360
WIDE = 384
DRV = 40
DP = 48
HALO = 3
KS = 640
KF = 64
HK = HID + SP + KF

LON_MOVES = [(0, 2), (0, 1), (0, 3)]
CORNER_MOVES = [(dl, k) for dl in (1, -1) for k in (1, 3)]
ROW_MOVES = [(1, 0), (-1, 0)]


def circle_tables():
    offset = np.arange(WIND_LONGITUDES)
    waves = np.arange(KM)
    weight = np.where(waves == 0, 1.0, 2.0) / WIND_LONGITUDES
    angle = 2.0 * math.pi / WIND_LONGITUDES * (offset[:, None] * waves[None, :] % WIND_LONGITUDES)
    low = (np.cos(angle) * weight).sum(1)
    quad = (np.sin(angle) * weight).sum(1)
    block = WIND_LONGITUDES // N_LON
    source = (block * np.arange(N_LON)[:, None] + np.arange(128)[None, :]).reshape(-1)
    real = np.tile(np.arange(128) < block, N_LON)
    target = np.arange(128) - 1
    gap = (source[:, None] - target[None, :]) % WIND_LONGITUDES
    keep = real[:, None] & (np.arange(128) < block + 2)[None, :]
    tables = [np.where(keep, t, 0.0) for t in (low[gap], quad[gap], (gap == 0) * 1.0)]
    return np.concatenate(tables, axis=1).astype(np.float32)


def area_table():
    latitude = 84.0 - 0.25 * (np.arange(N_LAT * ROWS) + 0.5)
    cosine = np.cos(latitude * (math.pi / 180.0)).astype(np.float32)
    return np.broadcast_to(cosine.reshape(N_LAT, ROWS, 1), (N_LAT, ROWS, 128)).copy()


def iota(shape, dim):
    return lax.broadcasted_iota(jnp.int32, shape, dim)


def dot(a, b):
    return jnp.dot(a, b, preferred_element_type=F32)


def put_zeros(rows, cols):
    return jnp.zeros((rows, cols), F32)


def padded_to(x, rows, cols):
    if x.shape[1] < cols:
        x = jnp.concatenate([x, put_zeros(x.shape[0], cols - x.shape[1])], axis=1)
    if x.shape[0] < rows:
        x = jnp.concatenate([x, put_zeros(rows - x.shape[0], cols)], axis=0)
    return x


def gelu(x):
    return 0.5 * x * (1.0 + lax.erf(x * (0.5**0.5)))


def kernel(
    state_h, flags_h, tiles_h, heat_h, drivers_h, circle_h, area_h,
    air_h, inphase_h, quadrature_h, exchange_h, intake_h, stencil_h, gain_h, widening_h, narrowing_h, readout_h,
    stepped, pooled, score, skill,
    state, flags, tiles, heat, drivers, circle, area,
    air, inphase, quadrature, exchange, intake, stencil, gain, widening, narrowing, readout,
    grid, base, pack, lon_recv, corner, rows_recv, flux_send, flux_recv,
    w_all, w_flux, w_wide, w_out, gains, w_atm, w_lift, w_exch,
    xs, xf, acc, hidden, fresh, out_buf, x_own, x_all, terms, pair, chips,
    load_sem, out_sem, send_sem, recv_sem,
):
    sec, lat, lon = lax.axis_index("sec"), lax.axis_index("lat"), lax.axis_index("lon")
    core = lax.rem(lat, 2)
    chip_y = lat // 2

    def at(ds, dl, dk):
        return (
            lax.rem(sec + (ds + N_SEC), N_SEC),
            lax.rem(lat + (dl + N_LAT), N_LAT),
            lax.rem(lon + (dk + N_LON), N_LON),
        )

    partners = []
    partners += [(0, 2 * dy, k) for dy in (2, 1, 3) for k in range(N_LON)]
    twin = 1 - 2 * core
    partners += [(ds, twin, 0) for ds in range(1, N_SEC)]
    partners += [(0, dl, k) for dl, k in LON_MOVES + CORNER_MOVES + ROW_MOVES] + [(ds, 0, 0) for ds in range(1, N_SEC)]
    barrier = pltpu.get_barrier_semaphore()
    for step in partners:
        pl.semaphore_signal(barrier, inc=1, device_id=at(*step), device_id_type=MESH)

    loads = {}
    for n, (src, dst) in enumerate(
        [
            (flags_h, flags), (state_h, state), (drivers_h, drivers), (intake_h, intake), (stencil_h, stencil),
            (narrowing_h, narrowing), (widening_h, widening), (circle_h, circle), (air_h, air),
            (inphase_h, inphase), (quadrature_h, quadrature), (exchange_h, exchange), (gain_h, gain),
            (readout_h, readout), (tiles_h, tiles), (heat_h, heat), (area_h, area),
        ]
    ):
        copy = pltpu.make_async_copy(src, dst, load_sem.at[n])
        copy.start()
        loads[id(dst)] = copy

    def loaded(*refs):
        for ref in refs:
            loads.pop(id(ref)).wait()

    loaded(flags, state)
    sea = flags[...].astype(F32)
    grid[:, :, 256:WIDE] = jnp.zeros((SP, ROWS, WIDE - 256), F32)
    grid[:STATE, :, :COLS] = state[...].astype(F32) * sea[None]
    grid[STATE, :, :COLS] = sea
    grid[STATE + 1 :] = jnp.zeros((SP - STATE - 1, ROWS, WIDE), F32)
    lane = iota((SP, 128), 1)
    left_edge = jnp.zeros((SP, 128), F32)
    right_edge = jnp.zeros((SP, 128), F32)
    for r in range(ROWS):
        row = pltpu.roll(grid[:, r, :], HALO, 1)
        base[r] = row.astype(BF16)
        here = (lane >= 3 * r) & (lane < 3 * r + 3)
        left_edge = jnp.where(here, pltpu.roll(row[:, :128], (3 * r - 3) % 128, 1), left_edge)
        right_edge = jnp.where(here, pltpu.roll(row[:, 256:], (3 * r - 104) % 128, 1), right_edge)
    pack[0, 2 * DP :] = right_edge.astype(BF16)
    pack[1, 2 * DP :] = left_edge.astype(BF16)
    loaded(drivers)
    driven = drivers[...].astype(F32)
    for i in range(2):
        own = padded_to(driven[:, i, :], DP, 128).astype(BF16)
        pack[0, DP * i : DP * (i + 1)] = own
        pack[1, DP * i : DP * (i + 1)] = own
        lon_recv[0, DP * i : DP * (i + 1)] = own

    pl.semaphore_wait(barrier, len(partners))

    copies = []

    def send(src, dst, step):
        n = len(copies)
        copy = pltpu.make_async_remote_copy(
            src_ref=src, dst_ref=dst, send_sem=send_sem.at[n], recv_sem=recv_sem.at[n],
            device_id=at(*step), device_id_type=MESH,
        )
        copy.start()
        copies.append(copy)
        return copy

    row_copies = [
        send(base.at[pl.ds(5, 3)], rows_recv.at[pl.ds(0, 3)], (0, 1, 0)),
        send(base.at[pl.ds(0, 3)], rows_recv.at[pl.ds(3, 3)], (0, -1, 0)),
    ]
    lon_copies = [
        send(pack.at[0, pl.ds(0, 2 * DP)], lon_recv.at[2, pl.ds(0, 2 * DP)], (0, 0, 2)),
        send(pack.at[0], lon_recv.at[3], (0, 0, 1)),
        send(pack.at[1], lon_recv.at[1], (0, 0, 3)),
    ]
    for dl, k in CORNER_MOVES:
        side, end = (0 if k == 1 else 1), (0 if dl == 1 else 1)
        row_copies.append(send(pack.at[side, pl.ds(2 * DP, SP)], corner.at[side, end], (0, dl, k)))

    def turned(x, rows, cols):
        return jnp.transpose(padded_to(x, rows, cols))

    loaded(intake, stencil)
    intake_t = turned(intake[...].astype(F32), 128, WIDE)[:CP].astype(BF16)
    stencil_t = turned(stencil[...].astype(F32), 64, WIDE)[:CP].astype(BF16)
    place = iota((8, KS), 1)
    tap = jnp.zeros((8, KS), jnp.int32)
    for m in range(1, 7):
        tap = jnp.where(place >= SP * m, m, tap)
    is_state = place < 7 * SP
    tap = jnp.where(is_state, tap, (place - 7 * SP) // 8)
    source = jnp.where(is_state, place - SP * tap, STATE + (place - 7 * SP) - 8 * tap)
    source = jnp.where((is_state & (source >= STATE)) | (tap > 6), -1, source)
    tap, source = tap[:1], source[:1]
    chan = iota((128, KS), 0)
    intake_rep = dot(intake_t, jnp.where(chan == source, 1.0, 0.0).astype(BF16))
    chan = iota((64, KS), 0) - tap
    def build(u):
        taps = dot(stencil_t, jnp.where(chan == 7 * u, 1.0, 0.0).astype(BF16))
        product = taps * intake_rep
        w_all[:, KS * u : KS * (u + 1)] = product.astype(BF16)
        w_flux[:, KF * u : KF * (u + 1)] = product[:, 7 * SP : 7 * SP + KF].astype(BF16)

    xs[:, 7 * SP :] = jnp.zeros((24, KS - 7 * SP, 512), BF16)

    def own_columns(row, e):
        places = [(p, h) for p, h in ((e, 0), (e - 1, 1)) if 0 <= p < 13]
        for v in range(7):
            shifted = pltpu.roll(row, WIDE - 52 - v, 1)[:, :256]
            for p, h in places:
                xs[p, SP * v : SP * (v + 1), 256 * h : 256 * (h + 1)] = shifted

    def stack(first, count):
        return xs[first : first + count].reshape(count * KS, 512)

    for u in range(4):
        build(u)
    for e in range(6, 11):
        own_columns(base[e - 3], e)
    acc[1, :, 512:] = dot(w_all[:, : 4 * KS], stack(6, 4))
    for u in (4, 5):
        build(u)
    for e in (4, 5):
        own_columns(base[e - 3], e)
    acc[1, :, :512] = dot(w_all[:, : 6 * KS], stack(4, 6))
    build(6)
    own_columns(base[0], 3)
    acc[0, :, :512] = dot(w_all[:, 3 * KS :], stack(3, 4))
    acc[0, :, 512:] = dot(w_all[:, KS:], stack(3, 6))

    loaded(tiles, area, heat)
    tile = iota((32, WIDE), 0) * 12
    column = iota((32, WIDE), 1)
    widen_tiles = jnp.where((column >= tile) & (column < tile + 12), 1.0, 0.0).astype(BF16)
    marks = padded_to(tiles[...].astype(F32), 1, 32)
    marked = dot(jnp.broadcast_to(marks, (8, 32)).astype(BF16), widen_tiles)
    mask = padded_to(sea, ROWS, WIDE) * marked
    terms[0, 0] = jnp.concatenate([area[lat]] * 3, axis=1) * mask
    terms[0, 1] = padded_to(heat[...], ROWS, WIDE)
    terms_copy = send(terms.at[0], terms.at[1], (0, twin, 0))

    loaded(widening, narrowing, readout, gain)
    w_wide[...] = turned(widening[...].astype(F32), WIDE, 1280)[:HID, :CP].astype(BF16)
    read = padded_to(readout[...].astype(F32), SP, CH).astype(BF16)
    w_out[:, :HID] = dot(read, narrowing[...]).astype(BF16)
    direct = dot(padded_to(read.astype(F32), SP, CP).astype(BF16), intake_t)
    own = iota((SP, 128), 1)
    w_out[:, HID : HID + SP] = jnp.where(own < STATE, direct, 0.0)[:, :SP].astype(BF16)
    direct = pltpu.roll(direct, 128 + 24 - STATE, 1)
    w_out[:, HID + SP :] = jnp.where((own >= 24) & (own < 32), direct, 0.0)[:, :KF].astype(BF16)
    gains[...] = jnp.transpose(jnp.broadcast_to(padded_to(gain[...].reshape(1, CH), 1, WIDE), (128, WIDE)))[:CP]
    loaded(air, inphase, quadrature, exchange, circle)
    air_wide = padded_to(air[...].astype(F32), DP, 384)
    mixed = jnp.concatenate(
        [
            padded_to(dot(air[...], inphase[...]), DP, 384),
            padded_to(dot(air[...], quadrature[...]), DP, 384),
        ],
        axis=0,
    )
    w_atm[...] = turned(mixed, 128, 384).astype(BF16)
    w_lift[...] = turned(air_wide, 128, 384).astype(BF16)
    w_exch[...] = padded_to(exchange[...].astype(F32), 16, 384).astype(BF16)

    for copy in lon_copies:
        copy.wait_recv()
    circles = jnp.concatenate([lon_recv[s, : 2 * DP] for s in range(N_LON)], axis=1)
    filtered = dot(circles, circle[...].astype(BF16))
    lanes_of = lambda t: jnp.concatenate(
        [filtered[i * DP : (i + 1) * DP, t * 128 : (t + 1) * 128] for i in range(2)], axis=1
    )
    smooth = jnp.concatenate([lanes_of(0), lanes_of(1), put_zeros(32, 256)], axis=0).astype(BF16)
    centre = jnp.concatenate([lanes_of(2), put_zeros(80, 256)], axis=0).astype(BF16)
    spectral = dot(w_atm[...], smooth)
    lifted = dot(w_lift[...], centre).astype(BF16).astype(F32)
    atm_hidden = (lifted + gelu(spectral)).astype(BF16)
    fluxes = dot(w_exch[...], atm_hidden)[:8]
    stacked = jnp.concatenate([fluxes[:, i * 128 : (i + 1) * 128] for i in range(2)], axis=0)
    box = 4 * iota((128, WIDE), 0) - 4
    column = iota((128, WIDE), 1) - HALO
    spread = jnp.where((column >= box) & (column < box + 4), 1.0, 0.0).astype(BF16)
    up_flux = dot(stacked.astype(BF16), spread)
    for i in range(2):
        flux_send[i] = up_flux[8 * i : 8 * i + 8]
    flux_copies = [
        send(flux_send.at[1], flux_recv.at[0], (0, 1, 0)),
        send(flux_send.at[0], flux_recv.at[1], (0, -1, 0)),
    ]

    for copy in row_copies:
        copy.wait_recv()
    lane = iota((SP, 128), 1)

    def ring(row, v):
        x = jnp.concatenate([row[:, 256:], row[:, :128]], axis=1)
        return pltpu.roll(x, 256 - 52 - v, 1)[:, :128]

    def put_flux(e, flux):
        inner = [pltpu.roll(flux, WIDE - 52 - v, 1)[:, :256] for v in range(7)]
        outer = [ring(flux, v) for v in range(7)]
        inner = jnp.concatenate(inner + [put_zeros(8, 256)], axis=0).astype(BF16)
        outer = jnp.concatenate(outer + [put_zeros(8, 128)], axis=0).astype(BF16)
        for p, h in ((e, 0), (e - 1, 1)):
            if 0 <= p < 13:
                xf[p, :, 256 * h : 256 * (h + 1)] = inner
        for h in range(4):
            if 0 <= e - h < 11:
                xf[13 + e - h, :, 128 * h : 128 * (h + 1)] = outer

    seas = {}
    def place(e):
        if e < 3:
            row, r = rows_recv[e].astype(F32), e + 5
            left, right = corner[0, 0], corner[1, 0]
        elif e < 11:
            row, r = base[e - 3].astype(F32), e - 3
            left, right = lon_recv[3, 2 * DP :], lon_recv[1, 2 * DP :]
        else:
            row, r = rows_recv[e - 8].astype(F32), e - 11
            left, right = corner[0, 1], corner[1, 1]
        left = pltpu.roll(left.astype(F32), (-3 * r) % 128, 1)
        right = pltpu.roll(right.astype(F32), (107 - 3 * r) % 128, 1)
        first = jnp.where(lane < 3, left, row[:, :128])
        last = jnp.where(lane >= 107, right, row[:, 256:])
        last = jnp.where(lane >= 110, 0.0, last)
        row = jnp.concatenate([first, row[:, 128:256], last], axis=1)
        if e < 3:
            row = row * jnp.where(lat == 0, 0.0, 1.0)
        if e >= 11:
            row = row * jnp.where(lat == N_LAT - 1, 0.0, 1.0)
        seas[e] = row[STATE : STATE + 1]
        row = row.astype(BF16)
        if e < 3 or e >= 11:
            own_columns(row, e)
        for v in range(7):
            shifted = ring(row, v)
            for h in range(4):
                if 0 <= e - h < 11:
                    xs[13 + e - h, SP * v : SP * (v + 1), 128 * h : 128 * (h + 1)] = shifted
        if 3 <= e < 11:
            i = (e - 3) // 4
            put_flux(e, up_flux[8 * i : 8 * i + 8] * seas[e])

    for e in (0, 1, 2):
        place(e)
    acc[0, :, :512] += dot(w_all[:, : 3 * KS], stack(0, 3))
    acc[0, :, 512:] += dot(w_all[:, :KS], stack(2, 1))
    for e in (11, 12, 13):
        place(e)
    acc[1, :, :512] += dot(w_all[:, 6 * KS :], stack(10, 1))
    acc[1, :, 512:] += dot(w_all[:, 4 * KS :], stack(10, 3))
    for e in range(3, 11):
        place(e)
    acc[2, :, :512] = dot(w_all[...], stack(13, 7))
    acc[2, :, 512:] = dot(w_all[...], stack(17, 7))
    for copy in flux_copies:
        copy.wait_recv()
    for e in (0, 1, 2, 11, 12, 13):
        put_flux(e, flux_recv[0 if e < 3 else 1] * seas[e])

    def flux_stack(first):
        return xf[first : first + 7].reshape(7 * KF, 512)

    for g, first in ((0, 0), (1, 4), (2, 13)):
        second = first + (2 if g < 2 else 4)
        sides = jnp.concatenate([flux_stack(first), flux_stack(second)], axis=1)
        acc[g] += dot(w_flux[...], sides)

    def group(g, carry):
        conv = acc[g]
        mean = jnp.sum(conv, axis=0, keepdims=True) * (1.0 / CH)
        centered = jnp.where(iota((CP, 1024), 0) < CH, conv - mean, 0.0)
        variance = jnp.sum(centered * centered, axis=0, keepdims=True) * (1.0 / CH)
        scale = jnp.concatenate([gains[...]] * 8, axis=1)
        normed = (centered * lax.rsqrt(variance + 1e-6) * scale).astype(BF16)
        wide = dot(w_wide[...], normed).astype(BF16)
        hidden[g, :HID] = (wide * jnp.bfloat16(0.5)) * (1 + lax.erf(wide * jnp.bfloat16(0.5**0.5)))
        for h in range(2):
            p = (4 * g + 2 * h if g < 2 else 13 + 4 * h) + 3
            hidden[g, HID : HID + SP, 512 * h : 512 * (h + 1)] = xs[p, 3 * SP : 4 * SP]
            hidden[g, HID + SP :, 512 * h : 512 * (h + 1)] = xf[p]
        fresh[g] = hidden[g, HID : HID + SP].astype(F32) + dot(w_out[...], hidden[g])
        return carry

    for g in (2, 0, 1):
        group(g, 0)

    def fresh_row(r, rows):
        inner = fresh[r // 4, :rows, 256 * (r % 4) : 256 * (r % 4 + 1)]
        outer = fresh[2, :rows, 128 * r : 128 * (r + 1)]
        return jnp.concatenate([inner, outer], axis=1)

    x_new = jnp.concatenate([fresh_row(r, 8)[:1] for r in range(ROWS)], axis=0)
    x_new = pltpu.roll(x_new, 52, 1).astype(BF16).astype(F32)
    x = jnp.where(mask > 0.5, x_new, padded_to(state[0].astype(F32), ROWS, WIDE))
    x_own[...] = x
    x_all[0, sec] = x
    x_copies = [send(x_own, x_all.at[0, sec], (ds, 0, 0)) for ds in (2, 1, 3)]
    x_copies += [send(x_own, x_all.at[1, sec], (ds, twin, 0)) for ds in (2, 1, 3, 0)]

    for r in range(ROWS):
        grid[:, r, :] = pltpu.roll(fresh_row(r, SP), 52, 1)
    mask_wide = jnp.broadcast_to(mask[None, :, :COLS], (STATE, ROWS, COLS))
    out_buf[...] = jnp.where(mask_wide > 0.5, grid[:STATE, :, :COLS], state[...].astype(F32)).astype(BF16)
    out_copy = pltpu.make_async_copy(out_buf, stepped, out_sem)
    out_copy.start()

    quad = iota((WIDE, 128), 1) * 4
    column = iota((WIDE, 128), 0)
    pool = jnp.where((column >= quad) & (column < quad + 4), 1.0, 0.0).astype(BF16)
    heat_boxes = dot((x * mask).astype(BF16), pool)
    count_boxes = dot(mask.astype(BF16), pool)
    for i in range(2):
        total = jnp.sum(heat_boxes[4 * i : 4 * i + 4], axis=0, keepdims=True)
        count = jnp.sum(count_boxes[4 * i : 4 * i + 4], axis=0, keepdims=True)
        pooled[i : i + 1, :] = (total / jnp.maximum(count, 1.0))[:, :90]
    def folded(y):
        return jnp.sum(y[:, :128] + y[:, 128:256] + y[:, 256:], axis=0, keepdims=True)

    terms_copy.wait_recv()
    area_sum = folded(terms[0, 0]) + folded(terms[1, 0])

    def fair_score(which):
        members = [x_all[which, m] for m in range(N_SEC)]
        deviation = sum(jnp.abs(m - terms[which, 1]) for m in members)
        gaps = sum(
            jnp.abs(members[m] - members[n]) for m in range(N_SEC) for n in range(m + 1, N_SEC)
        )
        epsilon = 0.05 / N_SEC
        return deviation * (1.0 / N_SEC) - (1.0 - epsilon) / (N_SEC * (N_SEC - 1)) * gaps

    for copy in x_copies:
        copy.wait_recv()
    fair = fair_score(0)

    heat_sum = folded(terms[0, 0] * fair) + folded(terms[1, 0] * fair_score(1))
    both = jnp.concatenate([heat_sum, area_sum, put_zeros(6, 128)], axis=0)
    pair[...] = both
    mine = chip_y * N_LON + lon
    chips[mine] = both
    chip_copies = [send(pair, chips.at[mine], (0, 2 * dy, k)) for dy, k in CHIP_MOVES]
    score[...] = fair[:, :COLS]
    for copy in chip_copies:
        copy.wait_recv()
    total = chips[0]
    for m in range(1, 16):
        total = total + chips[m]
    sums = jnp.sum(total, axis=1, keepdims=True)
    skill[...] = sums[0:1] / sums[1:2]

    for copy in copies:
        copy.wait_send()
    out_copy.wait()


CHIP_MOVES = [(2, 2), (2, 1), (2, 3), (1, 2), (3, 2), (2, 0), (0, 2), (1, 1), (1, 3), (3, 1), (3, 3)]
CHIP_MOVES += [(1, 0), (3, 0), (0, 1), (0, 3)]
N_COPIES = len(LON_MOVES) + len(ROW_MOVES) + len(CORNER_MOVES) + 2 + 1 + 7 + 15


def hand_over(*refs):
    count = len(refs) // 2
    for n in range(count):
        refs[count + n][...] = refs[n][...]


def on_device(*args):
    (drivers, state, flags, tiles, heat, air, inphase, quadrature, exchange, intake, stencil, gain,
     widening, narrowing, readout) = args
    anywhere = pl.BlockSpec(memory_space=pl.ANY)
    vmem = pl.BlockSpec(memory_space=pltpu.VMEM)
    operands = (
        state[0], flags, tiles, heat, drivers[0], jnp.asarray(circle_tables()), jnp.asarray(area_table()),
        air, inphase, quadrature, exchange.T, intake, stencil, gain,
        widening, narrowing.T, readout.T,
    )
    outputs = (
        jax.ShapeDtypeStruct((STATE, ROWS, COLS), BF16),
        jax.ShapeDtypeStruct((2, 90), F32),
        jax.ShapeDtypeStruct((ROWS, COLS), F32),
        jax.ShapeDtypeStruct((1, 1), F32),
    )
    results = pl.pallas_call(
        kernel,
        out_shape=outputs,
        in_specs=[anywhere] * len(operands),
        out_specs=(anywhere, vmem, vmem, vmem),
        scratch_shapes=[pltpu.VMEM(x.shape, x.dtype) for x in operands]
        + [
            pltpu.VMEM((SP, ROWS, WIDE), F32),
            pltpu.VMEM((ROWS, SP, WIDE), BF16),
            pltpu.VMEM((2, 2 * DP + SP, 128), BF16),
            pltpu.VMEM((N_LON, 2 * DP + SP, 128), BF16),
            pltpu.VMEM((2, 2, SP, 128), BF16),
            pltpu.VMEM((6, SP, WIDE), BF16),
            pltpu.VMEM((2, 8, WIDE), F32),
            pltpu.VMEM((2, 8, WIDE), F32),
            pltpu.VMEM((CP, 7 * KS), BF16),
            pltpu.VMEM((CP, 7 * KF), BF16),
            pltpu.VMEM((HID, CP), BF16),
            pltpu.VMEM((SP, HK), BF16),
            pltpu.VMEM((CP, 128), F32),
            pltpu.VMEM((384, 128), BF16),
            pltpu.VMEM((384, 128), BF16),
            pltpu.VMEM((16, 384), BF16),
            pltpu.VMEM((24, KS, 512), BF16),
            pltpu.VMEM((24, KF, 512), BF16),
            pltpu.VMEM((3, CP, 1024), F32),
            pltpu.VMEM((3, HK, 1024), BF16),
            pltpu.VMEM((3, SP, 1024), F32),
            pltpu.VMEM((STATE, ROWS, COLS), BF16),
            pltpu.VMEM((ROWS, WIDE), F32),
            pltpu.VMEM((2, N_SEC, ROWS, WIDE), F32),
            pltpu.VMEM((2, 2, ROWS, WIDE), F32),
            pltpu.VMEM((8, 128), F32),
            pltpu.VMEM((16, 8, 128), F32),
            pltpu.SemaphoreType.DMA((len(operands),)),
            pltpu.SemaphoreType.DMA,
            pltpu.SemaphoreType.DMA((N_COPIES,)),
            pltpu.SemaphoreType.DMA((N_COPIES,)),
        ],
        compiler_params=pltpu.CompilerParams(
            collective_id=0, has_side_effects=True, vmem_limit_bytes=58 << 20
        ),
        name="coupled_step",
    )(*operands)
    stepped, pooled, score, skill = pl.pallas_call(
        hand_over,
        out_shape=outputs,
        in_specs=[vmem] * 4,
        out_specs=(vmem,) * 4,
        name="hand_over",
    )(*results)
    return (
        stepped.reshape(1, STATE, ROWS, COLS),
        pooled.reshape(1, 2, 90),
        score,
        skill.reshape(()),
    )


def solution(mesh):
    in_specs = (
        P("sec", None, "lat", "lon"),
        P("sec", None, "lat", "lon"),
        P("lat", "lon"),
        P("lat", "lon"),
        P("lat", "lon"),
    ) + (P(),) * 10
    out_specs = (P("sec", None, "lat", "lon"), P("sec", "lat", "lon"), P("lat", "lon"), P())
    return jax.shard_map(
        on_device, mesh=mesh, in_specs=in_specs, out_specs=out_specs, check_vma=False
    )
```

```python
import functools
import math

import jax
import jax.numpy as jnp
import numpy as np
from jax import lax
from jax.experimental import pallas as pl
from jax.experimental.pallas import tpu as pltpu
from jax.sharding import PartitionSpec as P

F32 = jnp.float32
BF16 = jnp.bfloat16
MESH = pl.DeviceIdType.MESH

WIND_LONGITUDES = 360
KM = 128
N_SEC, N_LAT, N_LON = 4, 8, 4
STATE = 77
SP = 80
CH = 300
CP = 304
HID = 1200
ROWS = 8
COLS = 360
WIDE = 384
DRV = 40
DP = 48
HALO = 3
KS = 640
KF = 64
HK = HID + SP + KF

LON_MOVES = [(0, 2), (0, 1), (0, 3)]
CORNER_MOVES = [(dl, k) for dl in (1, -1) for k in (1, 3)]
ROW_MOVES = [(1, 0), (-1, 0)]


def circle_tables():
    offset = np.arange(WIND_LONGITUDES)
    waves = np.arange(KM)
    weight = np.where(waves == 0, 1.0, 2.0) / WIND_LONGITUDES
    angle = 2.0 * math.pi / WIND_LONGITUDES * (offset[:, None] * waves[None, :] % WIND_LONGITUDES)
    low = (np.cos(angle) * weight).sum(1)
    quad = (np.sin(angle) * weight).sum(1)
    block = WIND_LONGITUDES // N_LON
    source = (block * np.arange(N_LON)[:, None] + np.arange(128)[None, :]).reshape(-1)
    real = np.tile(np.arange(128) < block, N_LON)
    target = np.arange(128) - 1
    gap = (source[:, None] - target[None, :]) % WIND_LONGITUDES
    keep = real[:, None] & (np.arange(128) < block + 2)[None, :]
    tables = [np.where(keep, t, 0.0) for t in (low[gap], quad[gap], (gap == 0) * 1.0)]
    return np.concatenate(tables, axis=1).astype(np.float32)


def area_table():
    latitude = 84.0 - 0.25 * (np.arange(N_LAT * ROWS) + 0.5)
    cosine = np.cos(latitude * (math.pi / 180.0)).astype(np.float32)
    return np.broadcast_to(cosine.reshape(N_LAT, ROWS, 1), (N_LAT, ROWS, 128)).copy()


def iota(shape, dim):
    return lax.broadcasted_iota(jnp.int32, shape, dim)


def dot(a, b):
    return jnp.dot(a, b, preferred_element_type=F32)


def put_zeros(rows, cols):
    return jnp.zeros((rows, cols), F32)


def padded_to(x, rows, cols):
    if x.shape[1] < cols:
        x = jnp.concatenate([x, put_zeros(x.shape[0], cols - x.shape[1])], axis=1)
    if x.shape[0] < rows:
        x = jnp.concatenate([x, put_zeros(rows - x.shape[0], cols)], axis=0)
    return x


def gelu(x):
    return 0.5 * x * (1.0 + lax.erf(x * (0.5**0.5)))


def kernel(
    state_h, flags_h, tiles_h, heat_h, drivers_h, circle_h, area_h,
    air_h, inphase_h, quadrature_h, exchange_h, intake_h, stencil_h, gain_h, widening_h, narrowing_h, readout_h,
    stepped, pooled, score, skill,
    state, flags, tiles, heat, drivers, circle, area,
    air, inphase, quadrature, exchange, intake, stencil, gain, widening, narrowing, readout,
    grid, base, pack, lon_recv, corner, rows_recv, flux_send, flux_recv,
    w_all, w_flux, w_wide, w_out, gains, w_atm, w_lift, w_exch,
    xs, xf, acc, hidden, fresh, out_buf, x_own, x_all, terms, pair, chips,
    load_sem, out_sem, send_sem, recv_sem,
):
    sec, lat, lon = lax.axis_index("sec"), lax.axis_index("lat"), lax.axis_index("lon")
    core = lax.rem(lat, 2)
    chip_y = lat // 2

    def at(ds, dl, dk):
        return (
            lax.rem(sec + (ds + N_SEC), N_SEC),
            lax.rem(lat + (dl + N_LAT), N_LAT),
            lax.rem(lon + (dk + N_LON), N_LON),
        )

    partners = []
    partners += [(0, 2 * dy, k) for dy in (2, 1, 3) for k in range(N_LON)]
    twin = 1 - 2 * core
    partners += [(ds, twin, 0) for ds in range(1, N_SEC)]
    partners += [(0, dl, k) for dl, k in LON_MOVES + CORNER_MOVES + ROW_MOVES] + [(ds, 0, 0) for ds in range(1, N_SEC)]
    barrier = pltpu.get_barrier_semaphore()
    for step in partners:
        pl.semaphore_signal(barrier, inc=1, device_id=at(*step), device_id_type=MESH)

    loads = {}
    for n, (src, dst) in enumerate(
        [
            (flags_h, flags), (state_h, state), (drivers_h, drivers), (intake_h, intake), (stencil_h, stencil),
            (narrowing_h, narrowing), (widening_h, widening), (circle_h, circle), (air_h, air),
            (inphase_h, inphase), (quadrature_h, quadrature), (exchange_h, exchange), (gain_h, gain),
            (readout_h, readout), (tiles_h, tiles), (heat_h, heat), (area_h, area),
        ]
    ):
        copy = pltpu.make_async_copy(src, dst, load_sem.at[n])
        copy.start()
        loads[id(dst)] = copy

    def loaded(*refs):
        for ref in refs:
            loads.pop(id(ref)).wait()

    loaded(flags, state)
    sea = flags[...].astype(F32)
    grid[:, :, 256:WIDE] = jnp.zeros((SP, ROWS, WIDE - 256), F32)
    grid[:STATE, :, :COLS] = state[...].astype(F32) * sea[None]
    grid[STATE, :, :COLS] = sea
    grid[STATE + 1 :] = jnp.zeros((SP - STATE - 1, ROWS, WIDE), F32)
    lane = iota((SP, 128), 1)
    left_edge = jnp.zeros((SP, 128), F32)
    right_edge = jnp.zeros((SP, 128), F32)
    for r in range(ROWS):
        row = pltpu.roll(grid[:, r, :], HALO, 1)
        base[r] = row.astype(BF16)
        here = (lane >= 3 * r) & (lane < 3 * r + 3)
        left_edge = jnp.where(here, pltpu.roll(row[:, :128], (3 * r - 3) % 128, 1), left_edge)
        right_edge = jnp.where(here, pltpu.roll(row[:, 256:], (3 * r - 104) % 128, 1), right_edge)
    pack[0, 2 * DP :] = right_edge.astype(BF16)
    pack[1, 2 * DP :] = left_edge.astype(BF16)
    loaded(drivers)
    driven = drivers[...].astype(F32)
    for i in range(2):
        own = padded_to(driven[:, i, :], DP, 128).astype(BF16)
        pack[0, DP * i : DP * (i + 1)] = own
        pack[1, DP * i : DP * (i + 1)] = own
        lon_recv[0, DP * i : DP * (i + 1)] = own

    pl.semaphore_wait(barrier, len(partners))

    copies = []

    def send(src, dst, step):
        n = len(copies)
        copy = pltpu.make_async_remote_copy(
            src_ref=src, dst_ref=dst, send_sem=send_sem.at[n], recv_sem=recv_sem.at[n],
            device_id=at(*step), device_id_type=MESH,
        )
        copy.start()
        copies.append(copy)
        return copy

    row_copies = [
        send(base.at[pl.ds(5, 3)], rows_recv.at[pl.ds(0, 3)], (0, 1, 0)),
        send(base.at[pl.ds(0, 3)], rows_recv.at[pl.ds(3, 3)], (0, -1, 0)),
    ]
    lon_copies = [
        send(pack.at[0, pl.ds(0, 2 * DP)], lon_recv.at[2, pl.ds(0, 2 * DP)], (0, 0, 2)),
        send(pack.at[0], lon_recv.at[3], (0, 0, 1)),
        send(pack.at[1], lon_recv.at[1], (0, 0, 3)),
    ]
    for dl, k in CORNER_MOVES:
        side, end = (0 if k == 1 else 1), (0 if dl == 1 else 1)
        row_copies.append(send(pack.at[side, pl.ds(2 * DP, SP)], corner.at[side, end], (0, dl, k)))

    def turned(x, rows, cols):
        return jnp.transpose(padded_to(x, rows, cols))

    loaded(intake, stencil)
    intake_t = turned(intake[...].astype(F32), 128, WIDE)[:CP].astype(BF16)
    stencil_t = turned(stencil[...].astype(F32), 64, WIDE)[:CP].astype(BF16)
    place = iota((8, KS), 1)
    tap = jnp.zeros((8, KS), jnp.int32)
    for m in range(1, 7):
        tap = jnp.where(place >= SP * m, m, tap)
    is_state = place < 7 * SP
    tap = jnp.where(is_state, tap, (place - 7 * SP) // 8)
    source = jnp.where(is_state, place - SP * tap, STATE + (place - 7 * SP) - 8 * tap)
    source = jnp.where((is_state & (source >= STATE)) | (tap > 6), -1, source)
    tap, source = tap[:1], source[:1]
    chan = iota((128, KS), 0)
    intake_rep = dot(intake_t, jnp.where(chan == source, 1.0, 0.0).astype(BF16))
    chan = iota((64, KS), 0) - tap
    def build(u):
        taps = dot(stencil_t, jnp.where(chan == 7 * u, 1.0, 0.0).astype(BF16))
        product = taps * intake_rep
        w_all[:, KS * u : KS * (u + 1)] = product.astype(BF16)
        w_flux[:, KF * u : KF * (u + 1)] = product[:, 7 * SP : 7 * SP + KF].astype(BF16)

    xs[:, 7 * SP :] = jnp.zeros((24, KS - 7 * SP, 512), BF16)

    def own_columns(row, e):
        places = [(p, h) for p, h in ((e, 0), (e - 1, 1)) if 0 <= p < 13]
        for v in range(7):
            shifted = pltpu.roll(row, WIDE - 52 - v, 1)[:, :256]
            for p, h in places:
                xs[p, SP * v : SP * (v + 1), 256 * h : 256 * (h + 1)] = shifted

    def stack(first, count):
        return xs[first : first + count].reshape(count * KS, 512)

    for u in range(4):
        build(u)
    for e in range(6, 11):
        own_columns(base[e - 3], e)
    acc[1, :, 512:] = dot(w_all[:, : 4 * KS], stack(6, 4))
    for u in (4, 5):
        build(u)
    for e in (4, 5):
        own_columns(base[e - 3], e)
    acc[1, :, :512] = dot(w_all[:, : 6 * KS], stack(4, 6))
    build(6)
    own_columns(base[0], 3)
    acc[0, :, :512] = dot(w_all[:, 3 * KS :], stack(3, 4))
    acc[0, :, 512:] = dot(w_all[:, KS:], stack(3, 6))

    loaded(tiles, area, heat)
    tile = iota((32, WIDE), 0) * 12
    column = iota((32, WIDE), 1)
    widen_tiles = jnp.where((column >= tile) & (column < tile + 12), 1.0, 0.0).astype(BF16)
    marks = padded_to(tiles[...].astype(F32), 1, 32)
    marked = dot(jnp.broadcast_to(marks, (8, 32)).astype(BF16), widen_tiles)
    mask = padded_to(sea, ROWS, WIDE) * marked
    terms[0, 0] = jnp.concatenate([area[lat]] * 3, axis=1) * mask
    terms[0, 1] = padded_to(heat[...], ROWS, WIDE)
    terms_copy = send(terms.at[0], terms.at[1], (0, twin, 0))

    loaded(widening, narrowing, readout, gain)
    w_wide[...] = turned(widening[...].astype(F32), WIDE, 1280)[:HID, :CP].astype(BF16)
    read = padded_to(readout[...].astype(F32), SP, CH).astype(BF16)
    w_out[:, :HID] = dot(read, narrowing[...]).astype(BF16)
    direct = dot(padded_to(read.astype(F32), SP, CP).astype(BF16), intake_t)
    own = iota((SP, 128), 1)
    w_out[:, HID : HID + SP] = jnp.where(own < STATE, direct, 0.0)[:, :SP].astype(BF16)
    direct = pltpu.roll(direct, 128 + 24 - STATE, 1)
    w_out[:, HID + SP :] = jnp.where((own >= 24) & (own < 32), direct, 0.0)[:, :KF].astype(BF16)
    gains[...] = jnp.transpose(jnp.broadcast_to(padded_to(gain[...].reshape(1, CH), 1, WIDE), (128, WIDE)))[:CP]
    loaded(air, inphase, quadrature, exchange, circle)
    air_wide = padded_to(air[...].astype(F32), DP, 384)
    mixed = jnp.concatenate(
        [
            padded_to(dot(air[...], inphase[...]), DP, 384),
            padded_to(dot(air[...], quadrature[...]), DP, 384),
        ],
        axis=0,
    )
    w_atm[...] = turned(mixed, 128, 384).astype(BF16)
    w_lift[...] = turned(air_wide, 128, 384).astype(BF16)
    w_exch[...] = padded_to(exchange[...].astype(F32), 16, 384).astype(BF16)

    for copy in lon_copies:
        copy.wait_recv()
    circles = jnp.concatenate([lon_recv[s, : 2 * DP] for s in range(N_LON)], axis=1)
    filtered = dot(circles, circle[...].astype(BF16))
    lanes_of = lambda t: jnp.concatenate(
        [filtered[i * DP : (i + 1) * DP, t * 128 : (t + 1) * 128] for i in range(2)], axis=1
    )
    smooth = jnp.concatenate([lanes_of(0), lanes_of(1), put_zeros(32, 256)], axis=0).astype(BF16)
    centre = jnp.concatenate([lanes_of(2), put_zeros(80, 256)], axis=0).astype(BF16)
    spectral = dot(w_atm[...], smooth)
    lifted = dot(w_lift[...], centre).astype(BF16).astype(F32)
    atm_hidden = (lifted + gelu(spectral)).astype(BF16)
    fluxes = dot(w_exch[...], atm_hidden)[:8]
    stacked = jnp.concatenate([fluxes[:, i * 128 : (i + 1) * 128] for i in range(2)], axis=0)
    box = 4 * iota((128, WIDE), 0) - 4
    column = iota((128, WIDE), 1) - HALO
    spread = jnp.where((column >= box) & (column < box + 4), 1.0, 0.0).astype(BF16)
    up_flux = dot(stacked.astype(BF16), spread)
    for i in range(2):
        flux_send[i] = up_flux[8 * i : 8 * i + 8]
    flux_copies = [
        send(flux_send.at[1], flux_recv.at[0], (0, 1, 0)),
        send(flux_send.at[0], flux_recv.at[1], (0, -1, 0)),
    ]

    for copy in row_copies:
        copy.wait_recv()
    lane = iota((SP, 128), 1)

    def ring(row, v):
        x = jnp.concatenate([row[:, 256:], row[:, :128]], axis=1)
        return pltpu.roll(x, 256 - 52 - v, 1)[:, :128]

    def put_flux(e, flux):
        inner = [pltpu.roll(flux, WIDE - 52 - v, 1)[:, :256] for v in range(7)]
        outer = [ring(flux, v) for v in range(7)]
        inner = jnp.concatenate(inner + [put_zeros(8, 256)], axis=0).astype(BF16)
        outer = jnp.concatenate(outer + [put_zeros(8, 128)], axis=0).astype(BF16)
        for p, h in ((e, 0), (e - 1, 1)):
            if 0 <= p < 13:
                xf[p, :, 256 * h : 256 * (h + 1)] = inner
        for h in range(4):
            if 0 <= e - h < 11:
                xf[13 + e - h, :, 128 * h : 128 * (h + 1)] = outer

    seas = {}
    def place(e):
        if e < 3:
            row, r = rows_recv[e].astype(F32), e + 5
            left, right = corner[0, 0], corner[1, 0]
        elif e < 11:
            row, r = base[e - 3].astype(F32), e - 3
            left, right = lon_recv[3, 2 * DP :], lon_recv[1, 2 * DP :]
        else:
            row, r = rows_recv[e - 8].astype(F32), e - 11
            left, right = corner[0, 1], corner[1, 1]
        left = pltpu.roll(left.astype(F32), (-3 * r) % 128, 1)
        right = pltpu.roll(right.astype(F32), (107 - 3 * r) % 128, 1)
        first = jnp.where(lane < 3, left, row[:, :128])
        last = jnp.where(lane >= 107, right, row[:, 256:])
        last = jnp.where(lane >= 110, 0.0, last)
        row = jnp.concatenate([first, row[:, 128:256], last], axis=1)
        if e < 3:
            row = row * jnp.where(lat == 0, 0.0, 1.0)
        if e >= 11:
            row = row * jnp.where(lat == N_LAT - 1, 0.0, 1.0)
        seas[e] = row[STATE : STATE + 1]
        row = row.astype(BF16)
        if e < 3 or e >= 11:
            own_columns(row, e)
        for v in range(7):
            shifted = ring(row, v)
            for h in range(4):
                if 0 <= e - h < 11:
                    xs[13 + e - h, SP * v : SP * (v + 1), 128 * h : 128 * (h + 1)] = shifted
        if 3 <= e < 11:
            i = (e - 3) // 4
            put_flux(e, up_flux[8 * i : 8 * i + 8] * seas[e])

    for e in (0, 1, 2):
        place(e)
    acc[0, :, :512] += dot(w_all[:, : 3 * KS], stack(0, 3))
    acc[0, :, 512:] += dot(w_all[:, :KS], stack(2, 1))
    for e in (11, 12, 13):
        place(e)
    acc[1, :, :512] += dot(w_all[:, 6 * KS :], stack(10, 1))
    acc[1, :, 512:] += dot(w_all[:, 4 * KS :], stack(10, 3))
    for e in range(3, 11):
        place(e)
    acc[2, :, :512] = dot(w_all[...], stack(13, 7))
    acc[2, :, 512:] = dot(w_all[...], stack(17, 7))
    for copy in flux_copies:
        copy.wait_recv()
    for e in (0, 1, 2, 11, 12, 13):
        put_flux(e, flux_recv[0 if e < 3 else 1] * seas[e])

    def flux_stack(first):
        return xf[first : first + 7].reshape(7 * KF, 512)

    for g, first in ((0, 0), (1, 4), (2, 13)):
        second = first + (2 if g < 2 else 4)
        sides = jnp.concatenate([flux_stack(first), flux_stack(second)], axis=1)
        acc[g] += dot(w_flux[...], sides)

    def group(g, carry):
        conv = acc[g]
        mean = jnp.sum(conv, axis=0, keepdims=True) * (1.0 / CH)
        centered = conv - mean
        square = centered * centered
        end = jnp.where(iota((8, 1024), 0) < CH - (CP - 8), square[CP - 8 :], 0.0)
        variance = jnp.sum(square[: CP - 8], axis=0, keepdims=True)
        variance = (variance + jnp.sum(end, axis=0, keepdims=True)) * (1.0 / CH)
        scale = jnp.concatenate([gains[...]] * 8, axis=1)
        normed = (centered * lax.rsqrt(variance + 1e-6) * scale).astype(BF16)
        wide = dot(w_wide[...], normed).astype(BF16)
        hidden[g, :HID] = (wide * jnp.bfloat16(0.5)) * (1 + lax.erf(wide * jnp.bfloat16(0.5**0.5)))
        for h in range(2):
            p = (4 * g + 2 * h if g < 2 else 13 + 4 * h) + 3
            hidden[g, HID : HID + SP, 512 * h : 512 * (h + 1)] = xs[p, 3 * SP : 4 * SP]
            hidden[g, HID + SP :, 512 * h : 512 * (h + 1)] = xf[p]
        fresh[g] = hidden[g, HID : HID + SP].astype(F32) + dot(w_out[...], hidden[g])
        return carry

    for g in (2, 0, 1):
        group(g, 0)

    def fresh_row(r, rows):
        inner = fresh[r // 4, :rows, 256 * (r % 4) : 256 * (r % 4 + 1)]
        outer = fresh[2, :rows, 128 * r : 128 * (r + 1)]
        return jnp.concatenate([inner, outer], axis=1)

    x_new = jnp.concatenate([fresh_row(r, 8)[:1] for r in range(ROWS)], axis=0)
    x_new = pltpu.roll(x_new, 52, 1).astype(BF16).astype(F32)
    x = jnp.where(mask > 0.5, x_new, padded_to(state[0].astype(F32), ROWS, WIDE))
    x_own[...] = x
    x_all[0, sec] = x
    x_copies = [send(x_own, x_all.at[0, sec], (ds, 0, 0)) for ds in (2, 1, 3)]
    x_copies += [send(x_own, x_all.at[1, sec], (ds, twin, 0)) for ds in (2, 1, 3, 0)]

    for r in range(ROWS):
        grid[:, r, :] = pltpu.roll(fresh_row(r, SP), 52, 1)
    mask_wide = jnp.broadcast_to(mask[None, :, :COLS], (STATE, ROWS, COLS))
    out_buf[...] = jnp.where(mask_wide > 0.5, grid[:STATE, :, :COLS], state[...].astype(F32)).astype(BF16)
    out_copy = pltpu.make_async_copy(out_buf, stepped, out_sem)
    out_copy.start()

    quad = iota((WIDE, 128), 1) * 4
    column = iota((WIDE, 128), 0)
    pool = jnp.where((column >= quad) & (column < quad + 4), 1.0, 0.0).astype(BF16)
    heat_boxes = dot((x * mask).astype(BF16), pool)
    count_boxes = dot(mask.astype(BF16), pool)
    for i in range(2):
        total = jnp.sum(heat_boxes[4 * i : 4 * i + 4], axis=0, keepdims=True)
        count = jnp.sum(count_boxes[4 * i : 4 * i + 4], axis=0, keepdims=True)
        pooled[i : i + 1, :] = (total / jnp.maximum(count, 1.0))[:, :90]
    def folded(y):
        return jnp.sum(y[:, :128] + y[:, 128:256] + y[:, 256:], axis=0, keepdims=True)

    terms_copy.wait_recv()
    area_sum = folded(terms[0, 0]) + folded(terms[1, 0])

    def fair_score(which):
        members = [x_all[which, m] for m in range(N_SEC)]
        deviation = sum(jnp.abs(m - terms[which, 1]) for m in members)
        gaps = sum(
            jnp.abs(members[m] - members[n]) for m in range(N_SEC) for n in range(m + 1, N_SEC)
        )
        epsilon = 0.05 / N_SEC
        return deviation * (1.0 / N_SEC) - (1.0 - epsilon) / (N_SEC * (N_SEC - 1)) * gaps

    for copy in x_copies:
        copy.wait_recv()
    fair = fair_score(0)

    heat_sum = folded(terms[0, 0] * fair) + folded(terms[1, 0] * fair_score(1))
    both = jnp.concatenate([heat_sum, area_sum, put_zeros(6, 128)], axis=0)
    pair[...] = both
    mine = chip_y * N_LON + lon
    chips[mine] = both
    chip_copies = [send(pair, chips.at[mine], (0, 2 * dy, k)) for dy, k in CHIP_MOVES]
    score[...] = fair[:, :COLS]
    for copy in chip_copies:
        copy.wait_recv()
    total = chips[0]
    for m in range(1, 16):
        total = total + chips[m]
    sums = jnp.sum(total, axis=1, keepdims=True)
    skill[...] = sums[0:1] / sums[1:2]

    for copy in copies:
        copy.wait_send()
    out_copy.wait()


CHIP_MOVES = [(2, 2), (2, 1), (2, 3), (1, 2), (3, 2), (2, 0), (0, 2), (1, 1), (1, 3), (3, 1), (3, 3)]
CHIP_MOVES += [(1, 0), (3, 0), (0, 1), (0, 3)]
N_COPIES = len(LON_MOVES) + len(ROW_MOVES) + len(CORNER_MOVES) + 2 + 1 + 7 + 15


def hand_over(*refs):
    count = len(refs) // 2
    for n in range(count):
        refs[count + n][...] = refs[n][...]


def on_device(*args):
    (drivers, state, flags, tiles, heat, air, inphase, quadrature, exchange, intake, stencil, gain,
     widening, narrowing, readout) = args
    anywhere = pl.BlockSpec(memory_space=pl.ANY)
    vmem = pl.BlockSpec(memory_space=pltpu.VMEM)
    operands = (
        state[0], flags, tiles, heat, drivers[0], jnp.asarray(circle_tables()), jnp.asarray(area_table()),
        air, inphase, quadrature, exchange.T, intake, stencil, gain,
        widening, narrowing.T, readout.T,
    )
    outputs = (
        jax.ShapeDtypeStruct((STATE, ROWS, COLS), BF16),
        jax.ShapeDtypeStruct((2, 90), F32),
        jax.ShapeDtypeStruct((ROWS, COLS), F32),
        jax.ShapeDtypeStruct((1, 1), F32),
    )
    results = pl.pallas_call(
        kernel,
        out_shape=outputs,
        in_specs=[anywhere] * len(operands),
        out_specs=(anywhere, vmem, vmem, vmem),
        scratch_shapes=[pltpu.VMEM(x.shape, x.dtype) for x in operands]
        + [
            pltpu.VMEM((SP, ROWS, WIDE), F32),
            pltpu.VMEM((ROWS, SP, WIDE), BF16),
            pltpu.VMEM((2, 2 * DP + SP, 128), BF16),
            pltpu.VMEM((N_LON, 2 * DP + SP, 128), BF16),
            pltpu.VMEM((2, 2, SP, 128), BF16),
            pltpu.VMEM((6, SP, WIDE), BF16),
            pltpu.VMEM((2, 8, WIDE), F32),
            pltpu.VMEM((2, 8, WIDE), F32),
            pltpu.VMEM((CP, 7 * KS), BF16),
            pltpu.VMEM((CP, 7 * KF), BF16),
            pltpu.VMEM((HID, CP), BF16),
            pltpu.VMEM((SP, HK), BF16),
            pltpu.VMEM((CP, 128), F32),
            pltpu.VMEM((384, 128), BF16),
            pltpu.VMEM((384, 128), BF16),
            pltpu.VMEM((16, 384), BF16),
            pltpu.VMEM((24, KS, 512), BF16),
            pltpu.VMEM((24, KF, 512), BF16),
            pltpu.VMEM((3, CP, 1024), F32),
            pltpu.VMEM((3, HK, 1024), BF16),
            pltpu.VMEM((3, SP, 1024), F32),
            pltpu.VMEM((STATE, ROWS, COLS), BF16),
            pltpu.VMEM((ROWS, WIDE), F32),
            pltpu.VMEM((2, N_SEC, ROWS, WIDE), F32),
            pltpu.VMEM((2, 2, ROWS, WIDE), F32),
            pltpu.VMEM((8, 128), F32),
            pltpu.VMEM((16, 8, 128), F32),
            pltpu.SemaphoreType.DMA((len(operands),)),
            pltpu.SemaphoreType.DMA,
            pltpu.SemaphoreType.DMA((N_COPIES,)),
            pltpu.SemaphoreType.DMA((N_COPIES,)),
        ],
        compiler_params=pltpu.CompilerParams(
            collective_id=0, has_side_effects=True, vmem_limit_bytes=58 << 20
        ),
        name="coupled_step",
    )(*operands)
    stepped, pooled, score, skill = pl.pallas_call(
        hand_over,
        out_shape=outputs,
        in_specs=[vmem] * 4,
        out_specs=(vmem,) * 4,
        name="hand_over",
    )(*results)
    return (
        stepped.reshape(1, STATE, ROWS, COLS),
        pooled.reshape(1, 2, 90),
        score,
        skill.reshape(()),
    )


def solution(mesh):
    in_specs = (
        P("sec", None, "lat", "lon"),
        P("sec", None, "lat", "lon"),
        P("lat", "lon"),
        P("lat", "lon"),
        P("lat", "lon"),
    ) + (P(),) * 10
    out_specs = (P("sec", None, "lat", "lon"), P("sec", "lat", "lon"), P("lat", "lon"), P())
    return jax.shard_map(
        on_device, mesh=mesh, in_specs=in_specs, out_specs=out_specs, check_vma=False
    )
```
